256 devices in a mesh: prefix: 16 (over x_lo, y, core), head: 8 (over z), dp: 2 (over x_hi).
Axes of the slice: x: 4 (x_hi: 2, x_lo: 2; x = x_hi * 2 + x_lo), y: 4, z: 8, core: 2. Of those that a mesh axis runs over, the one named last changes fastest.
Arguments:
- query_nope: bfloat16 [128, 128, 128], P(('dp', 'prefix'), 'head'), may hold values from -5 to 5
- query_rope: bfloat16 [128, 128, 64], P(('dp', 'prefix'), 'head'), may hold values from -7 to 7
- latent_cache: bfloat16 [49152, 576], P(('prefix', 'head', 'dp')), may hold values from -7 to 7
- key_absorb: bfloat16 [128, 128, 512], P('head'), may hold values from -0.5 to 0.5
- value_absorb: bfloat16 [128, 512, 128], P(('head', 'prefix')), may hold values from -2 to 2
- output_proj: bfloat16 [16384, 7168], P(('head', 'prefix')), may hold values from -0.1875 to 0.1875
Outputs:
- attention_out: float32 [128, 7168], P(('dp', 'prefix'), 'head')
The draws below stay inside these ranges and needn't reach their ends.
All inputs are finite; a program needn't handle non-finite values.
Results may differ from the reference program's by a relative error of at most 0.01075.
Values may be sent and summed in bfloat16 or wider, within the bound.
A program may use at most 128 MiB of HBM per device.

```python
import jax
import jax.numpy as jnp
from jax import lax

D = 7168
H = 128
NOPE = 128
ROPE = 64
VDIM = 128
LATENT = 512
QTOK = 128
PREFIX = 49152


def draw_latent_cache(key, part):
    key = jax.random.fold_in(key, 11)
    key_base = jax.random.fold_in(key, 0)
    result = jnp.clip(jax.random.normal(key_base, (PREFIX, LATENT + ROPE), jnp.float32), -5.0, 5.0)
    return result.astype(jnp.bfloat16)


def draw_query_rope(key, part):
    key = jax.random.fold_in(key, 12)
    result = jnp.clip(jax.random.normal(key, (QTOK, H, ROPE), jnp.float32), -5.0, 5.0)
    return result.astype(jnp.bfloat16)


def with_spikes(array, stream_key, source, target, blocks, factor):
    owner, partner = [(jnp.arange(array.shape[dim]) // (array.shape[dim] // blocks)).reshape([-1 if axis == dim else 1 for axis in range(array.ndim)]) for dim in (source, target)]
    chosen = jax.random.permutation(stream_key, blocks)[partner]
    strong = (owner == chosen) | (owner == (partner + blocks // 2) % blocks)
    return jnp.where(strong, factor * array, array)


def block_levels(key, shape, shards, least, high):
    def one(position, blocks):
        steps = jax.random.uniform(jax.random.fold_in(jax.random.fold_in(key, 6), position), (blocks,), jnp.float32, least / len(shards), high / len(shards))
        return jnp.repeat(jnp.exp(steps), shape[position] // blocks).reshape((-1,) + (1,) * (len(shape) - position - 1))

    gain = one(*shards[0])
    for cut in shards[1:]:
        gain = gain * one(*cut)
    return gain


def bell_draw(key, dims, scale, reach, cuts=(), kind=jnp.bfloat16):
    level = block_levels(key, dims, cuts, -0.22, 0.18) if cuts else 1.0
    entries = jax.random.normal(key, dims, jnp.float32) * scale * level
    return jnp.minimum(jnp.maximum(entries, -reach), reach).astype(kind)


def heavy_noise(stream_key, shape, deviation, reach, shards, heavy, held_as=jnp.bfloat16):
    entries = deviation * jax.random.normal(stream_key, shape, jnp.float32)
    if shards:
        entries = entries * block_levels(stream_key, shape, shards, -0.22, 0.18)
    return jnp.clip(with_spikes(entries, jax.random.fold_in(stream_key, 3), *heavy), -reach, reach).astype(held_as)


def setup_inputs(seed: int = 0) -> dict:
    splits = jax.random.split(jax.random.key(seed), 7)
    query_nope = bell_draw(splits[0], (QTOK, H, NOPE), 1.0, 5.0, ((0, 32), (1, 8)))
    query_rope = draw_query_rope(jax.random.fold_in(splits[6], 71), 0)
    latent_cache = draw_latent_cache(jax.random.fold_in(splits[6], 71), 0)
    key_absorb = bell_draw(splits[3], (H, NOPE, LATENT), NOPE ** -0.5, 0.5, ((0, 8),))
    value_absorb = bell_draw(splits[4], (H, LATENT, VDIM), (LATENT // 64) ** -0.5, 2.0, ((0, 128),))
    output_proj = heavy_noise(splits[5], (H * VDIM, D), (H * VDIM) ** -0.5, 0.1875, ((0, 128),), (0, 1, 128, 5.5))
    return dict(query_nope=query_nope, query_rope=query_rope, latent_cache=latent_cache, key_absorb=key_absorb, value_absorb=value_absorb, output_proj=output_proj)


def reference(query_nope, query_rope, latent_cache, key_absorb, value_absorb, output_proj):
    factor = (NOPE + ROPE) ** -0.5
    absorbed = jnp.einsum("thn,hnl->thl", query_nope.astype(jnp.float32), key_absorb.astype(jnp.float32)).astype(jnp.bfloat16)
    latent_part = latent_cache[:, :LATENT]
    rope_part = latent_cache[:, LATENT:]

    def one_head(operands):
        head_query, head_rope = operands
        scores = jnp.dot(head_query, latent_part.T, preferred_element_type=jnp.float32)
        scores = (scores + jnp.dot(head_rope, rope_part.T, preferred_element_type=jnp.float32)) * factor
        highest = jnp.max(scores, axis=1, keepdims=True)
        expvals = jnp.exp(scores - highest)
        totals = jnp.sum(expvals, axis=1, keepdims=True)
        weighted = jnp.dot(expvals.astype(jnp.bfloat16), latent_part, preferred_element_type=jnp.float32)
        return (weighted / totals).astype(jnp.bfloat16)

    latent_out = lax.map(one_head, (jnp.swapaxes(absorbed, 0, 1), jnp.swapaxes(query_rope, 0, 1)))
    head_out = jnp.einsum("htl,hlv->thv", latent_out.astype(jnp.float32), value_absorb.astype(jnp.float32)).astype(jnp.bfloat16)
    flat_out = head_out.reshape(QTOK, H * VDIM)
    return jnp.dot(flat_out, output_proj, preferred_element_type=jnp.float32)
```

```python
import math

import jax
import jax.numpy as jnp
from jax import lax
from jax.experimental import pallas as pl
from jax.experimental.pallas import tpu as pltpu
from jax.sharding import PartitionSpec as P

MESH = pl.DeviceIdType.MESH

D = 7168
NOPE, ROPE, VDIM, LATENT = 128, 64, 128, 512
WIDTH = LATENT + ROPE
TOKENS = 128
Z = 8
PLANE = 16
OWNERS = 8
HEADS = 8
ROWS = HEADS * TOKENS
BLOCK = 192
MSG = 48
HALF = D // 2
COLS = D // Z
SCALE = (NOPE + ROPE) ** -0.5 * math.log2(math.e)

UP = (2, 6, 10, 14)
DOWN = (3, 7, 11, 14)
SIB_OF = {0: 1, 2: 4, 3: 5, 6: 8, 7: 9, 10: 12, 11: 13, 14: 15}
SIB_ORDER = (0, 2, 3, 6, 7, 10, 11, 14)
TILE = 256


def attend(first, base, size, q, kv, acc, top, tot):
    def tile(i, carry):
        rows = pl.ds(pl.multiple_of(i * TILE, TILE), TILE)
        keys = kv[pl.ds(base, size), :]
        s = lax.dot_general(
            q[rows, :], keys, (((1,), (1,)), ((), ())), preferred_element_type=jnp.float32
        )
        high = jnp.max(s, axis=1, keepdims=True)
        if first:
            new_top = jnp.broadcast_to(high, (TILE, 128))
        else:
            old_top = top[rows, :]
            new_top = jnp.maximum(old_top, high)
            alpha = jnp.exp2(old_top - new_top)
        part = None
        pieces = []
        for k in range(size // 128):
            e = jnp.exp2(s[:, k * 128 : (k + 1) * 128] - new_top)
            part = e if part is None else part + e
            pieces.append(e.astype(jnp.bfloat16))
        p = jnp.concatenate(pieces, axis=1)
        out = jnp.dot(p, kv[pl.ds(base, size), :LATENT], preferred_element_type=jnp.float32)
        top[rows, :] = new_top
        if first:
            tot[rows, :] = part
            acc[rows, :] = out
        else:
            tot[rows, :] = tot[rows, :] * alpha + part
            for k in range(LATENT // 128):
                cols = slice(k * 128, (k + 1) * 128)
                acc[rows, cols] = acc[rows, cols] * alpha + out[:, cols]
        return carry

    lax.fori_loop(0, ROWS // TILE, tile, 0)


def kernel(
    qn_ref, qr_ref, kv_ref, ka_ref, va_ref, wo_ref, out_ref,
    kv, q, acc, top, tot, ka, va, wo,
    tmpn, tmpr, qsend, qall, q32n, q32r,
    ysend, ssend, yrecv, srecv, wts, ho, dsend, drecv, esend, erecv,
    local, qs_send, qs_recv, q_send, q_recv,
    up_send, up_recv, dn_send, dn_recv, sb_send, sb_recv,
    v_send, v_recv, o_send, o_recv,
    y_send, y_recv, s_send, s_recv, h_send, h_recv, d_send, d_recv, e_send, e_recv,
):
    prefix, z, dp = lax.axis_index("prefix"), lax.axis_index("head"), lax.axis_index("dp")
    c = lax.rem(prefix, 2)
    j_me = lax.div(prefix, 2)
    chip = dp * OWNERS + j_me
    sib = (prefix + 1 - 2 * c, z, dp)
    above = (prefix, lax.rem(z + 1, Z), dp)
    below = (prefix, lax.rem(z + Z - 1, Z), dp)

    def plane(k):
        other = lax.rem(chip + k, PLANE)
        return other, (2 * lax.rem(other, OWNERS) + c, z, lax.div(other, OWNERS))

    def owner(k):
        other = lax.rem(j_me + k, OWNERS)
        return other, (2 * other + c, z, dp)

    def remote(src, dst, ssem, rsem, to):
        return pltpu.make_async_remote_copy(
            src_ref=src, dst_ref=dst, send_sem=ssem, recv_sem=rsem, device_id=to, device_id_type=MESH
        )

    def loop(n, body):
        def step(k, carry):
            body(k)
            return carry

        lax.fori_loop(0, n, step, 0)

    def load_ka(j):
        return pltpu.make_async_copy(ka_ref.at[2 * j + c], ka.at[j], local.at[j])

    loop(HEADS, lambda j: load_ka(j).start())
    load_kv = pltpu.make_async_copy(kv_ref, kv.at[pl.ds(0, BLOCK), :], local.at[8])
    load_kv.start()
    load_va = pltpu.make_async_copy(va_ref.at[0], va.at[j_me], local.at[9])
    load_va.start()
    own_rows = pl.ds(pl.multiple_of(c * VDIM, VDIM), VDIM)
    load_wo = pltpu.make_async_copy(
        wo_ref.at[:, pl.ds(pl.multiple_of(c * HALF, 128), HALF)], wo.at[own_rows, :], local.at[10]
    )
    load_wo.start()

    tmpn[...] = qn_ref[...].astype(jnp.float32).reshape(64, NOPE)
    tmpr[:, :ROPE] = qr_ref[...].astype(jnp.float32).reshape(64, ROPE)
    for parity in range(2):
        qsend[parity, 0:32, :] = tmpn[pl.ds(parity, 32, stride=2), :].astype(jnp.bfloat16)
        rope = tmpr[pl.ds(parity, 32, stride=2), :][:, :ROPE]
        qsend[parity, 32:48, :] = jnp.concatenate([rope[:16], rope[16:]], axis=1).astype(
            jnp.bfloat16
        )

    barrier = pltpu.get_barrier_semaphore()

    def greet(to):
        pl.semaphore_signal(barrier, inc=1, device_id=to, device_id_type=MESH)

    greet(sib)
    loop(PLANE - 1, lambda k: greet(plane(k + 1)[1]))

    def greet_line(k):
        other = lax.rem(z + k + 1, Z)
        greet((prefix, other, dp))
        greet((prefix + 1 - 2 * c, other, dp))

    loop(Z - 1, greet_line)
    pl.semaphore_wait(barrier, 1 + (PLANE - 1) + 2 * (Z - 1))

    q_sib = remote(qsend.at[1 - c], qall.at[chip, c], qs_send, qs_recv, sib)
    q_sib.start()

    def block(slot):
        return kv.at[pl.ds(slot * BLOCK, BLOCK), :]

    def up(step):
        src = kv_ref if step == 0 else block(UP[step - 1])
        dst = block(UP[step])
        if step == 3:
            src = kv.at[pl.ds(UP[2] * BLOCK, BLOCK // 2), :]
            dst = kv.at[pl.ds(14 * BLOCK, BLOCK // 2), :]
        return remote(src, dst, up_send.at[step], up_recv.at[step], above)

    def down(step):
        src = kv_ref if step == 0 else block(DOWN[step - 1])
        dst = block(DOWN[step])
        if step == 3:
            src = kv.at[pl.ds(DOWN[2] * BLOCK + BLOCK // 2, BLOCK // 2), :]
            dst = kv.at[pl.ds(14 * BLOCK + BLOCK // 2, BLOCK // 2), :]
        return remote(src, dst, dn_send.at[step], dn_recv.at[step], below)

    def across(slot):
        i = SIB_ORDER.index(slot)
        src = kv_ref if slot == 0 else block(slot)
        return remote(src, block(SIB_OF[slot]), sb_send.at[i], sb_recv.at[i], sib)

    up(0).start()
    down(0).start()
    across(0).start()
    qall[chip, c] = qsend[c]
    q_sib.wait_recv()

    def q_copy(k):
        _, to = plane(k + 1)
        return remote(qall.at[chip], qall.at[chip], q_send.at[k], q_recv.at[chip], to)

    loop(PLANE - 1, lambda k: q_copy(k).start())

    wo_copy = remote(
        wo_ref.at[:, pl.ds(pl.multiple_of((1 - c) * HALF, 128), HALF)],
        wo.at[own_rows, :], o_send, o_recv, sib,
    )
    wo_copy.start()

    def q_arrived(k):
        other, to = plane(k + 1)
        remote(qall.at[other], qall.at[other], q_send.at[k], q_recv.at[other], to).wait_recv()

    loop(PLANE - 1, q_arrived)

    def unpack(g):
        m = qall[lax.div(g, 2), lax.rem(g, 2)]
        at = pl.multiple_of(g * 32, 32)
        q32n[pl.ds(at, 32), :] = m[0:32].astype(jnp.float32)
        r = m[32:48].astype(jnp.float32)
        q32r[pl.ds(at, 16), 0:ROPE] = r[:, :ROPE]
        q32r[pl.ds(at + 16, 16), 0:ROPE] = r[:, ROPE:]

    loop(2 * PLANE, unpack)

    def v_copy(k):
        _, to = owner(k + 1)
        return remote(va_ref.at[0], va.at[j_me], v_send.at[k], v_recv.at[j_me], to)

    loop(OWNERS - 1, lambda k: v_copy(k).start())

    loop(HEADS, lambda j: load_ka(j).wait())

    def absorb(j):
        at = pl.ds(pl.multiple_of(j * TOKENS, TOKENS), TOKENS)
        nope = q32n[pl.ds(j, TOKENS, stride=HEADS), :].astype(jnp.bfloat16)
        part = jnp.dot(nope, ka[j], preferred_element_type=jnp.float32)
        q[at, 0:LATENT] = (part * SCALE).astype(jnp.bfloat16)
        rope = q32r[pl.ds(j, TOKENS, stride=HEADS), :][:, :ROPE]
        q[at, LATENT:WIDTH] = (rope * SCALE).astype(jnp.bfloat16)

    loop(HEADS, absorb)

    load_kv.wait()
    for step in range(5):
        if step < 4:
            up(step).wait_recv()
            down(step).wait_recv()
            if step < 3:
                up(step + 1).start()
                down(step + 1).start()
                across(UP[step]).start()
                across(DOWN[step]).start()
            else:
                across(14).start()
        if step == 0:
            across(0).wait_recv()
            attend(True, 0, 2 * BLOCK, q, kv, acc, top, tot)
        elif step < 4:
            across(UP[step - 1]).wait_recv()
            across(DOWN[step - 1]).wait_recv()
            attend(False, UP[step - 1] * BLOCK, 4 * BLOCK, q, kv, acc, top, tot)
        else:
            across(14).wait_recv()
            attend(False, 14 * BLOCK, 2 * BLOCK, q, kv, acc, top, tot)

    load_va.wait()

    def v_arrived(k):
        other, to = owner(k + 1)
        remote(va_ref.at[0], va.at[other], v_send.at[k], v_recv.at[other], to).wait_recv()

    loop(OWNERS - 1, v_arrived)
    lane = lax.broadcasted_iota(jnp.int32, (TOKENS, 128), 1)

    def y_copies(k):
        other, to = plane(k)
        j, t = lax.rem(other, OWNERS), lax.div(other, OWNERS)
        src = ysend.at[pl.ds(pl.multiple_of(j * TOKENS + t * 64, 64), 64), :]
        return (
            remote(src, yrecv.at[chip], y_send.at[k], y_recv.at[chip], to),
            remote(ssend.at[j], srecv.at[chip], s_send.at[k], s_recv.at[chip], to),
        )

    def project(k):
        j = lax.rem(j_me + k, OWNERS)
        rows = pl.ds(pl.multiple_of(j * TOKENS, TOKENS), TOKENS)
        total = jnp.sum(tot[rows, :], axis=1, keepdims=True)
        latent = (acc[rows, :] / total).astype(jnp.bfloat16)
        y = jnp.dot(latent, va[j], preferred_element_type=jnp.float32)
        ysend[rows, :] = y.astype(jnp.bfloat16)
        stats = jnp.where(lane == 0, top[rows, :], jnp.broadcast_to(total, (TOKENS, 128)))
        ssend[j] = stats.T[0:8, :]

        @pl.when(k > 0)
        def _():
            for copy in y_copies(k):
                copy.start()

        for copy in y_copies(k + OWNERS):
            copy.start()

    loop(HEADS, project)
    mine = pl.ds(pl.multiple_of(j_me * TOKENS + dp * 64, 64), 64)
    yrecv[chip] = ysend[mine, :]
    srecv[chip] = ssend[j_me]

    def y_arrived(k):
        other, to = plane(k + 1)
        remote(yrecv.at[other], yrecv.at[other], y_send.at[k], y_recv.at[other], to).wait_recv()
        remote(srecv.at[other], srecv.at[other], s_send.at[k], s_recv.at[other], to).wait_recv()

    loop(PLANE - 1, y_arrived)

    tops = jnp.concatenate([srecv[s, 0:1, :] for s in range(PLANE)], axis=0)
    sums = jnp.concatenate([srecv[s, 1:2, :] for s in range(PLANE)], axis=0)
    weight = sums * jnp.exp2(tops - jnp.max(tops, axis=0, keepdims=True))
    weight = weight / jnp.sum(weight, axis=0, keepdims=True)
    wts[...] = jnp.concatenate([weight, jnp.zeros((128 - PLANE, 128), jnp.float32)], axis=0).T
    w = wts[pl.ds(pl.multiple_of(dp * 64, 64), 64), :]
    merged = None
    for s in range(PLANE):
        term = yrecv[s].astype(jnp.float32) * w[:, s : s + 1]
        merged = term if merged is None else merged + term
    ho[c] = merged.astype(jnp.bfloat16)
    h_copy = remote(ho.at[c], ho.at[c], h_send, h_recv, sib)
    h_copy.start()
    load_wo.wait()
    wo_copy.wait_recv()
    h_copy.wait_recv()

    heads = jnp.concatenate([ho[0], ho[1]], axis=1)
    for n in range(4):
        part = jnp.dot(
            heads, wo[:, n * COLS : (n + 1) * COLS], preferred_element_type=jnp.float32
        )
        if n < 2:
            low = part if n == 0 else jnp.concatenate([low, part], axis=1)
        else:
            high = part if n == 2 else jnp.concatenate([high, part], axis=1)
    for i in range(OWNERS):
        rows = slice(i * 8, (i + 1) * 8)
        dsend[i] = jnp.concatenate([low[rows], high[rows]], axis=0).astype(jnp.bfloat16)

    def d_copy(k):
        other, to = owner(k + 1)
        return remote(dsend.at[other], drecv.at[j_me], d_send.at[k], d_recv.at[j_me], to)

    loop(OWNERS - 1, lambda k: d_copy(k).start())
    drecv[j_me] = dsend[j_me]

    def d_arrived(k):
        other, to = owner(k + 1)
        remote(dsend.at[other], drecv.at[other], d_send.at[k], d_recv.at[other], to).wait_recv()

    loop(OWNERS - 1, d_arrived)
    summed = drecv[0].astype(jnp.float32)
    for i in range(1, OWNERS):
        summed = summed + drecv[i].astype(jnp.float32)
    for k in range(4):
        piece = summed[(k // 2) * 8 : (k // 2) * 8 + 8, (k % 2) * COLS : (k % 2 + 1) * COLS]
        esend[k, 0] = piece[0:4]
        esend[k, 1] = piece[4:8]

    def e_copy(i):
        k, core = lax.div(i, 2), lax.rem(i, 2)
        to_z = 4 * c + k
        to = (2 * j_me + core, to_z, dp)
        return (to_z == z) & (core == c), k, core, remote(
            esend.at[k, core], erecv.at[z], e_send.at[i], e_recv.at[z], to
        )

    def e_start(i):
        here, k, core, copy = e_copy(i)

        @pl.when(jnp.logical_not(here))
        def _():
            copy.start()

        @pl.when(here)
        def _():
            erecv[z] = esend[k, core]

    loop(8, e_start)
    from_core = lax.div(z, 4)

    def e_arrived(s):
        frm = (2 * j_me + from_core, s, dp)

        @pl.when(jnp.logical_not((s == z) & (from_core == c)))
        def _():
            remote(esend.at[0, 0], erecv.at[s], e_send.at[0], e_recv.at[s], frm).wait_recv()

    loop(Z, e_arrived)
    result = erecv[0]
    for s in range(1, Z):
        result = result + erecv[s]
    out_ref[...] = result

    q_sib.wait_send()
    for step in range(4):
        up(step).wait_send()
        down(step).wait_send()
    for slot in SIB_ORDER:
        across(slot).wait_send()
    wo_copy.wait_send()
    h_copy.wait_send()

    def sent_plane(k):
        q_copy(k).wait_send()
        for copy in y_copies(k + 1):
            copy.wait_send()

    loop(PLANE - 1, sent_plane)

    def sent_owner(k):
        v_copy(k).wait_send()
        d_copy(k).wait_send()

    loop(OWNERS - 1, sent_owner)

    def e_sent(i):
        here, _, _, copy = e_copy(i)

        @pl.when(jnp.logical_not(here))
        def _():
            copy.wait_send()

    loop(8, e_sent)


def body(query_nope, query_rope, latent_cache, key_absorb, value_absorb, output_proj):
    vmem = pl.BlockSpec(memory_space=pltpu.VMEM)
    hbm = pl.BlockSpec(memory_space=pl.ANY)
    bf16, f32 = jnp.bfloat16, jnp.float32
    dma = pltpu.SemaphoreType.DMA
    return pl.pallas_call(
        kernel,
        out_shape=jax.ShapeDtypeStruct((4, COLS), f32),
        in_specs=[vmem, vmem, hbm, hbm, hbm, hbm],
        out_specs=vmem,
        scratch_shapes=[
            pltpu.VMEM((16 * BLOCK, WIDTH), bf16),
            pltpu.VMEM((ROWS, WIDTH), bf16),
            pltpu.VMEM((ROWS, LATENT), f32),
            pltpu.VMEM((ROWS, 128), f32),
            pltpu.VMEM((ROWS, 128), f32),
            pltpu.VMEM((HEADS, NOPE, LATENT), bf16),
            pltpu.VMEM((HEADS, LATENT, VDIM), bf16),
            pltpu.VMEM((2 * VDIM, HALF), bf16),
            pltpu.VMEM((64, NOPE), f32),
            pltpu.VMEM((64, 128), f32),
            pltpu.VMEM((2, MSG, 128), bf16),
            pltpu.VMEM((PLANE, 2, MSG, 128), bf16),
            pltpu.VMEM((ROWS, NOPE), f32),
            pltpu.VMEM((ROWS, 128), f32),
            pltpu.VMEM((ROWS, VDIM), bf16),
            pltpu.VMEM((HEADS, 8, 128), f32),
            pltpu.VMEM((PLANE, 64, VDIM), bf16),
            pltpu.VMEM((PLANE, 8, 128), f32),
            pltpu.VMEM((128, 128), f32),
            pltpu.VMEM((2, 64, VDIM), bf16),
            pltpu.VMEM((OWNERS, 16, HALF // 2), bf16),
            pltpu.VMEM((OWNERS, 16, HALF // 2), bf16),
            pltpu.VMEM((4, 2, 4, COLS), f32),
            pltpu.VMEM((Z, 4, COLS), f32),
            dma((11,)),
            dma, dma, dma((PLANE - 1,)), dma((PLANE,)),
            dma((4,)), dma((4,)), dma((4,)), dma((4,)), dma((8,)), dma((8,)),
            dma((OWNERS - 1,)), dma((OWNERS,)), dma, dma,
            dma((PLANE,)), dma((PLANE,)), dma((PLANE,)), dma((PLANE,)),
            dma, dma, dma((OWNERS - 1,)), dma((OWNERS,)), dma((8,)), dma((Z,)),
        ],
        compiler_params=pltpu.CompilerParams(
            collective_id=0, has_side_effects=True, vmem_limit_bytes=48 * 1024 * 1024
        ),
        cost_estimate=pl.CostEstimate(
            flops=7_000_000_000, bytes_accessed=10_000_000, transcendentals=3_145_728
        ),
        name="latent_attention",
    )(query_nope, query_rope, latent_cache, key_absorb, value_absorb, output_proj)


def solution(mesh):
    in_specs = (
        P(("dp", "prefix"), "head", None),
        P(("dp", "prefix"), "head", None),
        P(("prefix", "head", "dp"), None),
        P("head", None, None),
        P(("head", "prefix"), None, None),
        P(("head", "prefix"), None),
    )
    out_specs = P(("dp", "prefix"), "head")
    return jax.shard_map(body, mesh=mesh, in_specs=in_specs, out_specs=out_specs, check_vma=False)
```

```python
import math

import jax
import jax.numpy as jnp
from jax import lax
from jax.experimental import pallas as pl
from jax.experimental.pallas import tpu as pltpu
from jax.sharding import PartitionSpec as P

MESH = pl.DeviceIdType.MESH

D = 7168
NOPE, ROPE, VDIM, LATENT = 128, 64, 128, 512
WIDTH = LATENT + ROPE
TOKENS = 128
Z = 8
PLANE = 16
OWNERS = 8
HEADS = 8
ROWS = HEADS * TOKENS
BLOCK = 192
MSG = 48
HALF = D // 2
COLS = D // Z
SCALE = (NOPE + ROPE) ** -0.5 * math.log2(math.e)

HALFB = BLOCK // 2
PACK = 16
UP = (0, 2, 6, 10, 14)
DOWN = (0, 3, 7, 11, 14)
SIB_OF = {0: 1, 2: 4, 3: 5, 6: 8, 7: 9, 10: 12, 11: 13, 14: 15}
SIB_ORDER = (0, 2, 3, 6, 7, 10, 11, 14)
TILE = 512


def chunk_keys(kv, blocks):
    latent, rope = [], []
    for b in blocks:
        for h in range(2):
            latent.append(kv[b, h, 0:HALFB, :])
            packed = kv[b, h, HALFB : HALFB + PACK, 0 : 6 * ROPE]
            for g in range(6):
                rope.append(packed[:, g * ROPE : (g + 1) * ROPE])
    latent = jnp.concatenate(latent, axis=0)
    return jnp.concatenate([latent, jnp.concatenate(rope, axis=0)], axis=1), latent


def attend(first, blocks, q, kv, acc, top, tot, order=None, finish=None):
    keys, values = chunk_keys(kv, blocks)
    n = ROWS // TILE

    def at(i):
        if order is None:
            return pl.ds(i * TILE, TILE)
        return pl.ds(pl.multiple_of(order(i) * TILE, TILE), TILE)

    def score(i):
        return lax.dot_general(
            q[at(i), :], keys, (((1,), (1,)), ((), ())), preferred_element_type=jnp.float32
        )

    s = score(0)
    for i in range(n):
        later = score(i + 1) if i + 1 < n else None
        rows = at(i)
        high = jnp.max(s, axis=1, keepdims=True)
        if first:
            new_top = jnp.broadcast_to(high, (TILE, 128))
        else:
            old_top = top[rows, :]
            new_top = jnp.maximum(old_top, high)
            alpha = jnp.exp2(old_top - new_top)
        part = None
        pieces = []
        for k in range(s.shape[1] // 128):
            e = jnp.exp2(s[:, k * 128 : (k + 1) * 128] - new_top)
            part = e if part is None else part + e
            pieces.append(e.astype(jnp.bfloat16))
        p = jnp.concatenate(pieces, axis=1)
        out = jnp.dot(p, values, preferred_element_type=jnp.float32)
        if not first:
            part = tot[rows, :] * alpha + part
        if finish is not None:
            total = jnp.sum(part, axis=1, keepdims=True)
            scale = 1.0 / total
            latent = []
            for k in range(LATENT // 128):
                cols = slice(k * 128, (k + 1) * 128)
                latent.append(((acc[rows, cols] * alpha + out[:, cols]) * scale).astype(jnp.bfloat16))
            finish(i, jnp.concatenate(latent, axis=1), new_top, total)
        else:
            top[rows, :] = new_top
            tot[rows, :] = part
            for k in range(LATENT // 128):
                cols = slice(k * 128, (k + 1) * 128)
                if first:
                    acc[rows, cols] = out[:, cols]
                else:
                    acc[rows, cols] = acc[rows, cols] * alpha + out[:, cols]
        s = later


def kernel(
    qn_ref, qr_ref, kv_ref, ka_ref, va_ref, wo_ref, out_ref,
    kv, q, acc, top, tot, ka, va, wo,
    tmpn, tmpr, qsend, qall, q32n, q32r,
    kvraw, ysend, yrecv, wts, ho, dsend, drecv, esend, erecv,
    local, qs_send, qs_recv, q_send, q_recv,
    up_send, up_recv, dn_send, dn_recv, sb_send, sb_recv,
    v_send, v_recv, o_send, o_recv,
    y_send, y_recv, h_send, h_recv, d_send, d_recv, e_send, e_recv,
):
    prefix, z, dp = lax.axis_index("prefix"), lax.axis_index("head"), lax.axis_index("dp")
    c = lax.rem(prefix, 2)
    j_me = lax.div(prefix, 2)
    chip = dp * OWNERS + j_me
    sib = (prefix + 1 - 2 * c, z, dp)
    above = (prefix, lax.rem(z + 1, Z), dp)
    below = (prefix, lax.rem(z + Z - 1, Z), dp)

    def plane(k):
        other = lax.rem(chip + k, PLANE)
        return other, (2 * lax.rem(other, OWNERS) + c, z, lax.div(other, OWNERS))

    def owner(k):
        other = lax.rem(j_me + k, OWNERS)
        return other, (2 * other + c, z, dp)

    def remote(src, dst, ssem, rsem, to):
        return pltpu.make_async_remote_copy(
            src_ref=src, dst_ref=dst, send_sem=ssem, recv_sem=rsem, device_id=to, device_id_type=MESH
        )

    def loop(n, body):
        def step(k, carry):
            body(k)
            return carry

        lax.fori_loop(0, n, step, 0)

    def load_ka(j):
        return pltpu.make_async_copy(ka_ref.at[2 * j + c], ka.at[j], local.at[j])

    loop(HEADS, lambda j: load_ka(j).start())
    load_kv = pltpu.make_async_copy(kv_ref, kvraw, local.at[8])
    load_kv.start()
    load_va = pltpu.make_async_copy(va_ref.at[0], va.at[j_me], local.at[9])
    load_va.start()
    own_rows = pl.ds(pl.multiple_of(c * VDIM, VDIM), VDIM)
    load_wo = pltpu.make_async_copy(
        wo_ref.at[:, pl.ds(pl.multiple_of(c * HALF, 128), HALF)], wo.at[own_rows, :], local.at[10]
    )
    load_wo.start()

    tmpn[...] = qn_ref[...].astype(jnp.float32).reshape(64, NOPE)
    tmpr[:, :ROPE] = qr_ref[...].astype(jnp.float32).reshape(64, ROPE)
    for parity in range(2):
        qsend[parity, 0:32, :] = tmpn[pl.ds(parity, 32, stride=2), :].astype(jnp.bfloat16)
        rope = tmpr[pl.ds(parity, 32, stride=2), :][:, :ROPE]
        qsend[parity, 32:48, :] = jnp.concatenate([rope[:16], rope[16:]], axis=1).astype(
            jnp.bfloat16
        )

    load_kv.wait()
    for h in range(2):
        rows = slice(h * HALFB, (h + 1) * HALFB)
        kv[0, h, 0:HALFB, :] = kvraw[rows, 0:LATENT]
        rope = kvraw[rows, LATENT:WIDTH].astype(jnp.float32)
        packed = [rope[g * PACK : (g + 1) * PACK] for g in range(6)]
        packed.append(jnp.zeros((PACK, LATENT - 6 * ROPE), jnp.float32))
        kv[0, h, HALFB : HALFB + PACK, :] = jnp.concatenate(packed, axis=1).astype(jnp.bfloat16)

    barrier = pltpu.get_barrier_semaphore()

    def greet(to):
        pl.semaphore_signal(barrier, inc=1, device_id=to, device_id_type=MESH)

    for to in (sib, above, below):
        greet(to)
    loop(PLANE - 1, lambda k: greet(plane(k + 1)[1]))
    pl.semaphore_wait(barrier, 3 + (PLANE - 1))

    q_sib = remote(qsend.at[1 - c], qall.at[chip, c], qs_send, qs_recv, sib)
    q_sib.start()

    def up(step, h):
        return remote(
            kv.at[UP[step - 1], h], kv.at[UP[step], h],
            up_send.at[step - 1, h], up_recv.at[step - 1, h], above,
        )

    def down(step, h):
        return remote(
            kv.at[DOWN[step - 1], h], kv.at[DOWN[step], h],
            dn_send.at[step - 1, h], dn_recv.at[step - 1, h], below,
        )

    def across(slot, h):
        i = SIB_ORDER.index(slot)
        return remote(kv.at[slot, h], kv.at[SIB_OF[slot], h], sb_send.at[i, h], sb_recv.at[i, h], sib)

    def tick(step, h):
        up(step, h).wait_recv()
        if step < 3 or (step == 3 and h == 0):
            up(step + 1, h).start()
        down(step, 1 - h).wait_recv()
        if step < 3 or (step == 3 and h == 0):
            down(step + 1, 1 - h).start()
        across(UP[step], h).start()
        across(DOWN[step], 1 - h).start()

    def crossed(*slots):
        for slot in slots:
            for h in range(2):
                across(slot, h).wait_recv()

    for h in range(2):
        up(1, h).start()
        down(1, 1 - h).start()
    across(0, 0).start()
    across(0, 1).start()
    qall[chip, c] = qsend[c]
    q_sib.wait_recv()

    def q_copy(k):
        _, to = plane(k + 1)
        return remote(qall.at[chip], qall.at[chip], q_send.at[k], q_recv.at[chip], to)

    loop(PLANE - 1, lambda k: q_copy(k).start())

    wo_copy = remote(
        wo_ref.at[:, pl.ds(pl.multiple_of((1 - c) * HALF, 128), HALF)],
        wo.at[own_rows, :], o_send, o_recv, sib,
    )
    wo_copy.start()
    tick(1, 0)
    tick(1, 1)

    def q_arrived(k):
        other, to = plane(k + 1)
        remote(qall.at[other], qall.at[other], q_send.at[k], q_recv.at[other], to).wait_recv()

    loop(PLANE - 1, q_arrived)

    def v_copy(k):
        _, to = owner(k + 1)
        return remote(va_ref.at[0], va.at[j_me], v_send.at[k], v_recv.at[j_me], to)

    loop(OWNERS - 1, lambda k: v_copy(k).start())

    for g in range(2 * PLANE):
        m = qall[g // 2, g % 2]
        q32n[g * 32 : (g + 1) * 32, :] = m[0:32].astype(jnp.float32)
        r = m[32:48].astype(jnp.float32)
        q32r[g * 32 : g * 32 + 16, 0:ROPE] = r[:, :ROPE]
        q32r[g * 32 + 16 : g * 32 + 32, 0:ROPE] = r[:, ROPE:]
    tick(2, 0)


    loop(HEADS, lambda j: load_ka(j).wait())

    for j in range(HEADS):
        rows = slice(j * TOKENS, (j + 1) * TOKENS)
        nope = q32n[pl.ds(j, TOKENS, stride=HEADS), :].astype(jnp.bfloat16)
        part = jnp.dot(nope, ka[j], preferred_element_type=jnp.float32)
        q[rows, 0:LATENT] = (part * SCALE).astype(jnp.bfloat16)
        rope = q32r[pl.ds(j, TOKENS, stride=HEADS), :][:, :ROPE]
        q[rows, LATENT:WIDTH] = (rope * SCALE).astype(jnp.bfloat16)
    tick(2, 1)

    crossed(0)
    attend(True, (0, 1), q, kv, acc, top, tot)
    tick(3, 0)
    crossed(2, 3)
    attend(False, (2, 3, 4, 5), q, kv, acc, top, tot)
    tick(3, 1)
    crossed(6, 7)
    attend(False, (6, 7, 8, 9), q, kv, acc, top, tot)
    up(4, 0).wait_recv()
    down(4, 1).wait_recv()
    across(14, 0).start()
    across(14, 1).start()
    crossed(10, 11)
    attend(False, (10, 11, 12, 13), q, kv, acc, top, tot)

    load_va.wait()

    def v_arrived(k):
        other, to = owner(k + 1)
        remote(va_ref.at[0], va.at[other], v_send.at[k], v_recv.at[other], to).wait_recv()

    loop(OWNERS - 1, v_arrived)
    crossed(14)

    per = TILE // TOKENS
    lane = lax.broadcasted_iota(jnp.int32, (TOKENS, 128), 1)
    row = lax.broadcasted_iota(jnp.int32, (16, 128), 0)
    first_tile = 1 - lax.div(j_me, 4)

    def order(i):
        return first_tile if i == 0 else 1 - first_tile

    def y_copy(other):
        j, t = lax.rem(other, OWNERS), lax.div(other, OWNERS)
        to = (2 * j + c, z, t)
        return remote(ysend.at[j, t], yrecv.at[chip], y_send.at[other], y_recv.at[chip], to)

    def finish(i, latent, new_top, total):
        for h in range(per):
            j = order(i) * per + h
            rows = slice(h * TOKENS, (h + 1) * TOKENS)
            y = jnp.dot(latent[rows], va[j], preferred_element_type=jnp.float32)
            y = y.astype(jnp.bfloat16)
            stats = jnp.where(lane % 2 == 0, new_top[rows], total[rows])
            stats = stats.T[0:16, :]
            high = stats.astype(jnp.bfloat16)
            left = stats - high.astype(jnp.float32)
            middle = left.astype(jnp.bfloat16)
            low = left - middle.astype(jnp.float32)
            stats = jnp.where(
                row < 2,
                high.astype(jnp.float32),
                jnp.where(row < 4, middle.astype(jnp.float32), low),
            ).astype(jnp.bfloat16)
            for t in range(2):
                ysend[j, t, 0:64, :] = y[t * 64 : (t + 1) * 64]
                ysend[j, t, 64:80, :] = stats

        def send(k):
            j, t = order(i) * per + lax.div(k, 2), lax.rem(k, 2)
            other = t * OWNERS + j

            @pl.when(other != chip)
            def _():
                y_copy(other).start()

        loop(2 * per, send)

    attend(False, (14, 15), q, kv, acc, top, tot, order, finish)
    yrecv[chip] = ysend[j_me, dp]

    def y_arrived(k):
        other, to = plane(k + 1)
        remote(yrecv.at[other], yrecv.at[other], y_send.at[k], y_recv.at[other], to).wait_recv()

    loop(PLANE - 1, y_arrived)

    stats = [yrecv[s, 64:80, :].astype(jnp.float32) for s in range(PLANE)]
    tops = jnp.concatenate([x[0:1] + x[2:3] + x[4:5] for x in stats], axis=0)
    sums = jnp.concatenate([x[1:2] + x[3:4] + x[5:6] for x in stats], axis=0)
    weight = sums * jnp.exp2(tops - jnp.max(tops, axis=0, keepdims=True))
    weight = weight / jnp.sum(weight, axis=0, keepdims=True)
    wts[...] = jnp.concatenate([weight, jnp.zeros((128 - PLANE, 128), jnp.float32)], axis=0).T
    w = wts[pl.ds(pl.multiple_of(dp * 64, 64), 64), :]
    merged = None
    for s in range(PLANE):
        term = yrecv[s, 0:64, :].astype(jnp.float32) * w[:, s : s + 1]
        merged = term if merged is None else merged + term
    ho[c] = merged.astype(jnp.bfloat16)
    h_copy = remote(ho.at[c], ho.at[c], h_send, h_recv, sib)
    h_copy.start()
    load_wo.wait()
    wo_copy.wait_recv()
    h_copy.wait_recv()

    heads = jnp.concatenate([ho[0], ho[1]], axis=1)
    def d_copy(i):
        k, part = lax.div(i, 2), lax.rem(i, 2)
        other, to = owner(k + 1)
        return remote(
            dsend.at[part, other], drecv.at[part, j_me], d_send.at[i], d_recv.at[part, j_me], to
        )

    def d_arrived(part, k):
        other, to = owner(k + 1)
        remote(
            dsend.at[part, other], drecv.at[part, other], d_send.at[0], d_recv.at[part, other], to
        ).wait_recv()

    for part in range(2):
        low, high = [
            jnp.dot(
                heads, wo[:, n * COLS : (n + 1) * COLS], preferred_element_type=jnp.float32
            )
            for n in (part, part + 2)
        ]
        for i in range(OWNERS):
            rows = slice(i * 8, (i + 1) * 8)
            dsend[part, i] = jnp.concatenate([low[rows], high[rows]], axis=0).astype(jnp.bfloat16)
        loop(OWNERS - 1, lambda k: d_copy(2 * k + part).start())

    def e_copy(n, core):
        to_z = 4 * c + n
        return (to_z == z) & (core == c), remote(
            esend.at[n, core], erecv.at[z], e_send.at[n, core], e_recv.at[z],
            (2 * j_me + core, to_z, dp),
        )

    for part in range(2):
        drecv[part, j_me] = dsend[part, j_me]
        loop(OWNERS - 1, lambda k: d_arrived(part, k))
        summed = drecv[part, 0].astype(jnp.float32)
        for i in range(1, OWNERS):
            summed = summed + drecv[part, i].astype(jnp.float32)
        for n in (part, part + 2):
            for core in range(2):
                start = (n // 2) * 8 + core * 4
                pieces = [summed[start : start + 4, k * 128 : (k + 1) * 128] for k in range(7)]
                pieces.append(jnp.zeros((4, 128), jnp.float32))
                esend[n, core] = jnp.concatenate(pieces, axis=0).astype(jnp.bfloat16)
                here, copy = e_copy(n, core)

                @pl.when(jnp.logical_not(here))
                def _():
                    copy.start()

                @pl.when(here)
                def _():
                    erecv[z] = esend[n, core]

    from_core = lax.div(z, 4)

    def e_arrived(s):
        frm = (2 * j_me + from_core, s, dp)

        @pl.when(jnp.logical_not((s == z) & (from_core == c)))
        def _():
            remote(esend.at[0, 0], erecv.at[s], e_send.at[0, 0], e_recv.at[s], frm).wait_recv()

    loop(Z, e_arrived)
    result = erecv[0].astype(jnp.float32)
    for s in range(1, Z):
        result = result + erecv[s].astype(jnp.float32)
    for k in range(7):
        out_ref[:, k * 128 : (k + 1) * 128] = result[4 * k : 4 * k + 4]

    q_sib.wait_send()
    for step in range(1, 5):
        for h in range(2):
            if step < 4 or h == 0:
                up(step, h).wait_send()
                down(step, 1 - h).wait_send()
    for slot in SIB_ORDER:
        for h in range(2):
            across(slot, h).wait_send()
    wo_copy.wait_send()
    h_copy.wait_send()

    def sent_plane(k):
        q_copy(k).wait_send()
        y_copy(plane(k + 1)[0]).wait_send()

    loop(PLANE - 1, sent_plane)
    loop(OWNERS - 1, lambda k: v_copy(k).wait_send())
    loop(2 * (OWNERS - 1), lambda i: d_copy(i).wait_send())
    for n in range(4):
        for core in range(2):
            here, copy = e_copy(n, core)

            @pl.when(jnp.logical_not(here))
            def _():
                copy.wait_send()


def body(query_nope, query_rope, latent_cache, key_absorb, value_absorb, output_proj):
    vmem = pl.BlockSpec(memory_space=pltpu.VMEM)
    hbm = pl.BlockSpec(memory_space=pl.ANY)
    bf16, f32 = jnp.bfloat16, jnp.float32
    dma = pltpu.SemaphoreType.DMA
    return pl.pallas_call(
        kernel,
        out_shape=jax.ShapeDtypeStruct((4, COLS), f32),
        in_specs=[vmem, vmem, hbm, hbm, hbm, hbm],
        out_specs=vmem,
        scratch_shapes=[
            pltpu.VMEM((16, 2, HALFB + PACK, LATENT), bf16),
            pltpu.VMEM((ROWS, WIDTH), bf16),
            pltpu.VMEM((ROWS, LATENT), f32),
            pltpu.VMEM((ROWS, 128), f32),
            pltpu.VMEM((ROWS, 128), f32),
            pltpu.VMEM((HEADS, NOPE, LATENT), bf16),
            pltpu.VMEM((HEADS, LATENT, VDIM), bf16),
            pltpu.VMEM((2 * VDIM, HALF), bf16),
            pltpu.VMEM((64, NOPE), f32),
            pltpu.VMEM((64, 128), f32),
            pltpu.VMEM((2, MSG, 128), bf16),
            pltpu.VMEM((PLANE, 2, MSG, 128), bf16),
            pltpu.VMEM((ROWS, NOPE), f32),
            pltpu.VMEM((ROWS, 128), f32),
            pltpu.VMEM((BLOCK, WIDTH), bf16),
            pltpu.VMEM((HEADS, 2, 80, VDIM), bf16),
            pltpu.VMEM((PLANE, 80, VDIM), bf16),
            pltpu.VMEM((128, 128), f32),
            pltpu.VMEM((2, 64, VDIM), bf16),
            pltpu.VMEM((2, OWNERS, 16, COLS), bf16),
            pltpu.VMEM((2, OWNERS, 16, COLS), bf16),
            pltpu.VMEM((4, 2, 32, 128), bf16),
            pltpu.VMEM((Z, 32, 128), bf16),
            dma((11,)),
            dma, dma, dma((PLANE - 1,)), dma((PLANE,)),
            dma((4, 2)), dma((4, 2)), dma((4, 2)), dma((4, 2)), dma((8, 2)), dma((8, 2)),
            dma((OWNERS - 1,)), dma((OWNERS,)), dma, dma,
            dma((PLANE,)), dma((PLANE,)),
            dma, dma, dma((2 * (OWNERS - 1),)), dma((2, OWNERS)), dma((4, 2)), dma((Z,)),
        ],
        compiler_params=pltpu.CompilerParams(
            collective_id=0, has_side_effects=True, vmem_limit_bytes=127 * 512 * 1024
        ),
        cost_estimate=pl.CostEstimate(
            flops=7_000_000_000, bytes_accessed=10_000_000, transcendentals=3_145_728
        ),
        name="latent_attention",
    )(query_nope, query_rope, latent_cache, key_absorb, value_absorb, output_proj)


def solution(mesh):
    in_specs = (
        P(("dp", "prefix"), "head", None),
        P(("dp", "prefix"), "head", None),
        P(("prefix", "head", "dp"), None),
        P("head", None, None),
        P(("head", "prefix"), None, None),
        P(("head", "prefix"), None),
    )
    out_specs = P(("dp", "prefix"), "head")
    return jax.shard_map(body, mesh=mesh, in_specs=in_specs, out_specs=out_specs, check_vma=False)
```

```python
import math

import jax
import jax.numpy as jnp
from jax import lax
from jax.experimental import pallas as pl
from jax.experimental.pallas import tpu as pltpu
from jax.sharding import PartitionSpec as P

MESH = pl.DeviceIdType.MESH

D = 7168
NOPE, ROPE, VDIM, LATENT = 128, 64, 128, 512
WIDTH = LATENT + ROPE
TOKENS = 128
Z = 8
PLANE = 16
OWNERS = 8
HEADS = 8
ROWS = HEADS * TOKENS
BLOCK = 192
MSG = 48
QUARTER = D // 4
COLS = D // Z
SCALE = (NOPE + ROPE) ** -0.5 * math.log2(math.e)

HALFB = BLOCK // 2
PACK = 16
UP = (0, 2, 6, 10, 14)
DOWN = (0, 3, 7, 11, 14)
SIB_OF = {0: 1, 2: 4, 3: 5, 6: 8, 7: 9, 10: 12, 11: 13, 14: 15}
SIB_ORDER = (0, 2, 3, 6, 7, 10, 11, 14)
TILE = 512


def chunk_keys(kv, blocks):
    latent, rope = [], []
    for b in blocks:
        for h in range(2):
            latent.append(kv[b, h, 0:HALFB, :])
            packed = kv[b, h, HALFB : HALFB + PACK, 0 : 6 * ROPE]
            for g in range(6):
                rope.append(packed[:, g * ROPE : (g + 1) * ROPE])
    latent = jnp.concatenate(latent, axis=0)
    return jnp.concatenate([latent, jnp.concatenate(rope, axis=0)], axis=1), latent


def attend(first, blocks, q, kv, acc, top, tot, order=None, finish=None):
    keys, values = chunk_keys(kv, blocks)
    n = ROWS // TILE

    def at(i):
        if order is None:
            return pl.ds(i * TILE, TILE)
        return pl.ds(pl.multiple_of(order(i) * TILE, TILE), TILE)

    def score(i):
        return lax.dot_general(
            q[at(i), :], keys, (((1,), (1,)), ((), ())), preferred_element_type=jnp.float32
        )

    s = score(0)
    for i in range(n):
        later = score(i + 1) if i + 1 < n else None
        rows = at(i)
        high = jnp.max(s, axis=1, keepdims=True)
        if first:
            new_top = jnp.broadcast_to(high, (TILE, 128))
        else:
            old_top = top[rows, :]
            new_top = jnp.maximum(old_top, high)
            alpha = jnp.exp2(old_top - new_top)
        part = None
        pieces = []
        for k in range(s.shape[1] // 128):
            e = jnp.exp2(s[:, k * 128 : (k + 1) * 128] - new_top)
            part = e if part is None else part + e
            pieces.append(e.astype(jnp.bfloat16))
        p = jnp.concatenate(pieces, axis=1)
        out = jnp.dot(p, values, preferred_element_type=jnp.float32)
        if not first:
            part = tot[rows, :] * alpha + part
        if finish is not None:
            total = jnp.sum(part, axis=1, keepdims=True)
            scale = 1.0 / total
            latent = []
            for k in range(LATENT // 128):
                cols = slice(k * 128, (k + 1) * 128)
                latent.append(((acc[rows, cols] * alpha + out[:, cols]) * scale).astype(jnp.bfloat16))
            finish(i, jnp.concatenate(latent, axis=1), new_top, total)
        else:
            top[rows, :] = new_top
            tot[rows, :] = part
            for k in range(LATENT // 128):
                cols = slice(k * 128, (k + 1) * 128)
                if first:
                    acc[rows, cols] = out[:, cols]
                else:
                    acc[rows, cols] = acc[rows, cols] * alpha + out[:, cols]
        s = later


def kernel(
    qn_ref, qr_ref, kv_ref, ka_ref, va_ref, wo_ref, out_ref,
    kv, q, acc, top, tot, ka, va, wo,
    tmpn, tmpr, qsend, qall, q32n, q32r,
    kvraw, ysend, yrecv, wts, ho, dsend, drecv, esend, erecv,
    local, qs_send, qs_recv, q_send, q_recv,
    up_send, up_recv, dn_send, dn_recv, sb_send, sb_recv,
    vy_send, vy_recv, vf_send, vf_recv, vx_send, vx_recv, o_send, o_recv, ox_send, ox_recv,
    y_send, y_recv, h_send, h_recv, d_send, d_recv, e_send, e_recv,
):
    prefix, z, dp = lax.axis_index("prefix"), lax.axis_index("head"), lax.axis_index("dp")
    c = lax.rem(prefix, 2)
    j_me = lax.div(prefix, 2)
    chip = dp * OWNERS + j_me
    sib = (prefix + 1 - 2 * c, z, dp)
    above = (prefix, lax.rem(z + 1, Z), dp)
    below = (prefix, lax.rem(z + Z - 1, Z), dp)

    def plane(k):
        other = lax.rem(chip + k, PLANE)
        return other, (2 * lax.rem(other, OWNERS) + c, z, lax.div(other, OWNERS))

    xl, yy = lax.div(j_me, 4), lax.rem(j_me, 4)
    x = 2 * dp + xl
    quarter = 2 * xl + c

    def at(x_to, y_to, core):
        x_to, y_to = lax.rem(x_to, 4), lax.rem(y_to, 4)
        return ((lax.rem(x_to, 2) * 4 + y_to) * 2 + core, z, lax.div(x_to, 2))

    def head_of(x_low, y_of):
        return x_low * 4 + lax.rem(y_of, 4)

    def columns(quarter_of):
        return pl.ds(pl.multiple_of(quarter_of * QUARTER, 128), QUARTER)

    def remote(src, dst, ssem, rsem, to):
        return pltpu.make_async_remote_copy(
            src_ref=src, dst_ref=dst, send_sem=ssem, recv_sem=rsem, device_id=to, device_id_type=MESH
        )

    def loop(n, body):
        def step(k, carry):
            body(k)
            return carry

        lax.fori_loop(0, n, step, 0)

    def load_ka(j):
        return pltpu.make_async_copy(ka_ref.at[2 * j + c], ka.at[j], local.at[j])

    loop(HEADS, lambda j: load_ka(j).start())
    load_kv = pltpu.make_async_copy(kv_ref, kvraw, local.at[8])
    load_kv.start()
    load_va = pltpu.make_async_copy(va_ref.at[0], va.at[j_me], local.at[9])
    load_va.start()
    own_rows = pl.ds(pl.multiple_of(quarter * VDIM, VDIM), VDIM)
    load_wo = pltpu.make_async_copy(wo_ref.at[:, columns(quarter)], wo.at[own_rows, :], local.at[10])
    load_wo.start()

    tmpn[...] = qn_ref[...].astype(jnp.float32).reshape(64, NOPE)
    tmpr[:, :ROPE] = qr_ref[...].astype(jnp.float32).reshape(64, ROPE)
    for parity in range(2):
        qsend[parity, 0:32, :] = tmpn[pl.ds(parity, 32, stride=2), :].astype(jnp.bfloat16)
        rope = tmpr[pl.ds(parity, 32, stride=2), :][:, :ROPE]
        qsend[parity, 32:48, :] = jnp.concatenate([rope[:16], rope[16:]], axis=1).astype(
            jnp.bfloat16
        )

    load_kv.wait()
    for h in range(2):
        rows = slice(h * HALFB, (h + 1) * HALFB)
        kv[0, h, 0:HALFB, :] = kvraw[rows, 0:LATENT]
        rope = kvraw[rows, LATENT:WIDTH].astype(jnp.float32)
        packed = [rope[g * PACK : (g + 1) * PACK] for g in range(6)]
        packed.append(jnp.zeros((PACK, LATENT - 6 * ROPE), jnp.float32))
        kv[0, h, HALFB : HALFB + PACK, :] = jnp.concatenate(packed, axis=1).astype(jnp.bfloat16)

    barrier = pltpu.get_barrier_semaphore()

    def greet(to):
        pl.semaphore_signal(barrier, inc=1, device_id=to, device_id_type=MESH)

    for to in (sib, above, below):
        greet(to)
    loop(PLANE - 1, lambda k: greet(plane(k + 1)[1]))
    pl.semaphore_wait(barrier, 3 + (PLANE - 1))

    q_sib = remote(qsend.at[1 - c], qall.at[chip, c], qs_send, qs_recv, sib)
    q_sib.start()

    def up(step, h):
        return remote(
            kv.at[UP[step - 1], h], kv.at[UP[step], h],
            up_send.at[step - 1, h], up_recv.at[step - 1, h], above,
        )

    def down(step, h):
        return remote(
            kv.at[DOWN[step - 1], h], kv.at[DOWN[step], h],
            dn_send.at[step - 1, h], dn_recv.at[step - 1, h], below,
        )

    def across(slot, h):
        i = SIB_ORDER.index(slot)
        return remote(kv.at[slot, h], kv.at[SIB_OF[slot], h], sb_send.at[i, h], sb_recv.at[i, h], sib)

    def tick(step, h):
        up(step, h).wait_recv()
        if step < 3 or (step == 3 and h == 0):
            up(step + 1, h).start()
        down(step, 1 - h).wait_recv()
        if step < 3 or (step == 3 and h == 0):
            down(step + 1, 1 - h).start()
        across(UP[step], h).start()
        across(DOWN[step], 1 - h).start()

    def crossed(*slots):
        for slot in slots:
            for h in range(2):
                across(slot, h).wait_recv()

    for h in range(2):
        up(1, h).start()
        down(1, 1 - h).start()
    across(0, 0).start()
    across(0, 1).start()
    qall[chip, c] = qsend[c]
    q_sib.wait_recv()

    def q_copy(k):
        _, to = plane(k + 1)
        return remote(qall.at[chip], qall.at[chip], q_send.at[k], q_recv.at[chip], to)

    loop(PLANE - 1, lambda k: q_copy(k).start())

    wo_copy = remote(wo_ref.at[:, columns(2 * xl + 1 - c)], wo.at[own_rows, :], o_send, o_recv, sib)
    wo_copy.start()

    def wo_x(way, core):
        return remote(
            wo_ref.at[pl.ds(way * 64, 64), columns(2 * (1 - xl) + core)],
            wo.at[pl.ds(pl.multiple_of(quarter * VDIM + way * 64, 64), 64), :],
            ox_send.at[way, core], ox_recv.at[way, c], at(x + 1 + 2 * way, yy, core),
        )

    def wo_x_arrived(way, core):
        rows = pl.ds(pl.multiple_of((2 * (1 - xl) + core) * VDIM + way * 64, 64), 64)
        remote(
            wo.at[rows, :], wo.at[rows, :], ox_send.at[way, core], ox_recv.at[way, core],
            at(x + 3 - 2 * way, yy, core),
        ).wait_recv()

    tick(1, 0)
    tick(1, 1)

    def q_arrived(k):
        other, to = plane(k + 1)
        remote(qall.at[other], qall.at[other], q_send.at[k], q_recv.at[other], to).wait_recv()

    loop(PLANE - 1, q_arrived)

    def v_y(way):
        return remote(
            va_ref.at[0], va.at[j_me], vy_send.at[way], vy_recv.at[way], at(x, yy + 1 + 2 * way, c)
        )

    def v_relay(way):
        half = va.at[head_of(xl, yy + 3 - 2 * way), pl.ds(way * 256, 256), :]
        return remote(half, half, vf_send.at[way], vf_recv.at[way], at(x, yy + 1 + 2 * way, c))

    def v_x(i, way):
        half = va.at[head_of(xl, yy + i), pl.ds(way * 256, 256), :]
        src = va_ref.at[0, pl.ds(way * 256, 256), :] if i == 0 else half
        return remote(src, half, vx_send.at[i, way], vx_recv.at[i, way], at(x + 1 + 2 * way, yy, c))

    for way in range(2):
        v_y(way).start()
        v_x(0, way).start()

    for g in range(2 * PLANE):
        m = qall[g // 2, g % 2]
        q32n[g * 32 : (g + 1) * 32, :] = m[0:32].astype(jnp.float32)
        r = m[32:48].astype(jnp.float32)
        q32r[g * 32 : g * 32 + 16, 0:ROPE] = r[:, :ROPE]
        q32r[g * 32 + 16 : g * 32 + 32, 0:ROPE] = r[:, ROPE:]
    tick(2, 0)


    loop(HEADS, lambda j: load_ka(j).wait())

    for j in range(HEADS):
        rows = slice(j * TOKENS, (j + 1) * TOKENS)
        nope = q32n[pl.ds(j, TOKENS, stride=HEADS), :].astype(jnp.bfloat16)
        part = jnp.dot(nope, ka[j], preferred_element_type=jnp.float32)
        q[rows, 0:LATENT] = (part * SCALE).astype(jnp.bfloat16)
        rope = q32r[pl.ds(j, TOKENS, stride=HEADS), :][:, :ROPE]
        q[rows, LATENT:WIDTH] = (rope * SCALE).astype(jnp.bfloat16)
    tick(2, 1)

    crossed(0)
    attend(True, (0, 1), q, kv, acc, top, tot)
    for way in range(2):
        v_y(way).wait_recv()
        v_relay(way).start()
    for way in range(2):
        v_x(3, way).start()
        v_x(1, way).start()
    tick(3, 0)
    crossed(2, 3)
    attend(False, (2, 3, 4, 5), q, kv, acc, top, tot)
    for way in range(2):
        v_relay(way).wait_recv()
        v_x(2, way).start()
    for way in range(2):
        for core in range(2):
            wo_x(way, core).start()
    tick(3, 1)
    crossed(6, 7)
    attend(False, (6, 7, 8, 9), q, kv, acc, top, tot)
    up(4, 0).wait_recv()
    down(4, 1).wait_recv()
    across(14, 0).start()
    across(14, 1).start()
    crossed(10, 11)
    attend(False, (10, 11, 12, 13), q, kv, acc, top, tot)

    load_va.wait()

    for i in range(4):
        for way in range(2):
            v_x(i, way).wait_recv()
    crossed(14)

    per = TILE // TOKENS
    lane = lax.broadcasted_iota(jnp.int32, (TOKENS, 128), 1)
    row = lax.broadcasted_iota(jnp.int32, (16, 128), 0)
    first_tile = 1 - lax.div(j_me, 4)

    def order(i):
        return first_tile if i == 0 else 1 - first_tile

    def y_copy(other):
        j, t = lax.rem(other, OWNERS), lax.div(other, OWNERS)
        to = (2 * j + c, z, t)
        return remote(ysend.at[j, t], yrecv.at[chip], y_send.at[other], y_recv.at[chip], to)

    def finish(i, latent, new_top, total):
        for h in range(per):
            j = order(i) * per + h
            rows = slice(h * TOKENS, (h + 1) * TOKENS)
            y = jnp.dot(latent[rows], va[j], preferred_element_type=jnp.float32)
            y = y.astype(jnp.bfloat16)
            stats = jnp.where(lane % 2 == 0, new_top[rows], total[rows])
            stats = stats.T[0:16, :]
            high = stats.astype(jnp.bfloat16)
            left = stats - high.astype(jnp.float32)
            middle = left.astype(jnp.bfloat16)
            low = left - middle.astype(jnp.float32)
            stats = jnp.where(
                row < 2,
                high.astype(jnp.float32),
                jnp.where(row < 4, middle.astype(jnp.float32), low),
            ).astype(jnp.bfloat16)
            for t in range(2):
                ysend[j, t, 0:64, :] = y[t * 64 : (t + 1) * 64]
                ysend[j, t, 64:80, :] = stats

        def send(k):
            j, t = order(i) * per + lax.div(k, 2), lax.rem(k, 2)
            other = t * OWNERS + j

            @pl.when(other != chip)
            def _():
                y_copy(other).start()

        loop(2 * per, send)

    attend(False, (14, 15), q, kv, acc, top, tot, order, finish)
    yrecv[chip] = ysend[j_me, dp]

    def y_arrived(k):
        other, to = plane(k + 1)
        remote(yrecv.at[other], yrecv.at[other], y_send.at[k], y_recv.at[other], to).wait_recv()

    loop(PLANE - 1, y_arrived)

    stats = [yrecv[s, 64:80, :].astype(jnp.float32) for s in range(PLANE)]
    tops = jnp.concatenate([x[0:1] + x[2:3] + x[4:5] for x in stats], axis=0)
    sums = jnp.concatenate([x[1:2] + x[3:4] + x[5:6] for x in stats], axis=0)
    weight = sums * jnp.exp2(tops - jnp.max(tops, axis=0, keepdims=True))
    weight = weight / jnp.sum(weight, axis=0, keepdims=True)
    wts[...] = jnp.concatenate([weight, jnp.zeros((128 - PLANE, 128), jnp.float32)], axis=0).T
    w = wts[pl.ds(pl.multiple_of(dp * 64, 64), 64), :]
    merged = None
    for s in range(PLANE):
        term = yrecv[s, 0:64, :].astype(jnp.float32) * w[:, s : s + 1]
        merged = term if merged is None else merged + term
    ho[quarter] = merged.astype(jnp.bfloat16)

    def h_copy(k):
        core = 1 - c if k % 2 else c
        x_low = 1 - xl if k >= 2 else xl
        return remote(
            ho.at[quarter], ho.at[quarter], h_send.at[k - 1], h_recv.at[k - 1], at(2 * dp + x_low, yy, core)
        )

    for k in (2, 3, 1):
        h_copy(k).start()
    load_wo.wait()
    wo_copy.wait_recv()
    for way in range(2):
        for core in range(2):
            wo_x_arrived(way, core)
    for k in (1, 2, 3):
        h_copy(k).wait_recv()

    heads = jnp.concatenate([ho[k] for k in range(4)], axis=1)

    def d_copy(n, k):
        other = lax.rem(yy + k, 4)
        return remote(
            dsend.at[n, other], drecv.at[n, yy], d_send.at[n, k - 1], d_recv.at[n, yy], at(x, other, c)
        )

    def d_arrived(n, k):
        other = lax.rem(yy + k, 4)
        remote(
            dsend.at[n, other], drecv.at[n, other], d_send.at[n, k - 1], d_recv.at[n, other],
            at(x, other, c),
        ).wait_recv()

    for n in range(2):
        terms = jnp.dot(
            heads, wo[:, n * COLS : (n + 1) * COLS], preferred_element_type=jnp.float32
        )
        for i in range(4):
            dsend[n, i] = jnp.concatenate(
                [terms[i * 8 : i * 8 + 8], terms[32 + i * 8 : 40 + i * 8]], axis=0
            ).astype(jnp.bfloat16)
        for k in (2, 1, 3):
            d_copy(n, k).start()

    def e_copy(n, x_low, core):
        to_z = 2 * quarter + n
        return (to_z == z) & (x_low == xl) & (core == c), remote(
            esend.at[n, x_low, core], erecv.at[z], e_send.at[n, x_low, core], e_recv.at[z],
            ((4 * x_low + yy) * 2 + core, to_z, dp),
        )

    for n in range(2):
        drecv[n, yy] = dsend[n, yy]
        for k in (1, 3, 2):
            d_arrived(n, k)
        summed = drecv[n, 0].astype(jnp.float32)
        for i in range(1, 4):
            summed = summed + drecv[n, i].astype(jnp.float32)
        for x_low in range(2):
            for core in range(2):
                start = x_low * 8 + core * 4
                pieces = [summed[start : start + 4, k * 128 : (k + 1) * 128] for k in range(7)]
                pieces.append(jnp.zeros((4, 128), jnp.float32))
                esend[n, x_low, core] = jnp.concatenate(pieces, axis=0).astype(jnp.bfloat16)
                here, copy = e_copy(n, x_low, core)

                @pl.when(jnp.logical_not(here))
                def _():
                    copy.start()

                @pl.when(here)
                def _():
                    erecv[z] = esend[n, x_low, core]

    from_x, from_core = lax.div(z, 4), lax.rem(lax.div(z, 2), 2)

    def e_arrived(s):
        frm = ((4 * from_x + yy) * 2 + from_core, s, dp)

        @pl.when(jnp.logical_not((s == z) & (from_x == xl) & (from_core == c)))
        def _():
            remote(
                esend.at[0, 0, 0], erecv.at[s], e_send.at[0, 0, 0], e_recv.at[s], frm
            ).wait_recv()

    loop(Z, e_arrived)
    result = erecv[0].astype(jnp.float32)
    for s in range(1, Z):
        result = result + erecv[s].astype(jnp.float32)
    for k in range(7):
        out_ref[:, k * 128 : (k + 1) * 128] = result[4 * k : 4 * k + 4]

    q_sib.wait_send()
    for step in range(1, 5):
        for h in range(2):
            if step < 4 or h == 0:
                up(step, h).wait_send()
                down(step, 1 - h).wait_send()
    for slot in SIB_ORDER:
        for h in range(2):
            across(slot, h).wait_send()
    wo_copy.wait_send()
    for k in (1, 2, 3):
        h_copy(k).wait_send()

    def sent_plane(k):
        q_copy(k).wait_send()
        y_copy(plane(k + 1)[0]).wait_send()

    loop(PLANE - 1, sent_plane)
    for way in range(2):
        v_y(way).wait_send()
        v_relay(way).wait_send()
        for i in range(4):
            v_x(i, way).wait_send()
        for core in range(2):
            wo_x(way, core).wait_send()
    for n in range(2):
        for k in (1, 2, 3):
            d_copy(n, k).wait_send()
        for x_low in range(2):
            for core in range(2):
                here, copy = e_copy(n, x_low, core)

                @pl.when(jnp.logical_not(here))
                def _():
                    copy.wait_send()


def body(query_nope, query_rope, latent_cache, key_absorb, value_absorb, output_proj):
    vmem = pl.BlockSpec(memory_space=pltpu.VMEM)
    hbm = pl.BlockSpec(memory_space=pl.ANY)
    bf16, f32 = jnp.bfloat16, jnp.float32
    dma = pltpu.SemaphoreType.DMA
    return pl.pallas_call(
        kernel,
        out_shape=jax.ShapeDtypeStruct((4, COLS), f32),
        in_specs=[vmem, vmem, hbm, hbm, hbm, hbm],
        out_specs=vmem,
        scratch_shapes=[
            pltpu.VMEM((16, 2, HALFB + PACK, LATENT), bf16),
            pltpu.VMEM((ROWS, WIDTH), bf16),
            pltpu.VMEM((ROWS, LATENT), f32),
            pltpu.VMEM((ROWS, 128), f32),
            pltpu.VMEM((ROWS, 128), f32),
            pltpu.VMEM((HEADS, NOPE, LATENT), bf16),
            pltpu.VMEM((HEADS, LATENT, VDIM), bf16),
            pltpu.VMEM((4 * VDIM, QUARTER), bf16),
            pltpu.VMEM((64, NOPE), f32),
            pltpu.VMEM((64, 128), f32),
            pltpu.VMEM((2, MSG, 128), bf16),
            pltpu.VMEM((PLANE, 2, MSG, 128), bf16),
            pltpu.VMEM((ROWS, NOPE), f32),
            pltpu.VMEM((ROWS, 128), f32),
            pltpu.VMEM((BLOCK, WIDTH), bf16),
            pltpu.VMEM((HEADS, 2, 80, VDIM), bf16),
            pltpu.VMEM((PLANE, 80, VDIM), bf16),
            pltpu.VMEM((128, 128), f32),
            pltpu.VMEM((4, 64, VDIM), bf16),
            pltpu.VMEM((2, 4, 16, COLS), bf16),
            pltpu.VMEM((2, 4, 16, COLS), bf16),
            pltpu.VMEM((2, 2, 2, 32, 128), bf16),
            pltpu.VMEM((Z, 32, 128), bf16),
            dma((11,)),
            dma, dma, dma((PLANE - 1,)), dma((PLANE,)),
            dma((4, 2)), dma((4, 2)), dma((4, 2)), dma((4, 2)), dma((8, 2)), dma((8, 2)),
            dma((2,)), dma((2,)), dma((2,)), dma((2,)), dma((4, 2)), dma((4, 2)),
            dma, dma, dma((2, 2)), dma((2, 2)),
            dma((PLANE,)), dma((PLANE,)),
            dma((3,)), dma((3,)), dma((2, 3)), dma((2, 4)), dma((2, 2, 2)), dma((Z,)),
        ],
        compiler_params=pltpu.CompilerParams(
            collective_id=0, has_side_effects=True, vmem_limit_bytes=127 * 512 * 1024
        ),
        cost_estimate=pl.CostEstimate(
            flops=7_000_000_000, bytes_accessed=10_000_000, transcendentals=3_145_728
        ),
        name="latent_attention",
    )(query_nope, query_rope, latent_cache, key_absorb, value_absorb, output_proj)


def solution(mesh):
    in_specs = (
        P(("dp", "prefix"), "head", None),
        P(("dp", "prefix"), "head", None),
        P(("prefix", "head", "dp"), None),
        P("head", None, None),
        P(("head", "prefix"), None, None),
        P(("head", "prefix"), None),
    )
    out_specs = P(("dp", "prefix"), "head")
    return jax.shard_map(body, mesh=mesh, in_specs=in_specs, out_specs=out_specs, check_vma=False)
```

```python
import math

import jax
import jax.numpy as jnp
from jax import lax
from jax.experimental import pallas as pl
from jax.experimental.pallas import tpu as pltpu
from jax.sharding import PartitionSpec as P

MESH = pl.DeviceIdType.MESH

D = 7168
NOPE, ROPE, VDIM, LATENT = 128, 64, 128, 512
WIDTH = LATENT + ROPE
TOKENS = 128
Z = 8
PLANE = 16
OWNERS = 8
HEADS = 8
ROWS = HEADS * TOKENS
BLOCK = 192
MSG = 48
QUARTER = D // 4
COLS = D // Z
SCALE = (NOPE + ROPE) ** -0.5 * math.log2(math.e)

HALFB = BLOCK // 2
PACK = 16
UP = (0, 2, 6, 10, 14)
DOWN = (0, 3, 7, 11, 14)
SIB_OF = {0: 1, 2: 4, 3: 5, 6: 8, 7: 9, 10: 12, 11: 13, 14: 15}
SIB_ORDER = (0, 2, 3, 6, 7, 10, 11, 14)
TILE = 512


def chunk_keys(kv, blocks):
    latent, rope = [], []
    for b in blocks:
        for h in range(2):
            latent.append(kv[b, h, 0:HALFB, :])
            packed = kv[b, h, HALFB : HALFB + PACK, 0 : 6 * ROPE]
            for g in range(6):
                rope.append(packed[:, g * ROPE : (g + 1) * ROPE])
    latent = jnp.concatenate(latent, axis=0)
    return jnp.concatenate([latent, jnp.concatenate(rope, axis=0)], axis=1), latent


def attend(first, blocks, q, kv, acc, top, tot, order=None, finish=None):
    keys, values = chunk_keys(kv, blocks)
    n = ROWS // TILE

    def at(i):
        if order is None:
            return pl.ds(i * TILE, TILE)
        return pl.ds(pl.multiple_of(order(i) * TILE, TILE), TILE)

    def score(i):
        return lax.dot_general(
            q[at(i), :], keys, (((1,), (1,)), ((), ())), preferred_element_type=jnp.float32
        )

    s = score(0)
    for i in range(n):
        later = score(i + 1) if i + 1 < n else None
        rows = at(i)
        high = jnp.max(s, axis=1, keepdims=True)
        if first:
            new_top = jnp.broadcast_to(high, (TILE, 128))
        else:
            old_top = top[rows, :]
            new_top = jnp.maximum(old_top, high)
            alpha = jnp.exp2(old_top - new_top)
        part = None
        pieces = []
        for k in range(s.shape[1] // 128):
            e = jnp.exp2(s[:, k * 128 : (k + 1) * 128] - new_top)
            part = e if part is None else part + e
            pieces.append(e.astype(jnp.bfloat16))
        p = jnp.concatenate(pieces, axis=1)
        out = jnp.dot(p, values, preferred_element_type=jnp.float32)
        if not first:
            part = tot[rows, :] * alpha + part
        if finish is not None:
            total = jnp.sum(part, axis=1, keepdims=True)
            scale = 1.0 / total
            latent = []
            for k in range(LATENT // 128):
                cols = slice(k * 128, (k + 1) * 128)
                latent.append(((acc[rows, cols] * alpha + out[:, cols]) * scale).astype(jnp.bfloat16))
            finish(i, jnp.concatenate(latent, axis=1), new_top, total)
        else:
            top[rows, :] = new_top
            tot[rows, :] = part
            for k in range(LATENT // 128):
                cols = slice(k * 128, (k + 1) * 128)
                if first:
                    acc[rows, cols] = out[:, cols]
                else:
                    acc[rows, cols] = acc[rows, cols] * alpha + out[:, cols]
        s = later


def kernel(
    qn_ref, qr_ref, kv_ref, ka_ref, va_ref, wo_ref, out_ref,
    kv, q, acc, top, tot, ka, va, wo,
    qn, qr, tmpn, tmpr, qsend, qall, q32n, q32r,
    kvraw, ysend, yrecv, wts, ho, esend, erecv,
    local, qs_send, qs_recv, q_send, q_recv,
    up_send, up_recv, dn_send, dn_recv, sb_send, sb_recv,
    vy_send, vy_recv, vf_send, vf_recv, vx_send, vx_recv, o_send, o_recv, ox_send, ox_recv,
    y_send, y_recv, h_send, h_recv, e_send, e_recv,
):
    prefix, z, dp = lax.axis_index("prefix"), lax.axis_index("head"), lax.axis_index("dp")
    c = lax.rem(prefix, 2)
    j_me = lax.div(prefix, 2)
    chip = dp * OWNERS + j_me
    sib = (prefix + 1 - 2 * c, z, dp)
    above = (prefix, lax.rem(z + 1, Z), dp)
    below = (prefix, lax.rem(z + Z - 1, Z), dp)

    def plane(k):
        other = lax.rem(chip + k, PLANE)
        return other, (2 * lax.rem(other, OWNERS) + c, z, lax.div(other, OWNERS))

    xl, yy = lax.div(j_me, 4), lax.rem(j_me, 4)
    x = 2 * dp + xl
    quarter = 2 * xl + c

    def at(x_to, y_to, core):
        x_to, y_to = lax.rem(x_to, 4), lax.rem(y_to, 4)
        return ((lax.rem(x_to, 2) * 4 + y_to) * 2 + core, z, lax.div(x_to, 2))

    def head_of(x_low, y_of):
        return x_low * 4 + lax.rem(y_of, 4)

    def columns(quarter_of):
        return pl.ds(pl.multiple_of(quarter_of * QUARTER, 128), QUARTER)

    def remote(src, dst, ssem, rsem, to):
        return pltpu.make_async_remote_copy(
            src_ref=src, dst_ref=dst, send_sem=ssem, recv_sem=rsem, device_id=to, device_id_type=MESH
        )

    def loop(n, body):
        def step(k, carry):
            body(k)
            return carry

        lax.fori_loop(0, n, step, 0)

    def load_ka(j):
        return pltpu.make_async_copy(ka_ref.at[2 * j + c], ka.at[j], local.at[j])

    load_kv = pltpu.make_async_copy(kv_ref, kvraw, local.at[8])
    load_kv.start()
    load_qn = pltpu.make_async_copy(qn_ref, qn, local.at[11])
    load_qn.start()
    load_qr = pltpu.make_async_copy(qr_ref, qr, local.at[12])
    load_qr.start()

    barrier = pltpu.get_barrier_semaphore()

    def greet(to):
        pl.semaphore_signal(barrier, inc=1, device_id=to, device_id_type=MESH)

    loop(PLANE - 1, lambda k: greet(plane(k + 1)[1]))
    for to in (above, below, sib):
        greet(to)

    loop(HEADS, lambda j: load_ka(j).start())
    load_va = pltpu.make_async_copy(va_ref.at[0], va.at[j_me], local.at[9])
    load_va.start()
    own_rows = pl.ds(pl.multiple_of(quarter * VDIM, VDIM), VDIM)
    load_wo = pltpu.make_async_copy(wo_ref.at[:, columns(quarter)], wo.at[own_rows, :], local.at[10])
    load_wo.start()

    load_kv.wait()
    for h in range(2):
        rows = slice(h * HALFB, (h + 1) * HALFB)
        kv[0, h, 0:HALFB, :] = kvraw[rows, 0:LATENT]
        rope = kvraw[rows, LATENT:WIDTH].astype(jnp.float32)
        packed = [rope[g * PACK : (g + 1) * PACK] for g in range(6)]
        packed.append(jnp.zeros((PACK, LATENT - 6 * ROPE), jnp.float32))
        kv[0, h, HALFB : HALFB + PACK, :] = jnp.concatenate(packed, axis=1).astype(jnp.bfloat16)

    load_qn.wait()
    load_qr.wait()
    tmpn[...] = qn[...].astype(jnp.float32).reshape(64, NOPE)
    tmpr[:, :ROPE] = qr[...].astype(jnp.float32).reshape(64, ROPE)
    for parity in range(2):
        qsend[parity, 0:32, :] = tmpn[pl.ds(parity, 32, stride=2), :].astype(jnp.bfloat16)
        rope = tmpr[pl.ds(parity, 32, stride=2), :][:, :ROPE]
        qsend[parity, 32:48, :] = jnp.concatenate([rope[:16], rope[16:]], axis=1).astype(
            jnp.bfloat16
        )
    pl.semaphore_wait(barrier, 3 + (PLANE - 1))

    q_sib = remote(qsend.at[1 - c], qall.at[chip, c], qs_send, qs_recv, sib)
    q_sib.start()

    def up(step, h):
        return remote(
            kv.at[UP[step - 1], h], kv.at[UP[step], h],
            up_send.at[step - 1, h], up_recv.at[step - 1, h], above,
        )

    def down(step, h):
        return remote(
            kv.at[DOWN[step - 1], h], kv.at[DOWN[step], h],
            dn_send.at[step - 1, h], dn_recv.at[step - 1, h], below,
        )

    def across(slot, h):
        i = SIB_ORDER.index(slot)
        return remote(kv.at[slot, h], kv.at[SIB_OF[slot], h], sb_send.at[i, h], sb_recv.at[i, h], sib)

    def tick(step, h):
        up(step, h).wait_recv()
        if step < 3 or (step == 3 and h == 0):
            up(step + 1, h).start()
        down(step, 1 - h).wait_recv()
        if step < 3 or (step == 3 and h == 0):
            down(step + 1, 1 - h).start()
        across(UP[step], h).start()
        across(DOWN[step], 1 - h).start()

    def crossed(*slots):
        for slot in slots:
            for h in range(2):
                across(slot, h).wait_recv()

    for h in range(2):
        up(1, h).start()
        down(1, 1 - h).start()
    across(0, 0).start()
    across(0, 1).start()
    def v_y(way):
        return remote(
            va_ref.at[0], va.at[j_me], vy_send.at[way], vy_recv.at[way], at(x, yy + 1 + 2 * way, c)
        )

    def v_relay(way):
        half = va.at[head_of(xl, yy + 3 - 2 * way), pl.ds(way * 256, 256), :]
        return remote(half, half, vf_send.at[way], vf_recv.at[way], at(x, yy + 1 + 2 * way, c))

    def v_x(i, way):
        half = va.at[head_of(xl, yy + i), pl.ds(way * 256, 256), :]
        src = va_ref.at[0, pl.ds(way * 256, 256), :] if i == 0 else half
        return remote(src, half, vx_send.at[i, way], vx_recv.at[i, way], at(x + 1 + 2 * way, yy, c))

    for way in range(2):
        v_y(way).start()
        v_x(0, way).start()

    qall[chip, c] = qsend[c]
    q_sib.wait_recv()

    def q_copy(k):
        _, to = plane(k + 1)
        return remote(qall.at[chip], qall.at[chip], q_send.at[k], q_recv.at[chip], to)

    loop(PLANE - 1, lambda k: q_copy(k).start())

    wo_copy = remote(wo_ref.at[:, columns(2 * xl + 1 - c)], wo.at[own_rows, :], o_send, o_recv, sib)
    wo_copy.start()

    def wo_x(way, core):
        return remote(
            wo_ref.at[pl.ds(way * 64, 64), columns(2 * (1 - xl) + core)],
            wo.at[pl.ds(pl.multiple_of(quarter * VDIM + way * 64, 64), 64), :],
            ox_send.at[way, core], ox_recv.at[way, c], at(x + 1 + 2 * way, yy, core),
        )

    def wo_x_arrived(way, core):
        rows = pl.ds(pl.multiple_of((2 * (1 - xl) + core) * VDIM + way * 64, 64), 64)
        remote(
            wo.at[rows, :], wo.at[rows, :], ox_send.at[way, core], ox_recv.at[way, core],
            at(x + 3 - 2 * way, yy, core),
        ).wait_recv()

    tick(1, 0)
    tick(1, 1)

    def q_arrived(k):
        other, to = plane(k + 1)
        remote(qall.at[other], qall.at[other], q_send.at[k], q_recv.at[other], to).wait_recv()

    loop(PLANE - 1, q_arrived)
    for way in range(2):
        v_y(way).wait_recv()
        v_relay(way).start()
    for way in range(2):
        v_x(3, way).start()
        v_x(1, way).start()
    for way in range(2):
        for core in range(2):
            wo_x(way, core).start()

    for g in range(2 * PLANE):
        m = qall[g // 2, g % 2]
        q32n[g * 32 : (g + 1) * 32, :] = m[0:32].astype(jnp.float32)
        r = m[32:48].astype(jnp.float32)
        q32r[g * 32 : g * 32 + 16, 0:ROPE] = r[:, :ROPE]
        q32r[g * 32 + 16 : g * 32 + 32, 0:ROPE] = r[:, ROPE:]
    tick(2, 0)


    loop(HEADS, lambda j: load_ka(j).wait())

    for j in range(HEADS):
        rows = slice(j * TOKENS, (j + 1) * TOKENS)
        nope = q32n[pl.ds(j, TOKENS, stride=HEADS), :].astype(jnp.bfloat16)
        part = jnp.dot(nope, ka[j], preferred_element_type=jnp.float32)
        q[rows, 0:LATENT] = (part * SCALE).astype(jnp.bfloat16)
        rope = q32r[pl.ds(j, TOKENS, stride=HEADS), :][:, :ROPE]
        q[rows, LATENT:WIDTH] = (rope * SCALE).astype(jnp.bfloat16)
    tick(2, 1)

    crossed(0)
    attend(True, (0, 1), q, kv, acc, top, tot)
    for way in range(2):
        v_relay(way).wait_recv()
        v_x(2, way).start()
    crossed(2, 3)
    attend(False, (2, 3, 4, 5), q, kv, acc, top, tot)
    crossed(6, 7)
    attend(False, (6, 7, 8, 9), q, kv, acc, top, tot)
    tick(3, 0)
    tick(3, 1)
    up(4, 0).wait_recv()
    down(4, 1).wait_recv()
    across(14, 0).start()
    across(14, 1).start()
    crossed(10, 11)
    attend(False, (10, 11, 12, 13), q, kv, acc, top, tot)

    load_va.wait()

    for i in range(4):
        for way in range(2):
            v_x(i, way).wait_recv()
    crossed(14)

    per = TILE // TOKENS
    lane = lax.broadcasted_iota(jnp.int32, (TOKENS, 128), 1)
    row = lax.broadcasted_iota(jnp.int32, (16, 128), 0)
    first_tile = 1 - lax.div(j_me, 4)

    def order(i):
        return first_tile if i == 0 else 1 - first_tile

    def y_copy(other):
        j, t = lax.rem(other, OWNERS), lax.div(other, OWNERS)
        to = (2 * j + c, z, t)
        return remote(ysend.at[j, t], yrecv.at[chip], y_send.at[other], y_recv.at[chip], to)

    def finish(i, latent, new_top, total):
        for h in range(per):
            j = order(i) * per + h
            rows = slice(h * TOKENS, (h + 1) * TOKENS)
            y = jnp.dot(latent[rows], va[j], preferred_element_type=jnp.float32)
            y = y.astype(jnp.bfloat16)
            stats = jnp.where(lane % 2 == 0, new_top[rows], total[rows])
            stats = stats.T[0:16, :]
            high = stats.astype(jnp.bfloat16)
            left = stats - high.astype(jnp.float32)
            middle = left.astype(jnp.bfloat16)
            low = left - middle.astype(jnp.float32)
            stats = jnp.where(
                row < 2,
                high.astype(jnp.float32),
                jnp.where(row < 4, middle.astype(jnp.float32), low),
            ).astype(jnp.bfloat16)
            for t in range(2):
                ysend[j, t, 0:64, :] = y[t * 64 : (t + 1) * 64]
                ysend[j, t, 64:80, :] = stats

        def send(k):
            j, t = order(i) * per + lax.div(k, 2), lax.rem(k, 2)
            other = t * OWNERS + j

            @pl.when(other != chip)
            def _():
                y_copy(other).start()

        loop(2 * per, send)

    attend(False, (14, 15), q, kv, acc, top, tot, order, finish)
    yrecv[chip] = ysend[j_me, dp]

    def y_arrived(k):
        other, to = plane(k + 1)
        remote(yrecv.at[other], yrecv.at[other], y_send.at[k], y_recv.at[other], to).wait_recv()

    loop(PLANE - 1, y_arrived)

    stats = [yrecv[s, 64:80, :].astype(jnp.float32) for s in range(PLANE)]
    tops = jnp.concatenate([x[0:1] + x[2:3] + x[4:5] for x in stats], axis=0)
    sums = jnp.concatenate([x[1:2] + x[3:4] + x[5:6] for x in stats], axis=0)
    weight = sums * jnp.exp2(tops - jnp.max(tops, axis=0, keepdims=True))
    weight = weight / jnp.sum(weight, axis=0, keepdims=True)
    wts[...] = jnp.concatenate([weight, jnp.zeros((128 - PLANE, 128), jnp.float32)], axis=0).T
    w = wts[pl.ds(pl.multiple_of(dp * 64, 64), 64), :]
    merged = None
    for s in range(PLANE):
        term = yrecv[s, 0:64, :].astype(jnp.float32) * w[:, s : s + 1]
        merged = term if merged is None else merged + term
    ho[quarter] = merged.astype(jnp.bfloat16)

    def h_copy(k):
        core = 1 - c if k % 2 else c
        x_low = 1 - xl if k >= 2 else xl
        return remote(
            ho.at[quarter], ho.at[quarter], h_send.at[k - 1], h_recv.at[k - 1], at(2 * dp + x_low, yy, core)
        )

    for k in (2, 3, 1):
        h_copy(k).start()
    load_wo.wait()
    wo_copy.wait_recv()
    for way in range(2):
        for core in range(2):
            wo_x_arrived(way, core)
    for k in (1, 2, 3):
        h_copy(k).wait_recv()

    heads = jnp.concatenate([ho[k] for k in range(4)], axis=1)
    mine = 8 * xl + 2 * yy + c

    def e_copy(n, k):
        to = lax.rem(mine + k, 16)
        to_z = 2 * quarter + n
        return (to_z == z) & (k == 0), to, remote(
            esend.at[n, to], erecv.at[z, yy], e_send.at[n, to], e_recv.at[z, yy], (to, to_z, dp)
        )

    for n in range(2):
        terms = jnp.dot(
            heads, wo[:, n * COLS : (n + 1) * COLS], preferred_element_type=jnp.float32
        )
        for i in range(16):
            rows = slice(i * 4, i * 4 + 4)
            pieces = [terms[rows, k * 128 : (k + 1) * 128] for k in range(7)]
            pieces.append(jnp.zeros((4, 128), jnp.float32))
            esend[n, i] = jnp.concatenate(pieces, axis=0).astype(jnp.bfloat16)

        def e_start(k):
            here, to, copy = e_copy(n, k)

            @pl.when(jnp.logical_not(here))
            def _():
                copy.start()

            @pl.when(here)
            def _():
                erecv[z, yy] = esend[n, to]

        loop(16, e_start)

    from_x, from_core = lax.div(z, 4), lax.rem(lax.div(z, 2), 2)

    def e_arrived(i):
        s, y_from = lax.div(i, 4), lax.rem(i, 4)
        frm = ((4 * from_x + y_from) * 2 + from_core, s, dp)

        @pl.when(
            jnp.logical_not((s == z) & (y_from == yy) & (from_x == xl) & (from_core == c))
        )
        def _():
            remote(
                esend.at[0, 0], erecv.at[s, y_from], e_send.at[0, 0], e_recv.at[s, y_from], frm
            ).wait_recv()

    loop(4 * Z, e_arrived)
    result = None
    for s in range(Z):
        for y_from in range(4):
            term = erecv[s, y_from].astype(jnp.float32)
            result = term if result is None else result + term
    for k in range(7):
        out_ref[:, k * 128 : (k + 1) * 128] = result[4 * k : 4 * k + 4]

    q_sib.wait_send()
    for step in range(1, 5):
        for h in range(2):
            if step < 4 or h == 0:
                up(step, h).wait_send()
                down(step, 1 - h).wait_send()
    for slot in SIB_ORDER:
        for h in range(2):
            across(slot, h).wait_send()
    wo_copy.wait_send()
    for k in (1, 2, 3):
        h_copy(k).wait_send()

    def sent_plane(k):
        q_copy(k).wait_send()
        y_copy(plane(k + 1)[0]).wait_send()

    loop(PLANE - 1, sent_plane)
    for way in range(2):
        v_y(way).wait_send()
        v_relay(way).wait_send()
        for i in range(4):
            v_x(i, way).wait_send()
        for core in range(2):
            wo_x(way, core).wait_send()
    def e_sent(i):
        for n in range(2):
            here, _, copy = e_copy(n, i)

            @pl.when(jnp.logical_not(here))
            def _():
                copy.wait_send()

    loop(16, e_sent)


def body(query_nope, query_rope, latent_cache, key_absorb, value_absorb, output_proj):
    vmem = pl.BlockSpec(memory_space=pltpu.VMEM)
    hbm = pl.BlockSpec(memory_space=pl.ANY)
    bf16, f32 = jnp.bfloat16, jnp.float32
    dma = pltpu.SemaphoreType.DMA
    return pl.pallas_call(
        kernel,
        out_shape=jax.ShapeDtypeStruct((4, COLS), f32),
        in_specs=[hbm] * 6,
        out_specs=vmem,
        scratch_shapes=[
            pltpu.VMEM((16, 2, HALFB + PACK, LATENT), bf16),
            pltpu.VMEM((ROWS, WIDTH), bf16),
            pltpu.VMEM((ROWS, LATENT), f32),
            pltpu.VMEM((ROWS, 128), f32),
            pltpu.VMEM((ROWS, 128), f32),
            pltpu.VMEM((HEADS, NOPE, LATENT), bf16),
            pltpu.VMEM((HEADS, LATENT, VDIM), bf16),
            pltpu.VMEM((4 * VDIM, QUARTER), bf16),
            pltpu.VMEM((4, 16, NOPE), bf16),
            pltpu.VMEM((4, 16, ROPE), bf16),
            pltpu.VMEM((64, NOPE), f32),
            pltpu.VMEM((64, 128), f32),
            pltpu.VMEM((2, MSG, 128), bf16),
            pltpu.VMEM((PLANE, 2, MSG, 128), bf16),
            pltpu.VMEM((ROWS, NOPE), f32),
            pltpu.VMEM((ROWS, 128), f32),
            pltpu.VMEM((BLOCK, WIDTH), bf16),
            pltpu.VMEM((HEADS, 2, 80, VDIM), bf16),
            pltpu.VMEM((PLANE, 80, VDIM), bf16),
            pltpu.VMEM((128, 128), f32),
            pltpu.VMEM((4, 64, VDIM), bf16),
            pltpu.VMEM((2, 16, 32, 128), bf16),
            pltpu.VMEM((Z, 4, 32, 128), bf16),
            dma((13,)),
            dma, dma, dma((PLANE - 1,)), dma((PLANE,)),
            dma((4, 2)), dma((4, 2)), dma((4, 2)), dma((4, 2)), dma((8, 2)), dma((8, 2)),
            dma((2,)), dma((2,)), dma((2,)), dma((2,)), dma((4, 2)), dma((4, 2)),
            dma, dma, dma((2, 2)), dma((2, 2)),
            dma((PLANE,)), dma((PLANE,)),
            dma((3,)), dma((3,)), dma((2, 16)), dma((Z, 4)),
        ],
        compiler_params=pltpu.CompilerParams(
            collective_id=0, has_side_effects=True, vmem_limit_bytes=127 * 512 * 1024
        ),
        cost_estimate=pl.CostEstimate(
            flops=7_000_000_000, bytes_accessed=10_000_000, transcendentals=3_145_728
        ),
        name="latent_attention",
    )(query_nope, query_rope, latent_cache, key_absorb, value_absorb, output_proj)


def solution(mesh):
    in_specs = (
        P(("dp", "prefix"), "head", None),
        P(("dp", "prefix"), "head", None),
        P(("prefix", "head", "dp"), None),
        P("head", None, None),
        P(("head", "prefix"), None, None),
        P(("head", "prefix"), None),
    )
    out_specs = P(("dp", "prefix"), "head")
    return jax.shard_map(body, mesh=mesh, in_specs=in_specs, out_specs=out_specs, check_vma=False)
```

```python
import math

import jax
import jax.numpy as jnp
from jax import lax
from jax.experimental import pallas as pl
from jax.experimental.pallas import tpu as pltpu
from jax.sharding import PartitionSpec as P

MESH = pl.DeviceIdType.MESH

D = 7168
NOPE, ROPE, VDIM, LATENT = 128, 64, 128, 512
WIDTH = LATENT + ROPE
TOKENS = 128
Z = 8
PLANE = 16
OWNERS = 8
HEADS = 8
ROWS = HEADS * TOKENS
BLOCK = 192
MSG = 48
QUARTER = D // 4
COLS = D // Z
SCALE = (NOPE + ROPE) ** -0.5 * math.log2(math.e)

HALFB = BLOCK // 2
PACK = 16
UP = (0, 2, 6, 10, 14)
DOWN = (0, 3, 7, 11, 14)
SIB_OF = {0: 1, 2: 4, 3: 5, 6: 8, 7: 9, 10: 12, 11: 13, 14: 15}
SIB_ORDER = (0, 2, 3, 6, 7, 10, 11, 14)
TILE = 512


def chunk_keys(kv, blocks):
    latent, rope = [], []
    for b in blocks:
        for h in range(2):
            latent.append(kv[b, h, 0:HALFB, :])
            packed = kv[b, h, HALFB : HALFB + PACK, 0 : 6 * ROPE]
            for g in range(6):
                rope.append(packed[:, g * ROPE : (g + 1) * ROPE])
    latent = jnp.concatenate(latent, axis=0)
    return jnp.concatenate([latent, jnp.concatenate(rope, axis=0)], axis=1), latent


def attend(first, blocks, q, kv, acc, top, tot, order=None, finish=None):
    keys, values = chunk_keys(kv, blocks)
    n = ROWS // TILE

    def at(i):
        if order is None:
            return pl.ds(i * TILE, TILE)
        return pl.ds(pl.multiple_of(order(i) * TILE, TILE), TILE)

    def score(i):
        return lax.dot_general(
            q[at(i), :], keys, (((1,), (1,)), ((), ())), preferred_element_type=jnp.float32
        )

    s = score(0)
    for i in range(n):
        later = score(i + 1) if i + 1 < n else None
        rows = at(i)
        high = jnp.max(s, axis=1, keepdims=True)
        if first:
            new_top = jnp.broadcast_to(high, (TILE, 128))
        else:
            old_top = top[rows, :]
            new_top = jnp.maximum(old_top, high)
            alpha = jnp.exp2(old_top - new_top)
        part = None
        pieces = []
        for k in range(s.shape[1] // 128):
            e = jnp.exp2(s[:, k * 128 : (k + 1) * 128] - new_top)
            part = e if part is None else part + e
            pieces.append(e.astype(jnp.bfloat16))
        p = jnp.concatenate(pieces, axis=1)
        out = jnp.dot(p, values, preferred_element_type=jnp.float32)
        if not first:
            part = tot[rows, :] * alpha + part
        if finish is not None:
            total = jnp.sum(part, axis=1, keepdims=True)
            scale = 1.0 / total
            latent = []
            for k in range(LATENT // 128):
                cols = slice(k * 128, (k + 1) * 128)
                latent.append(((acc[rows, cols] * alpha + out[:, cols]) * scale).astype(jnp.bfloat16))
            finish(i, jnp.concatenate(latent, axis=1), new_top, total)
        else:
            top[rows, :] = new_top
            tot[rows, :] = part
            for k in range(LATENT // 128):
                cols = slice(k * 128, (k + 1) * 128)
                if first:
                    acc[rows, cols] = out[:, cols]
                else:
                    acc[rows, cols] = acc[rows, cols] * alpha + out[:, cols]
        s = later


def kernel(
    qn_ref, qr_ref, kv_ref, ka_ref, va_ref, wo_ref, out_ref,
    kv, q, acc, top, tot, ka, va, wo,
    qn, qr, tmpn, tmpr, qsend, qall, q32n, q32r,
    kvraw, ysend, yrecv, wts, ho, dsend, drecv, esend, erecv,
    local, qs_send, qs_recv, q_send, q_recv,
    up_send, up_recv, dn_send, dn_recv, sb_send, sb_recv,
    vy_send, vy_recv, vf_send, vf_recv, vx_send, vx_recv, o_send, o_recv, ox_send, ox_recv,
    y_send, y_recv, h_send, h_recv, d_send, d_recv, e_send, e_recv,
):
    prefix, z, dp = lax.axis_index("prefix"), lax.axis_index("head"), lax.axis_index("dp")
    c = lax.rem(prefix, 2)
    j_me = lax.div(prefix, 2)
    chip = dp * OWNERS + j_me
    sib = (prefix + 1 - 2 * c, z, dp)
    above = (prefix, lax.rem(z + 1, Z), dp)
    below = (prefix, lax.rem(z + Z - 1, Z), dp)

    def plane(k):
        other = lax.rem(chip + k, PLANE)
        return other, (2 * lax.rem(other, OWNERS) + c, z, lax.div(other, OWNERS))

    xl, yy = lax.div(j_me, 4), lax.rem(j_me, 4)
    x = 2 * dp + xl
    quarter = 2 * xl + c

    def at(x_to, y_to, core):
        x_to, y_to = lax.rem(x_to, 4), lax.rem(y_to, 4)
        return ((lax.rem(x_to, 2) * 4 + y_to) * 2 + core, z, lax.div(x_to, 2))

    def head_of(x_low, y_of):
        return x_low * 4 + lax.rem(y_of, 4)

    def columns(quarter_of, n):
        return pl.ds(pl.multiple_of((quarter_of + 4 * n) * COLS, 128), COLS)

    def owned(n):
        return pl.ds(n * COLS, COLS)

    def remote(src, dst, ssem, rsem, to):
        return pltpu.make_async_remote_copy(
            src_ref=src, dst_ref=dst, send_sem=ssem, recv_sem=rsem, device_id=to, device_id_type=MESH
        )

    def loop(n, body):
        def step(k, carry):
            body(k)
            return carry

        lax.fori_loop(0, n, step, 0)

    def load_ka(j):
        return pltpu.make_async_copy(ka_ref.at[2 * j + c], ka.at[j], local.at[j])

    load_kv = pltpu.make_async_copy(kv_ref, kvraw, local.at[8])
    load_kv.start()
    load_qn = pltpu.make_async_copy(qn_ref, qn, local.at[11])
    load_qn.start()
    load_qr = pltpu.make_async_copy(qr_ref, qr, local.at[12])
    load_qr.start()

    barrier = pltpu.get_barrier_semaphore()

    def greet(to):
        pl.semaphore_signal(barrier, inc=1, device_id=to, device_id_type=MESH)

    loop(PLANE - 1, lambda k: greet(plane(k + 1)[1]))
    for to in (above, below, sib):
        greet(to)

    loop(HEADS, lambda j: load_ka(j).start())
    load_va = pltpu.make_async_copy(va_ref.at[0], va.at[j_me], local.at[9])
    load_va.start()
    own_rows = pl.ds(pl.multiple_of(quarter * VDIM, VDIM), VDIM)
    load_wo = [
        pltpu.make_async_copy(
            wo_ref.at[:, columns(quarter, n)], wo.at[own_rows, owned(n)], local.at[13 + n]
        )
        for n in range(2)
    ]
    for copy in load_wo:
        copy.start()

    load_kv.wait()
    for h in range(2):
        rows = slice(h * HALFB, (h + 1) * HALFB)
        kv[0, h, 0:HALFB, :] = kvraw[rows, 0:LATENT]
        rope = kvraw[rows, LATENT:WIDTH].astype(jnp.float32)
        packed = [rope[g * PACK : (g + 1) * PACK] for g in range(6)]
        packed.append(jnp.zeros((PACK, LATENT - 6 * ROPE), jnp.float32))
        kv[0, h, HALFB : HALFB + PACK, :] = jnp.concatenate(packed, axis=1).astype(jnp.bfloat16)

    load_qn.wait()
    load_qr.wait()
    tmpn[...] = qn[...].astype(jnp.float32).reshape(64, NOPE)
    tmpr[:, :ROPE] = qr[...].astype(jnp.float32).reshape(64, ROPE)
    for parity in range(2):
        qsend[parity, 0:32, :] = tmpn[pl.ds(parity, 32, stride=2), :].astype(jnp.bfloat16)
        rope = tmpr[pl.ds(parity, 32, stride=2), :][:, :ROPE]
        qsend[parity, 32:48, :] = jnp.concatenate([rope[:16], rope[16:]], axis=1).astype(
            jnp.bfloat16
        )
    pl.semaphore_wait(barrier, 3 + (PLANE - 1))

    q_sib = remote(qsend.at[1 - c], qall.at[chip, c], qs_send, qs_recv, sib)
    q_sib.start()

    def up(step, h):
        return remote(
            kv.at[UP[step - 1], h], kv.at[UP[step], h],
            up_send.at[step - 1, h], up_recv.at[step - 1, h], above,
        )

    def down(step, h):
        return remote(
            kv.at[DOWN[step - 1], h], kv.at[DOWN[step], h],
            dn_send.at[step - 1, h], dn_recv.at[step - 1, h], below,
        )

    def across(slot, h):
        i = SIB_ORDER.index(slot)
        return remote(kv.at[slot, h], kv.at[SIB_OF[slot], h], sb_send.at[i, h], sb_recv.at[i, h], sib)

    def tick(step, h):
        up(step, h).wait_recv()
        if step < 3 or (step == 3 and h == 0):
            up(step + 1, h).start()
        down(step, 1 - h).wait_recv()
        if step < 3 or (step == 3 and h == 0):
            down(step + 1, 1 - h).start()
        across(UP[step], h).start()
        across(DOWN[step], 1 - h).start()

    def crossed(*slots):
        for slot in slots:
            for h in range(2):
                across(slot, h).wait_recv()

    for h in range(2):
        up(1, h).start()
        down(1, 1 - h).start()
    across(0, 0).start()
    across(0, 1).start()
    def v_y(way):
        return remote(
            va_ref.at[0], va.at[j_me], vy_send.at[way], vy_recv.at[way], at(x, yy + 1 + 2 * way, c)
        )

    def v_relay(way):
        half = va.at[head_of(xl, yy + 3 - 2 * way), pl.ds(way * 256, 256), :]
        return remote(half, half, vf_send.at[way], vf_recv.at[way], at(x, yy + 1 + 2 * way, c))

    def v_x(i, way):
        half = va.at[head_of(xl, yy + i), pl.ds(way * 256, 256), :]
        src = va_ref.at[0, pl.ds(way * 256, 256), :] if i == 0 else half
        return remote(src, half, vx_send.at[i, way], vx_recv.at[i, way], at(x + 1 + 2 * way, yy, c))

    for way in range(2):
        v_y(way).start()
        v_x(0, way).start()

    qall[chip, c] = qsend[c]
    q_sib.wait_recv()

    def q_copy(k):
        _, to = plane(k + 1)
        return remote(qall.at[chip], qall.at[chip], q_send.at[k], q_recv.at[chip], to)

    loop(PLANE - 1, lambda k: q_copy(k).start())

    wo_copies = [
        remote(
            wo_ref.at[:, columns(2 * xl + 1 - c, n)], wo.at[own_rows, owned(n)],
            o_send.at[n], o_recv.at[n], sib,
        )
        for n in range(2)
    ]
    for copy in wo_copies:
        copy.start()

    def wo_x(way, core, n):
        return remote(
            wo_ref.at[pl.ds(way * 64, 64), columns(2 * (1 - xl) + core, n)],
            wo.at[pl.ds(pl.multiple_of(quarter * VDIM + way * 64, 64), 64), owned(n)],
            ox_send.at[way, core, n], ox_recv.at[way, c, n], at(x + 1 + 2 * way, yy, core),
        )

    def wo_x_arrived(way, core, n):
        rows = pl.ds(pl.multiple_of((2 * (1 - xl) + core) * VDIM + way * 64, 64), 64)
        remote(
            wo.at[rows, owned(n)], wo.at[rows, owned(n)],
            ox_send.at[way, core, n], ox_recv.at[way, core, n], at(x + 3 - 2 * way, yy, core),
        ).wait_recv()

    tick(1, 0)
    tick(1, 1)

    def q_arrived(k):
        other, to = plane(k + 1)
        remote(qall.at[other], qall.at[other], q_send.at[k], q_recv.at[other], to).wait_recv()

    loop(PLANE - 1, q_arrived)
    for way in range(2):
        for core in range(2):
            for n in range(2):
                wo_x(way, core, n).start()

    for g in range(2 * PLANE):
        m = qall[g // 2, g % 2]
        q32n[g * 32 : (g + 1) * 32, :] = m[0:32].astype(jnp.float32)
        r = m[32:48].astype(jnp.float32)
        q32r[g * 32 : g * 32 + 16, 0:ROPE] = r[:, :ROPE]
        q32r[g * 32 + 16 : g * 32 + 32, 0:ROPE] = r[:, ROPE:]


    loop(HEADS, lambda j: load_ka(j).wait())

    for j in range(HEADS):
        rows = slice(j * TOKENS, (j + 1) * TOKENS)
        nope = q32n[pl.ds(j, TOKENS, stride=HEADS), :].astype(jnp.bfloat16)
        part = jnp.dot(nope, ka[j], preferred_element_type=jnp.float32)
        q[rows, 0:LATENT] = (part * SCALE).astype(jnp.bfloat16)
        rope = q32r[pl.ds(j, TOKENS, stride=HEADS), :][:, :ROPE]
        q[rows, LATENT:WIDTH] = (rope * SCALE).astype(jnp.bfloat16)
    for way in range(2):
        v_y(way).wait_recv()
        v_relay(way).start()
    for way in range(2):
        v_x(3, way).start()
        v_x(1, way).start()
    tick(2, 0)
    tick(2, 1)

    crossed(0)
    attend(True, (0, 1), q, kv, acc, top, tot)
    for way in range(2):
        v_relay(way).wait_recv()
        v_x(2, way).start()
    crossed(2, 3)
    attend(False, (2, 3, 4, 5), q, kv, acc, top, tot)
    tick(3, 0)
    tick(3, 1)
    crossed(6, 7)
    attend(False, (6, 7, 8, 9), q, kv, acc, top, tot)
    crossed(10, 11)
    attend(False, (10, 11, 12, 13), q, kv, acc, top, tot)
    up(4, 0).wait_recv()
    across(14, 0).start()
    down(4, 1).wait_recv()
    across(14, 1).start()

    load_va.wait()

    for i in range(4):
        for way in range(2):
            v_x(i, way).wait_recv()
    crossed(14)

    per = TILE // TOKENS
    lane = lax.broadcasted_iota(jnp.int32, (TOKENS, 128), 1)
    row = lax.broadcasted_iota(jnp.int32, (16, 128), 0)
    first_tile = 1 - lax.div(j_me, 4)

    def order(i):
        return first_tile if i == 0 else 1 - first_tile

    def y_copy(other):
        j, t = lax.rem(other, OWNERS), lax.div(other, OWNERS)
        to = (2 * j + c, z, t)
        return remote(ysend.at[j, t], yrecv.at[chip], y_send.at[other], y_recv.at[chip], to)

    def finish(i, latent, new_top, total):
        for h in range(per):
            j = order(i) * per + h
            rows = slice(h * TOKENS, (h + 1) * TOKENS)
            y = jnp.dot(latent[rows], va[j], preferred_element_type=jnp.float32)
            y = y.astype(jnp.bfloat16)
            stats = jnp.where(lane % 2 == 0, new_top[rows], total[rows])
            stats = stats.T[0:16, :]
            high = stats.astype(jnp.bfloat16)
            left = stats - high.astype(jnp.float32)
            middle = left.astype(jnp.bfloat16)
            low = left - middle.astype(jnp.float32)
            stats = jnp.where(
                row < 2,
                high.astype(jnp.float32),
                jnp.where(row < 4, middle.astype(jnp.float32), low),
            ).astype(jnp.bfloat16)
            for t in range(2):
                ysend[j, t, 0:64, :] = y[t * 64 : (t + 1) * 64]
                ysend[j, t, 64:80, :] = stats

        def send(k):
            j, t = order(i) * per + lax.div(k, 2), lax.rem(k, 2)
            other = t * OWNERS + j

            @pl.when(other != chip)
            def _():
                y_copy(other).start()

        loop(2 * per, send)

    attend(False, (14, 15), q, kv, acc, top, tot, order, finish)
    yrecv[chip] = ysend[j_me, dp]

    def y_arrived(k):
        other, to = plane(k + 1)
        remote(yrecv.at[other], yrecv.at[other], y_send.at[k], y_recv.at[other], to).wait_recv()

    loop(PLANE - 1, y_arrived)

    stats = [yrecv[s, 64:80, :].astype(jnp.float32) for s in range(PLANE)]
    tops = jnp.concatenate([x[0:1] + x[2:3] + x[4:5] for x in stats], axis=0)
    sums = jnp.concatenate([x[1:2] + x[3:4] + x[5:6] for x in stats], axis=0)
    weight = sums * jnp.exp2(tops - jnp.max(tops, axis=0, keepdims=True))
    weight = weight / jnp.sum(weight, axis=0, keepdims=True)
    wts[...] = jnp.concatenate([weight, jnp.zeros((128 - PLANE, 128), jnp.float32)], axis=0).T
    w = wts[pl.ds(pl.multiple_of(dp * 64, 64), 64), :]
    merged = None
    for s in range(PLANE):
        term = yrecv[s, 0:64, :].astype(jnp.float32) * w[:, s : s + 1]
        merged = term if merged is None else merged + term
    ho[quarter] = merged.astype(jnp.bfloat16)

    def h_copy(k):
        core = 1 - c if k % 2 else c
        x_low = 1 - xl if k >= 2 else xl
        return remote(
            ho.at[quarter], ho.at[quarter], h_send.at[k - 1], h_recv.at[k - 1], at(2 * dp + x_low, yy, core)
        )

    for k in (2, 3, 1):
        h_copy(k).start()
    for n in range(2):
        load_wo[n].wait()
        wo_copies[n].wait_recv()
        for way in range(2):
            for core in range(2):
                wo_x_arrived(way, core, n)
    for k in (1, 2, 3):
        h_copy(k).wait_recv()

    heads = jnp.concatenate([ho[k] for k in range(4)], axis=1)

    def d_copy(n, k):
        other = lax.rem(yy + k, 4)
        return remote(
            dsend.at[n, other], drecv.at[n, yy], d_send.at[n, k - 1], d_recv.at[n, yy], at(x, other, c)
        )

    def d_arrived(n, k):
        other = lax.rem(yy + k, 4)
        remote(
            dsend.at[n, other], drecv.at[n, other], d_send.at[n, k - 1], d_recv.at[n, other],
            at(x, other, c),
        ).wait_recv()

    for n in range(2):
        terms = jnp.dot(
            heads, wo[:, n * COLS : (n + 1) * COLS], preferred_element_type=jnp.float32
        )
        for i in range(4):
            dsend[n, i] = jnp.concatenate(
                [terms[i * 8 : i * 8 + 8], terms[32 + i * 8 : 40 + i * 8]], axis=0
            ).astype(jnp.bfloat16)
        for k in (2, 1, 3):
            d_copy(n, k).start()

    def e_copy(n, x_low, core):
        to_z = quarter + 4 * n
        return (to_z == z) & (x_low == xl) & (core == c), remote(
            esend.at[n, x_low, core], erecv.at[z], e_send.at[n, x_low, core], e_recv.at[z],
            ((4 * x_low + yy) * 2 + core, to_z, dp),
        )

    for n in range(2):
        drecv[n, yy] = dsend[n, yy]
        for k in (1, 3, 2):
            d_arrived(n, k)
        summed = drecv[n, 0].astype(jnp.float32)
        for i in range(1, 4):
            summed = summed + drecv[n, i].astype(jnp.float32)
        for x_low in range(2):
            for core in range(2):
                start = x_low * 8 + core * 4
                pieces = [summed[start : start + 4, k * 128 : (k + 1) * 128] for k in range(7)]
                pieces.append(jnp.zeros((4, 128), jnp.float32))
                esend[n, x_low, core] = jnp.concatenate(pieces, axis=0).astype(jnp.bfloat16)
                here, copy = e_copy(n, x_low, core)

                @pl.when(jnp.logical_not(here))
                def _():
                    copy.start()

                @pl.when(here)
                def _():
                    erecv[z] = esend[n, x_low, core]

    from_x, from_core = lax.rem(lax.div(z, 2), 2), lax.rem(z, 2)

    def e_arrived(s):
        frm = ((4 * from_x + yy) * 2 + from_core, s, dp)

        @pl.when(jnp.logical_not((s == z) & (from_x == xl) & (from_core == c)))
        def _():
            remote(
                esend.at[0, 0, 0], erecv.at[s], e_send.at[0, 0, 0], e_recv.at[s], frm
            ).wait_recv()

    loop(Z, e_arrived)
    result = erecv[0].astype(jnp.float32)
    for s in range(1, Z):
        result = result + erecv[s].astype(jnp.float32)
    for k in range(7):
        out_ref[:, k * 128 : (k + 1) * 128] = result[4 * k : 4 * k + 4]

    q_sib.wait_send()
    for step in range(1, 5):
        for h in range(2):
            if step < 4 or h == 0:
                up(step, h).wait_send()
                down(step, 1 - h).wait_send()
    for slot in SIB_ORDER:
        for h in range(2):
            across(slot, h).wait_send()
    for copy in wo_copies:
        copy.wait_send()
    for k in (1, 2, 3):
        h_copy(k).wait_send()

    def sent_plane(k):
        q_copy(k).wait_send()
        y_copy(plane(k + 1)[0]).wait_send()

    loop(PLANE - 1, sent_plane)
    for way in range(2):
        v_y(way).wait_send()
        v_relay(way).wait_send()
        for i in range(4):
            v_x(i, way).wait_send()
        for core in range(2):
            for n in range(2):
                wo_x(way, core, n).wait_send()
    for n in range(2):
        for k in (1, 2, 3):
            d_copy(n, k).wait_send()
        for x_low in range(2):
            for core in range(2):
                here, copy = e_copy(n, x_low, core)

                @pl.when(jnp.logical_not(here))
                def _():
                    copy.wait_send()


def body(query_nope, query_rope, latent_cache, key_absorb, value_absorb, output_proj):
    vmem = pl.BlockSpec(memory_space=pltpu.VMEM)
    hbm = pl.BlockSpec(memory_space=pl.ANY)
    bf16, f32 = jnp.bfloat16, jnp.float32
    dma = pltpu.SemaphoreType.DMA
    return pl.pallas_call(
        kernel,
        out_shape=jax.ShapeDtypeStruct((4, COLS), f32),
        in_specs=[hbm] * 6,
        out_specs=vmem,
        scratch_shapes=[
            pltpu.VMEM((16, 2, HALFB + PACK, LATENT), bf16),
            pltpu.VMEM((ROWS, WIDTH), bf16),
            pltpu.VMEM((ROWS, LATENT), f32),
            pltpu.VMEM((ROWS, 128), f32),
            pltpu.VMEM((ROWS, 128), f32),
            pltpu.VMEM((HEADS, NOPE, LATENT), bf16),
            pltpu.VMEM((HEADS, LATENT, VDIM), bf16),
            pltpu.VMEM((4 * VDIM, QUARTER), bf16),
            pltpu.VMEM((4, 16, NOPE), bf16),
            pltpu.VMEM((4, 16, ROPE), bf16),
            pltpu.VMEM((64, NOPE), f32),
            pltpu.VMEM((64, 128), f32),
            pltpu.VMEM((2, MSG, 128), bf16),
            pltpu.VMEM((PLANE, 2, MSG, 128), bf16),
            pltpu.VMEM((ROWS, NOPE), f32),
            pltpu.VMEM((ROWS, 128), f32),
            pltpu.VMEM((BLOCK, WIDTH), bf16),
            pltpu.VMEM((HEADS, 2, 80, VDIM), bf16),
            pltpu.VMEM((PLANE, 80, VDIM), bf16),
            pltpu.VMEM((128, 128), f32),
            pltpu.VMEM((4, 64, VDIM), bf16),
            pltpu.VMEM((2, 4, 16, COLS), bf16),
            pltpu.VMEM((2, 4, 16, COLS), bf16),
            pltpu.VMEM((2, 2, 2, 32, 128), bf16),
            pltpu.VMEM((Z, 32, 128), bf16),
            dma((15,)),
            dma, dma, dma((PLANE - 1,)), dma((PLANE,)),
            dma((4, 2)), dma((4, 2)), dma((4, 2)), dma((4, 2)), dma((8, 2)), dma((8, 2)),
            dma((2,)), dma((2,)), dma((2,)), dma((2,)), dma((4, 2)), dma((4, 2)),
            dma((2,)), dma((2,)), dma((2, 2, 2)), dma((2, 2, 2)),
            dma((PLANE,)), dma((PLANE,)),
            dma((3,)), dma((3,)), dma((2, 3)), dma((2, 4)), dma((2, 2, 2)), dma((Z,)),
        ],
        compiler_params=pltpu.CompilerParams(
            collective_id=0, has_side_effects=True, vmem_limit_bytes=127 * 512 * 1024
        ),
        cost_estimate=pl.CostEstimate(
            flops=7_000_000_000, bytes_accessed=10_000_000, transcendentals=3_145_728
        ),
        name="latent_attention",
    )(query_nope, query_rope, latent_cache, key_absorb, value_absorb, output_proj)


def solution(mesh):
    in_specs = (
        P(("dp", "prefix"), "head", None),
        P(("dp", "prefix"), "head", None),
        P(("prefix", "head", "dp"), None),
        P("head", None, None),
        P(("head", "prefix"), None, None),
        P(("head", "prefix"), None),
    )
    out_specs = P(("dp", "prefix"), "head")
    return jax.shard_map(body, mesh=mesh, in_specs=in_specs, out_specs=out_specs, check_vma=False)
```

```python
import math

import jax
import jax.numpy as jnp
from jax import lax
from jax.experimental import pallas as pl
from jax.experimental.pallas import tpu as pltpu
from jax.sharding import PartitionSpec as P

MESH = pl.DeviceIdType.MESH

D = 7168
NOPE, ROPE, VDIM, LATENT = 128, 64, 128, 512
WIDTH = LATENT + ROPE
TOKENS = 128
Z = 8
PLANE = 16
OWNERS = 8
HEADS = 8
ROWS = HEADS * TOKENS
BLOCK = 192
MSG = 48
QUARTER = D // 4
COLS = D // Z
SCALE = (NOPE + ROPE) ** -0.5 * math.log2(math.e)

HALFB = BLOCK // 2
PACK = 16
UP = (0, 2, 6, 10, 14)
DOWN = (0, 3, 7, 11, 14)
SIB_OF = {0: 1, 2: 4, 3: 5, 6: 8, 7: 9, 10: 12, 11: 13, 14: 15}
SIB_ORDER = (0, 2, 3, 6, 7, 10, 11, 14)
TILE = 512


def chunk_keys(kv, blocks):
    latent, rope = [], []
    for b in blocks:
        for h in range(2):
            latent.append(kv[b, h, 0:HALFB, :])
            packed = kv[b, h, HALFB : HALFB + PACK, 0 : 6 * ROPE]
            for g in range(6):
                rope.append(packed[:, g * ROPE : (g + 1) * ROPE])
    latent = jnp.concatenate(latent, axis=0)
    return jnp.concatenate([latent, jnp.concatenate(rope, axis=0)], axis=1), latent


def attend(first, blocks, q, kv, acc, top, tot, order=None, finish=None):
    keys, values = chunk_keys(kv, blocks)
    n = ROWS // TILE

    def at(i):
        if order is None:
            return pl.ds(i * TILE, TILE)
        return pl.ds(pl.multiple_of(order(i) * TILE, TILE), TILE)

    def score(i):
        return lax.dot_general(
            q[at(i), :], keys, (((1,), (1,)), ((), ())), preferred_element_type=jnp.float32
        )

    s = score(0)
    for i in range(n):
        later = score(i + 1) if i + 1 < n else None
        rows = at(i)
        high = jnp.max(s, axis=1, keepdims=True)
        if first:
            new_top = jnp.broadcast_to(high, (TILE, 128))
        else:
            old_top = top[rows, :]
            new_top = jnp.maximum(old_top, high)
            alpha = jnp.exp2(old_top - new_top)
        part = None
        pieces = []
        for k in range(0, s.shape[1], 128):
            width = min(128, s.shape[1] - k)
            e = jnp.exp2(s[:, k : k + width] - new_top[:, :width])
            pieces.append(e.astype(jnp.bfloat16))
            if width < 128:
                e = jnp.concatenate([e, jnp.zeros((TILE, 128 - width), jnp.float32)], axis=1)
            part = e if part is None else part + e
        p = jnp.concatenate(pieces, axis=1)
        out = jnp.dot(p, values, preferred_element_type=jnp.float32)
        if not first:
            part = tot[rows, :] * alpha + part
        if finish is not None:
            total = jnp.sum(part, axis=1, keepdims=True)
            scale = 1.0 / total
            latent = []
            for k in range(LATENT // 128):
                cols = slice(k * 128, (k + 1) * 128)
                latent.append(((acc[rows, cols] * alpha + out[:, cols]) * scale).astype(jnp.bfloat16))
            finish(i, jnp.concatenate(latent, axis=1), new_top, total)
        else:
            top[rows, :] = new_top
            tot[rows, :] = part
            for k in range(LATENT // 128):
                cols = slice(k * 128, (k + 1) * 128)
                if first:
                    acc[rows, cols] = out[:, cols]
                else:
                    acc[rows, cols] = acc[rows, cols] * alpha + out[:, cols]
        s = later


def kernel(
    qn_ref, qr_ref, kv_ref, ka_ref, va_ref, wo_ref, out_ref,
    kv, q, acc, top, tot, ka, va, wo,
    qn, qr, tmpn, tmpr, qsend, qall, q32n, q32r,
    kvraw, ysend, yrecv, wts, ho, dsend, drecv, esend, erecv,
    local, qs_send, qs_recv, q_send, q_recv,
    up_send, up_recv, dn_send, dn_recv, sb_send, sb_recv,
    vy_send, vy_recv, vf_send, vf_recv, vx_send, vx_recv, o_send, o_recv, ox_send, ox_recv,
    y_send, y_recv, h_send, h_recv, d_send, d_recv, e_send, e_recv,
):
    prefix, z, dp = lax.axis_index("prefix"), lax.axis_index("head"), lax.axis_index("dp")
    c = lax.rem(prefix, 2)
    j_me = lax.div(prefix, 2)
    chip = dp * OWNERS + j_me
    sib = (prefix + 1 - 2 * c, z, dp)
    above = (prefix, lax.rem(z + 1, Z), dp)
    below = (prefix, lax.rem(z + Z - 1, Z), dp)

    def plane(k):
        other = lax.rem(chip + k, PLANE)
        return other, (2 * lax.rem(other, OWNERS) + c, z, lax.div(other, OWNERS))

    xl, yy = lax.div(j_me, 4), lax.rem(j_me, 4)
    x = 2 * dp + xl
    quarter = 2 * xl + c

    def at(x_to, y_to, core):
        x_to, y_to = lax.rem(x_to, 4), lax.rem(y_to, 4)
        return ((lax.rem(x_to, 2) * 4 + y_to) * 2 + core, z, lax.div(x_to, 2))

    def head_of(x_low, y_of):
        return x_low * 4 + lax.rem(y_of, 4)

    def columns(quarter_of, n):
        return pl.ds(pl.multiple_of((quarter_of + 4 * n) * COLS, 128), COLS)

    def owned(n):
        return pl.ds(n * COLS, COLS)

    def remote(src, dst, ssem, rsem, to):
        return pltpu.make_async_remote_copy(
            src_ref=src, dst_ref=dst, send_sem=ssem, recv_sem=rsem, device_id=to, device_id_type=MESH
        )

    def loop(n, body):
        def step(k, carry):
            body(k)
            return carry

        lax.fori_loop(0, n, step, 0)

    def load_ka(j):
        return pltpu.make_async_copy(ka_ref.at[2 * j + c], ka.at[j], local.at[j])

    load_kv = pltpu.make_async_copy(kv_ref, kvraw, local.at[8])
    load_kv.start()
    load_qn = pltpu.make_async_copy(qn_ref, qn, local.at[11])
    load_qn.start()
    load_qr = pltpu.make_async_copy(qr_ref, qr, local.at[12])
    load_qr.start()

    barrier = pltpu.get_barrier_semaphore()

    def greet(to):
        pl.semaphore_signal(barrier, inc=1, device_id=to, device_id_type=MESH)

    for to in (above, below, sib):
        greet(to)
    loop(PLANE - 1, lambda k: greet(plane(k + 1)[1]))

    load_kv.wait()
    for h in range(2):
        rows = slice(h * HALFB, (h + 1) * HALFB)
        kv[0, h, 0:HALFB, :] = kvraw[rows, 0:LATENT]
        rope = kvraw[rows, LATENT:WIDTH].astype(jnp.float32)
        packed = [rope[g * PACK : (g + 1) * PACK] for g in range(6)]
        packed.append(jnp.zeros((PACK, LATENT - 6 * ROPE), jnp.float32))
        kv[0, h, HALFB : HALFB + PACK, :] = jnp.concatenate(packed, axis=1).astype(jnp.bfloat16)

    pl.semaphore_wait(barrier, 3 + (PLANE - 1))

    def up(step, h):
        return remote(
            kv.at[UP[step - 1], h], kv.at[UP[step], h],
            up_send.at[step - 1, h], up_recv.at[step - 1, h], above,
        )

    def down(step, h):
        return remote(
            kv.at[DOWN[step - 1], h], kv.at[DOWN[step], h],
            dn_send.at[step - 1, h], dn_recv.at[step - 1, h], below,
        )

    def across(slot, h):
        i = SIB_ORDER.index(slot)
        return remote(kv.at[slot, h], kv.at[SIB_OF[slot], h], sb_send.at[i, h], sb_recv.at[i, h], sib)

    def tick(step, h):
        up(step, h).wait_recv()
        if step < 3 or (step == 3 and h == 0):
            up(step + 1, h).start()
        down(step, 1 - h).wait_recv()
        if step < 3 or (step == 3 and h == 0):
            down(step + 1, 1 - h).start()
        across(UP[step], h).start()
        across(DOWN[step], 1 - h).start()

    def crossed(*slots):
        for slot in slots:
            for h in range(2):
                across(slot, h).wait_recv()

    for h in range(2):
        up(1, h).start()
        down(1, 1 - h).start()
    across(0, 0).start()
    across(0, 1).start()

    load_qn.wait()
    load_qr.wait()
    tmpn[...] = qn[...].astype(jnp.float32).reshape(64, NOPE)
    tmpr[:, :ROPE] = qr[...].astype(jnp.float32).reshape(64, ROPE)
    for parity in range(2):
        qsend[parity, 0:32, :] = tmpn[pl.ds(parity, 32, stride=2), :].astype(jnp.bfloat16)
        rope = tmpr[pl.ds(parity, 32, stride=2), :][:, :ROPE]
        qsend[parity, 32:48, :] = jnp.concatenate([rope[:16], rope[16:]], axis=1).astype(
            jnp.bfloat16
        )
    q_sib = remote(qsend.at[1 - c], qall.at[chip, c], qs_send, qs_recv, sib)
    q_sib.start()
    loop(HEADS, lambda j: load_ka(j).start())
    load_va = pltpu.make_async_copy(va_ref.at[0], va.at[j_me], local.at[9])
    load_va.start()
    own_rows = pl.ds(pl.multiple_of(quarter * VDIM, VDIM), VDIM)
    load_wo = [
        pltpu.make_async_copy(
            wo_ref.at[:, columns(quarter, n)], wo.at[own_rows, owned(n)], local.at[13 + n]
        )
        for n in range(2)
    ]
    for copy in load_wo:
        copy.start()

    def v_y(way):
        return remote(
            va_ref.at[0], va.at[j_me], vy_send.at[way], vy_recv.at[way], at(x, yy + 1 + 2 * way, c)
        )

    def v_relay(way):
        half = va.at[head_of(xl, yy + 3 - 2 * way), pl.ds(way * 256, 256), :]
        return remote(half, half, vf_send.at[way], vf_recv.at[way], at(x, yy + 1 + 2 * way, c))

    def v_x(i, way):
        half = va.at[head_of(xl, yy + i), pl.ds(way * 256, 256), :]
        src = va_ref.at[0, pl.ds(way * 256, 256), :] if i == 0 else half
        return remote(src, half, vx_send.at[i, way], vx_recv.at[i, way], at(x + 1 + 2 * way, yy, c))

    for way in range(2):
        v_y(way).start()
        v_x(0, way).start()

    qall[chip, c] = qsend[c]
    q_sib.wait_recv()

    def q_copy(k):
        _, to = plane(k + 1)
        return remote(qall.at[chip], qall.at[chip], q_send.at[k], q_recv.at[chip], to)

    loop(PLANE - 1, lambda k: q_copy(k).start())

    wo_copies = [
        remote(
            wo_ref.at[:, columns(2 * xl + 1 - c, n)], wo.at[own_rows, owned(n)],
            o_send.at[n], o_recv.at[n], sib,
        )
        for n in range(2)
    ]
    for copy in wo_copies:
        copy.start()

    def wo_x(way, core, n):
        return remote(
            wo_ref.at[pl.ds(way * 64, 64), columns(2 * (1 - xl) + core, n)],
            wo.at[pl.ds(pl.multiple_of(quarter * VDIM + way * 64, 64), 64), owned(n)],
            ox_send.at[way, core, n], ox_recv.at[way, c, n], at(x + 1 + 2 * way, yy, core),
        )

    def wo_x_arrived(way, core, n):
        rows = pl.ds(pl.multiple_of((2 * (1 - xl) + core) * VDIM + way * 64, 64), 64)
        remote(
            wo.at[rows, owned(n)], wo.at[rows, owned(n)],
            ox_send.at[way, core, n], ox_recv.at[way, core, n], at(x + 3 - 2 * way, yy, core),
        ).wait_recv()

    tick(1, 0)
    tick(1, 1)

    def q_arrived(k):
        other, to = plane(k + 1)
        remote(qall.at[other], qall.at[other], q_send.at[k], q_recv.at[other], to).wait_recv()

    loop(PLANE - 1, q_arrived)
    for way in range(2):
        for core in range(2):
            for n in range(2):
                wo_x(way, core, n).start()

    for g in range(2 * PLANE):
        m = qall[g // 2, g % 2]
        q32n[g * 32 : (g + 1) * 32, :] = m[0:32].astype(jnp.float32)
        r = m[32:48].astype(jnp.float32)
        q32r[g * 32 : g * 32 + 16, 0:ROPE] = r[:, :ROPE]
        q32r[g * 32 + 16 : g * 32 + 32, 0:ROPE] = r[:, ROPE:]


    loop(HEADS, lambda j: load_ka(j).wait())

    for j in range(HEADS):
        rows = slice(j * TOKENS, (j + 1) * TOKENS)
        nope = q32n[pl.ds(j, TOKENS, stride=HEADS), :].astype(jnp.bfloat16)
        part = jnp.dot(nope, ka[j], preferred_element_type=jnp.float32)
        q[rows, 0:LATENT] = (part * SCALE).astype(jnp.bfloat16)
        rope = q32r[pl.ds(j, TOKENS, stride=HEADS), :][:, :ROPE]
        q[rows, LATENT:WIDTH] = (rope * SCALE).astype(jnp.bfloat16)
    for way in range(2):
        v_y(way).wait_recv()
        v_relay(way).start()
    for way in range(2):
        v_x(3, way).start()
        v_x(1, way).start()
    tick(2, 0)
    tick(2, 1)

    crossed(0)
    attend(True, (0, 1), q, kv, acc, top, tot)
    for way in range(2):
        v_relay(way).wait_recv()
        v_x(2, way).start()
    crossed(2, 3)
    attend(False, (2, 3, 4, 5), q, kv, acc, top, tot)
    tick(3, 0)
    tick(3, 1)
    crossed(6, 7)
    attend(False, (6, 7, 8, 9), q, kv, acc, top, tot)
    crossed(10, 11)
    attend(False, (10, 11, 12, 13), q, kv, acc, top, tot)
    up(4, 0).wait_recv()
    across(14, 0).start()
    down(4, 1).wait_recv()
    across(14, 1).start()

    attend(False, (14,), q, kv, acc, top, tot)
    load_va.wait()

    for i in range(4):
        for way in range(2):
            v_x(i, way).wait_recv()
    crossed(14)

    per = TILE // TOKENS
    lane = lax.broadcasted_iota(jnp.int32, (TOKENS, 128), 1)
    row = lax.broadcasted_iota(jnp.int32, (16, 128), 0)
    first_tile = 1 - lax.div(j_me, 4)

    def order(i):
        return first_tile if i == 0 else 1 - first_tile

    def y_copy(other):
        j, t = lax.rem(other, OWNERS), lax.div(other, OWNERS)
        to = (2 * j + c, z, t)
        return remote(ysend.at[j, t], yrecv.at[chip], y_send.at[other], y_recv.at[chip], to)

    def finish(i, latent, new_top, total):
        for h in range(per):
            j = order(i) * per + h
            rows = slice(h * TOKENS, (h + 1) * TOKENS)
            y = jnp.dot(latent[rows], va[j], preferred_element_type=jnp.float32)
            y = y.astype(jnp.bfloat16)
            stats = jnp.where(lane % 2 == 0, new_top[rows], total[rows])
            stats = stats.T[0:16, :]
            high = stats.astype(jnp.bfloat16)
            left = stats - high.astype(jnp.float32)
            middle = left.astype(jnp.bfloat16)
            low = left - middle.astype(jnp.float32)
            stats = jnp.where(
                row < 2,
                high.astype(jnp.float32),
                jnp.where(row < 4, middle.astype(jnp.float32), low),
            ).astype(jnp.bfloat16)
            for t in range(2):
                ysend[j, t, 0:64, :] = y[t * 64 : (t + 1) * 64]
                ysend[j, t, 64:80, :] = stats
            for t in range(2):

                @pl.when(t * OWNERS + j != chip)
                def _():
                    y_copy(t * OWNERS + j).start()

    attend(False, (15,), q, kv, acc, top, tot, order, finish)
    yrecv[chip] = ysend[j_me, dp]

    def y_arrived(k):
        other, to = plane(k + 1)
        remote(yrecv.at[other], yrecv.at[other], y_send.at[k], y_recv.at[other], to).wait_recv()

    loop(PLANE - 1, y_arrived)

    stats = [yrecv[s, 64:80, :].astype(jnp.float32) for s in range(PLANE)]
    tops = jnp.concatenate([x[0:1] + x[2:3] + x[4:5] for x in stats], axis=0)
    sums = jnp.concatenate([x[1:2] + x[3:4] + x[5:6] for x in stats], axis=0)
    weight = sums * jnp.exp2(tops - jnp.max(tops, axis=0, keepdims=True))
    weight = weight / jnp.sum(weight, axis=0, keepdims=True)
    wts[...] = jnp.concatenate([weight, jnp.zeros((128 - PLANE, 128), jnp.float32)], axis=0).T
    w = wts[pl.ds(pl.multiple_of(dp * 64, 64), 64), :]
    merged = None
    for s in range(PLANE):
        term = yrecv[s, 0:64, :].astype(jnp.float32) * w[:, s : s + 1]
        merged = term if merged is None else merged + term
    ho[quarter] = merged.astype(jnp.bfloat16)

    def h_copy(k):
        core = 1 - c if k % 2 else c
        x_low = 1 - xl if k >= 2 else xl
        return remote(
            ho.at[quarter], ho.at[quarter], h_send.at[k - 1], h_recv.at[k - 1], at(2 * dp + x_low, yy, core)
        )

    for k in (2, 3, 1):
        h_copy(k).start()
    for n in range(2):
        load_wo[n].wait()
        wo_copies[n].wait_recv()
        for way in range(2):
            for core in range(2):
                wo_x_arrived(way, core, n)
    for k in (1, 2, 3):
        h_copy(k).wait_recv()

    heads = jnp.concatenate([ho[k] for k in range(4)], axis=1)

    def d_copy(n, k):
        other = lax.rem(yy + k, 4)
        return remote(
            dsend.at[n, other], drecv.at[n, yy], d_send.at[n, k - 1], d_recv.at[n, yy], at(x, other, c)
        )

    def d_arrived(n, k):
        other = lax.rem(yy + k, 4)
        remote(
            dsend.at[n, other], drecv.at[n, other], d_send.at[n, k - 1], d_recv.at[n, other],
            at(x, other, c),
        ).wait_recv()

    for n in range(2):
        terms = jnp.dot(
            heads, wo[:, n * COLS : (n + 1) * COLS], preferred_element_type=jnp.float32
        )
        for i in range(4):
            dsend[n, i] = jnp.concatenate(
                [terms[i * 8 : i * 8 + 8], terms[32 + i * 8 : 40 + i * 8]], axis=0
            ).astype(jnp.bfloat16)
        for k in (2, 1, 3):
            d_copy(n, k).start()

    def e_copy(n, x_low, core):
        to_z = quarter + 4 * n
        return (to_z == z) & (x_low == xl) & (core == c), remote(
            esend.at[n, x_low, core], erecv.at[z], e_send.at[n, x_low, core], e_recv.at[z],
            ((4 * x_low + yy) * 2 + core, to_z, dp),
        )

    for n in range(2):
        drecv[n, yy] = dsend[n, yy]
        for k in (1, 3, 2):
            d_arrived(n, k)
        summed = drecv[n, 0].astype(jnp.float32)
        for i in range(1, 4):
            summed = summed + drecv[n, i].astype(jnp.float32)
        for x_low in range(2):
            for core in range(2):
                start = x_low * 8 + core * 4
                pieces = [summed[start : start + 4, k * 128 : (k + 1) * 128] for k in range(7)]
                pieces.append(jnp.zeros((4, 128), jnp.float32))
                esend[n, x_low, core] = jnp.concatenate(pieces, axis=0).astype(jnp.bfloat16)
                here, copy = e_copy(n, x_low, core)

                @pl.when(jnp.logical_not(here))
                def _():
                    copy.start()

                @pl.when(here)
                def _():
                    erecv[z] = esend[n, x_low, core]

    q_sib.wait_send()
    for step in range(1, 5):
        for h in range(2):
            if step < 4 or h == 0:
                up(step, h).wait_send()
                down(step, 1 - h).wait_send()
    for slot in SIB_ORDER:
        for h in range(2):
            across(slot, h).wait_send()
    for copy in wo_copies:
        copy.wait_send()
    for k in (1, 2, 3):
        h_copy(k).wait_send()

    def sent_plane(k):
        q_copy(k).wait_send()
        y_copy(plane(k + 1)[0]).wait_send()

    loop(PLANE - 1, sent_plane)
    for way in range(2):
        v_y(way).wait_send()
        v_relay(way).wait_send()
        for i in range(4):
            v_x(i, way).wait_send()
        for core in range(2):
            for n in range(2):
                wo_x(way, core, n).wait_send()

    from_x, from_core = lax.rem(lax.div(z, 2), 2), lax.rem(z, 2)

    def e_arrived(s):
        frm = ((4 * from_x + yy) * 2 + from_core, s, dp)

        @pl.when(jnp.logical_not((s == z) & (from_x == xl) & (from_core == c)))
        def _():
            remote(
                esend.at[0, 0, 0], erecv.at[s], e_send.at[0, 0, 0], e_recv.at[s], frm
            ).wait_recv()

    loop(Z, e_arrived)
    result = erecv[0].astype(jnp.float32)
    for s in range(1, Z):
        result = result + erecv[s].astype(jnp.float32)
    for k in range(7):
        out_ref[:, k * 128 : (k + 1) * 128] = result[4 * k : 4 * k + 4]

    for n in range(2):
        for k in (1, 2, 3):
            d_copy(n, k).wait_send()
        for x_low in range(2):
            for core in range(2):
                here, copy = e_copy(n, x_low, core)

                @pl.when(jnp.logical_not(here))
                def _():
                    copy.wait_send()


def body(query_nope, query_rope, latent_cache, key_absorb, value_absorb, output_proj):
    vmem = pl.BlockSpec(memory_space=pltpu.VMEM)
    hbm = pl.BlockSpec(memory_space=pl.ANY)
    bf16, f32 = jnp.bfloat16, jnp.float32
    dma = pltpu.SemaphoreType.DMA
    return pl.pallas_call(
        kernel,
        out_shape=jax.ShapeDtypeStruct((4, COLS), f32),
        in_specs=[hbm] * 6,
        out_specs=vmem,
        scratch_shapes=[
            pltpu.VMEM((16, 2, HALFB + PACK, LATENT), bf16),
            pltpu.VMEM((ROWS, WIDTH), bf16),
            pltpu.VMEM((ROWS, LATENT), f32),
            pltpu.VMEM((ROWS, 128), f32),
            pltpu.VMEM((ROWS, 128), f32),
            pltpu.VMEM((HEADS, NOPE, LATENT), bf16),
            pltpu.VMEM((HEADS, LATENT, VDIM), bf16),
            pltpu.VMEM((4 * VDIM, QUARTER), bf16),
            pltpu.VMEM((4, 16, NOPE), bf16),
            pltpu.VMEM((4, 16, ROPE), bf16),
            pltpu.VMEM((64, NOPE), f32),
            pltpu.VMEM((64, 128), f32),
            pltpu.VMEM((2, MSG, 128), bf16),
            pltpu.VMEM((PLANE, 2, MSG, 128), bf16),
            pltpu.VMEM((ROWS, NOPE), f32),
            pltpu.VMEM((ROWS, 128), f32),
            pltpu.VMEM((BLOCK, WIDTH), bf16),
            pltpu.VMEM((HEADS, 2, 80, VDIM), bf16),
            pltpu.VMEM((PLANE, 80, VDIM), bf16),
            pltpu.VMEM((128, 128), f32),
            pltpu.VMEM((4, 64, VDIM), bf16),
            pltpu.VMEM((2, 4, 16, COLS), bf16),
            pltpu.VMEM((2, 4, 16, COLS), bf16),
            pltpu.VMEM((2, 2, 2, 32, 128), bf16),
            pltpu.VMEM((Z, 32, 128), bf16),
            dma((15,)),
            dma, dma, dma((PLANE - 1,)), dma((PLANE,)),
            dma((4, 2)), dma((4, 2)), dma((4, 2)), dma((4, 2)), dma((8, 2)), dma((8, 2)),
            dma((2,)), dma((2,)), dma((2,)), dma((2,)), dma((4, 2)), dma((4, 2)),
            dma((2,)), dma((2,)), dma((2, 2, 2)), dma((2, 2, 2)),
            dma((PLANE,)), dma((PLANE,)),
            dma((3,)), dma((3,)), dma((2, 3)), dma((2, 4)), dma((2, 2, 2)), dma((Z,)),
        ],
        compiler_params=pltpu.CompilerParams(
            collective_id=0, has_side_effects=True, vmem_limit_bytes=127 * 512 * 1024
        ),
        cost_estimate=pl.CostEstimate(
            flops=7_000_000_000, bytes_accessed=10_000_000, transcendentals=3_145_728
        ),
        name="latent_attention",
    )(query_nope, query_rope, latent_cache, key_absorb, value_absorb, output_proj)


def solution(mesh):
    in_specs = (
        P(("dp", "prefix"), "head", None),
        P(("dp", "prefix"), "head", None),
        P(("prefix", "head", "dp"), None),
        P("head", None, None),
        P(("head", "prefix"), None, None),
        P(("head", "prefix"), None),
    )
    out_specs = P(("dp", "prefix"), "head")
    return jax.shard_map(body, mesh=mesh, in_specs=in_specs, out_specs=out_specs, check_vma=False)
```

```python
import math

import jax
import jax.numpy as jnp
from jax import lax
from jax.experimental import pallas as pl
from jax.experimental.pallas import tpu as pltpu
from jax.sharding import PartitionSpec as P

MESH = pl.DeviceIdType.MESH

D = 7168
NOPE, ROPE, VDIM, LATENT = 128, 64, 128, 512
WIDTH = LATENT + ROPE
TOKENS = 128
Z = 8
PLANE = 16
OWNERS = 8
HEADS = 8
ROWS = HEADS * TOKENS
BLOCK = 192
MSG = 48
QUARTER = D // 4
COLS = D // Z
SCALE = (NOPE + ROPE) ** -0.5 * math.log2(math.e)

HALFB = BLOCK // 2
PACK = 16
UP = (0, 2, 6, 10, 14)
DOWN = (0, 3, 7, 11, 14)
SIB_OF = {0: 1, 2: 4, 3: 5, 6: 8, 7: 9, 10: 12, 11: 13, 14: 15}
SIB_ORDER = (0, 2, 3, 6, 7, 10, 11, 14)
TILE = 512
OFFSETS = sorted(
    [(dx, dy) for dx in range(4) for dy in range(4) if dx or dy],
    key=lambda o: -(min(o[0], 4 - o[0]) + min(o[1], 4 - o[1])),
)


def chunk_keys(kv, blocks):
    latent, rope = [], []
    for b in blocks:
        for h in range(2):
            latent.append(kv[b, h, 0:HALFB, :])
            packed = kv[b, h, HALFB : HALFB + PACK, 0 : 6 * ROPE]
            for g in range(6):
                rope.append(packed[:, g * ROPE : (g + 1) * ROPE])
    latent = jnp.concatenate(latent, axis=0)
    return jnp.concatenate([latent, jnp.concatenate(rope, axis=0)], axis=1), latent


def attend(first, blocks, q, kv, acc, top, tot, finish=None):
    keys, values = chunk_keys(kv, blocks)
    n = ROWS // TILE

    def at(i):
        return pl.ds(i * TILE, TILE)

    def score(i):
        return lax.dot_general(
            q[at(i), :], keys, (((1,), (1,)), ((), ())), preferred_element_type=jnp.float32
        )

    s = score(0)
    for i in range(n):
        later = score(i + 1) if i + 1 < n else None
        rows = at(i)
        high = jnp.max(s, axis=1, keepdims=True)
        if first:
            new_top = jnp.broadcast_to(high, (TILE, 128))
        else:
            old_top = top[rows, :]
            new_top = jnp.maximum(old_top, high)
            alpha = jnp.exp2(old_top - new_top)
        part = None
        pieces = []
        for k in range(0, s.shape[1], 128):
            width = min(128, s.shape[1] - k)
            e = jnp.exp2(s[:, k : k + width] - new_top[:, :width])
            pieces.append(e.astype(jnp.bfloat16))
            if width < 128:
                e = jnp.concatenate([e, jnp.zeros((TILE, 128 - width), jnp.float32)], axis=1)
            part = e if part is None else part + e
        p = jnp.concatenate(pieces, axis=1)
        out = jnp.dot(p, values, preferred_element_type=jnp.float32)
        if not first:
            part = tot[rows, :] * alpha + part
        if finish is not None:
            total = jnp.sum(part, axis=1, keepdims=True)
            scale = 1.0 / total
            latent = []
            for k in range(LATENT // 128):
                cols = slice(k * 128, (k + 1) * 128)
                latent.append(((acc[rows, cols] * alpha + out[:, cols]) * scale).astype(jnp.bfloat16))
            finish(i, jnp.concatenate(latent, axis=1), new_top, total)
        else:
            top[rows, :] = new_top
            tot[rows, :] = part
            for k in range(LATENT // 128):
                cols = slice(k * 128, (k + 1) * 128)
                if first:
                    acc[rows, cols] = out[:, cols]
                else:
                    acc[rows, cols] = acc[rows, cols] * alpha + out[:, cols]
        s = later


def kernel(
    qn_ref, qr_ref, kv_ref, ka_ref, va_ref, wo_ref, out_ref,
    kv, q, acc, top, tot, ka, va, wo,
    qn, qr, tmpn, tmpr, qsend, qall, q32n, q32r,
    kvraw, ysend, yrecv, wts, ho, dsend, drecv, esend, erecv,
    local, qs_send, qs_recv, q_send, q_recv,
    up_send, up_recv, dn_send, dn_recv, sb_send, sb_recv,
    vy_send, vy_recv, vf_send, vf_recv, vx_send, vx_recv, o_send, o_recv, ox_send, ox_recv,
    y_send, y_recv, h_send, h_recv, d_send, d_recv, e_send, e_recv,
):
    prefix, z, dp = lax.axis_index("prefix"), lax.axis_index("head"), lax.axis_index("dp")
    c = lax.rem(prefix, 2)
    j_me = lax.div(prefix, 2)
    chip = dp * OWNERS + j_me
    sib = (prefix + 1 - 2 * c, z, dp)
    above = (prefix, lax.rem(z + 1, Z), dp)
    below = (prefix, lax.rem(z + Z - 1, Z), dp)

    xl, yy = lax.div(j_me, 4), lax.rem(j_me, 4)
    x = 2 * dp + xl
    quarter = 2 * xl + c

    def at(x_to, y_to, core):
        x_to, y_to = lax.rem(x_to, 4), lax.rem(y_to, 4)
        return ((lax.rem(x_to, 2) * 4 + y_to) * 2 + core, z, lax.div(x_to, 2))

    def peer(offset):
        x_to, y_to = lax.rem(x + offset[0], 4), lax.rem(yy + offset[1], 4)
        x_low, x_high = lax.rem(x_to, 2), lax.div(x_to, 2)
        index = x_low * 4 + y_to
        return x_high * OWNERS + index, (2 * index + c, z, x_high)

    def head(r):
        x_low = 1 - xl if r < 4 else xl
        return x_low * 4 + lax.rem(yy + (2, 1, 3, 0)[r % 4], 4)

    def head_of(x_low, y_of):
        return x_low * 4 + lax.rem(y_of, 4)

    def columns(quarter_of, n):
        return pl.ds(pl.multiple_of((quarter_of + 4 * n) * COLS, 128), COLS)

    def owned(n):
        return pl.ds(n * COLS, COLS)

    def remote(src, dst, ssem, rsem, to):
        return pltpu.make_async_remote_copy(
            src_ref=src, dst_ref=dst, send_sem=ssem, recv_sem=rsem, device_id=to, device_id_type=MESH
        )

    def loop(n, body):
        def step(k, carry):
            body(k)
            return carry

        lax.fori_loop(0, n, step, 0)

    def load_ka(r):
        return pltpu.make_async_copy(ka_ref.at[2 * head(r) + c], ka.at[r], local.at[r])

    load_kv = pltpu.make_async_copy(kv_ref, kvraw, local.at[8])
    load_kv.start()
    load_qn = pltpu.make_async_copy(qn_ref, qn, local.at[11])
    load_qn.start()
    load_qr = pltpu.make_async_copy(qr_ref, qr, local.at[12])
    load_qr.start()

    barrier = pltpu.get_barrier_semaphore()

    def greet(to):
        pl.semaphore_signal(barrier, inc=1, device_id=to, device_id_type=MESH)

    for offset in OFFSETS:
        greet(peer(offset)[1])
    for to in (above, below, sib):
        greet(to)

    load_kv.wait()
    for h in range(2):
        rows = slice(h * HALFB, (h + 1) * HALFB)
        kv[0, h, 0:HALFB, :] = kvraw[rows, 0:LATENT]
        rope = kvraw[rows, LATENT:WIDTH].astype(jnp.float32)
        packed = [rope[g * PACK : (g + 1) * PACK] for g in range(6)]
        packed.append(jnp.zeros((PACK, LATENT - 6 * ROPE), jnp.float32))
        kv[0, h, HALFB : HALFB + PACK, :] = jnp.concatenate(packed, axis=1).astype(jnp.bfloat16)

    pl.semaphore_wait(barrier, 3 + (PLANE - 1))

    def up(step, h):
        return remote(
            kv.at[UP[step - 1], h], kv.at[UP[step], h],
            up_send.at[step - 1, h], up_recv.at[step - 1, h], above,
        )

    def down(step, h):
        return remote(
            kv.at[DOWN[step - 1], h], kv.at[DOWN[step], h],
            dn_send.at[step - 1, h], dn_recv.at[step - 1, h], below,
        )

    def across(slot, h):
        i = SIB_ORDER.index(slot)
        return remote(kv.at[slot, h], kv.at[SIB_OF[slot], h], sb_send.at[i, h], sb_recv.at[i, h], sib)

    def tick(step, h):
        up(step, h).wait_recv()
        if step < 3 or (step == 3 and h == 0):
            up(step + 1, h).start()
        down(step, 1 - h).wait_recv()
        if step < 3 or (step == 3 and h == 0):
            down(step + 1, 1 - h).start()
        across(UP[step], h).start()
        across(DOWN[step], 1 - h).start()

    def crossed(*slots):
        for slot in slots:
            for h in range(2):
                across(slot, h).wait_recv()

    for h in range(2):
        up(1, h).start()
        down(1, 1 - h).start()
    across(0, 0).start()
    across(0, 1).start()

    load_qn.wait()
    load_qr.wait()
    tmpn[...] = qn[...].astype(jnp.float32).reshape(64, NOPE)
    tmpr[:, :ROPE] = qr[...].astype(jnp.float32).reshape(64, ROPE)
    for parity in range(2):
        qsend[parity, 0:32, :] = tmpn[pl.ds(parity, 32, stride=2), :].astype(jnp.bfloat16)
        rope = tmpr[pl.ds(parity, 32, stride=2), :][:, :ROPE]
        qsend[parity, 32:48, :] = jnp.concatenate([rope[:16], rope[16:]], axis=1).astype(
            jnp.bfloat16
        )
    q_sib = remote(qsend.at[1 - c], qall.at[chip, c], qs_send, qs_recv, sib)
    q_sib.start()
    for r in range(HEADS):
        load_ka(r).start()
    load_va = pltpu.make_async_copy(va_ref.at[0], va.at[j_me], local.at[9])
    load_va.start()
    own_rows = pl.ds(pl.multiple_of(quarter * VDIM, VDIM), VDIM)
    load_wo = [
        pltpu.make_async_copy(
            wo_ref.at[:, columns(quarter, n)], wo.at[own_rows, owned(n)], local.at[13 + n]
        )
        for n in range(2)
    ]
    for copy in load_wo:
        copy.start()

    def v_y(way):
        return remote(
            va_ref.at[0], va.at[j_me], vy_send.at[way], vy_recv.at[way], at(x, yy + 1 + 2 * way, c)
        )

    def v_relay(way):
        half = va.at[head_of(xl, yy + 3 - 2 * way), pl.ds(way * 256, 256), :]
        return remote(half, half, vf_send.at[way], vf_recv.at[way], at(x, yy + 1 + 2 * way, c))

    def v_x(i, way):
        half = va.at[head_of(xl, yy + i), pl.ds(way * 256, 256), :]
        src = va_ref.at[0, pl.ds(way * 256, 256), :] if i == 0 else half
        return remote(src, half, vx_send.at[i, way], vx_recv.at[i, way], at(x + 1 + 2 * way, yy, c))

    for way in range(2):
        v_y(way).start()
        v_x(0, way).start()

    qall[chip, c] = qsend[c]
    q_sib.wait_recv()

    def q_copy(k):
        _, to = peer(OFFSETS[k])
        return remote(qall.at[chip], qall.at[chip], q_send.at[k], q_recv.at[chip], to)

    for k in range(PLANE - 1):
        q_copy(k).start()

    wo_copies = [
        remote(
            wo_ref.at[:, columns(2 * xl + 1 - c, n)], wo.at[own_rows, owned(n)],
            o_send.at[n], o_recv.at[n], sib,
        )
        for n in range(2)
    ]
    for copy in wo_copies:
        copy.start()

    def wo_x(way, core, n):
        return remote(
            wo_ref.at[pl.ds(way * 64, 64), columns(2 * (1 - xl) + core, n)],
            wo.at[pl.ds(pl.multiple_of(quarter * VDIM + way * 64, 64), 64), owned(n)],
            ox_send.at[way, core, n], ox_recv.at[way, c, n], at(x + 1 + 2 * way, yy, core),
        )

    def wo_x_arrived(way, core, n):
        rows = pl.ds(pl.multiple_of((2 * (1 - xl) + core) * VDIM + way * 64, 64), 64)
        remote(
            wo.at[rows, owned(n)], wo.at[rows, owned(n)],
            ox_send.at[way, core, n], ox_recv.at[way, core, n], at(x + 3 - 2 * way, yy, core),
        ).wait_recv()

    tick(1, 0)
    tick(1, 1)

    for k in range(PLANE - 1):
        other, to = peer(OFFSETS[k])
        remote(qall.at[other], qall.at[other], q_send.at[k], q_recv.at[other], to).wait_recv()
    for way in range(2):
        for core in range(2):
            for n in range(2):
                wo_x(way, core, n).start()

    for g in range(2 * PLANE):
        m = qall[g // 2, g % 2]
        q32n[g * 32 : (g + 1) * 32, :] = m[0:32].astype(jnp.float32)
        r = m[32:48].astype(jnp.float32)
        q32r[g * 32 : g * 32 + 16, 0:ROPE] = r[:, :ROPE]
        q32r[g * 32 + 16 : g * 32 + 32, 0:ROPE] = r[:, ROPE:]


    for r in range(HEADS):
        load_ka(r).wait()

    for r in range(HEADS):
        j = head(r)
        rows = slice(r * TOKENS, (r + 1) * TOKENS)
        nope = q32n[pl.ds(j, TOKENS, stride=HEADS), :].astype(jnp.bfloat16)
        part = jnp.dot(nope, ka[r], preferred_element_type=jnp.float32)
        q[rows, 0:LATENT] = (part * SCALE).astype(jnp.bfloat16)
        rope = q32r[pl.ds(j, TOKENS, stride=HEADS), :][:, :ROPE]
        q[rows, LATENT:WIDTH] = (rope * SCALE).astype(jnp.bfloat16)
    for way in range(2):
        v_y(way).wait_recv()
        v_relay(way).start()
    for way in range(2):
        v_x(3, way).start()
        v_x(1, way).start()
    tick(2, 0)
    tick(2, 1)

    crossed(0)
    attend(True, (0, 1), q, kv, acc, top, tot)
    for way in range(2):
        v_relay(way).wait_recv()
        v_x(2, way).start()
    crossed(2, 3)
    attend(False, (2, 3, 4, 5), q, kv, acc, top, tot)
    tick(3, 0)
    tick(3, 1)
    crossed(6, 7)
    attend(False, (6, 7, 8, 9), q, kv, acc, top, tot)
    crossed(10, 11)
    attend(False, (10, 11, 12, 13), q, kv, acc, top, tot)
    up(4, 0).wait_recv()
    across(14, 0).start()
    down(4, 1).wait_recv()
    across(14, 1).start()

    attend(False, (14,), q, kv, acc, top, tot)
    load_va.wait()

    for i in range(4):
        for way in range(2):
            v_x(i, way).wait_recv()
    crossed(14)

    per = TILE // TOKENS
    lane = lax.broadcasted_iota(jnp.int32, (TOKENS, 128), 1)
    row = lax.broadcasted_iota(jnp.int32, (16, 128), 0)

    def y_copy(r, t):
        j = head(r)
        return remote(
            ysend.at[r, t], yrecv.at[chip], y_send.at[r, t], y_recv.at[chip], (2 * j + c, z, t)
        )

    def each_y(r, action):
        for t in range(2):
            if r < HEADS - 1:
                action(y_copy(r, t))
            else:

                @pl.when(t != dp)
                def _():
                    action(y_copy(r, t))

    def finish(i, latent, new_top, total):
        for h in range(per):
            r = i * per + h
            j = head(r)
            rows = slice(h * TOKENS, (h + 1) * TOKENS)
            y = jnp.dot(latent[rows], va[j], preferred_element_type=jnp.float32)
            y = y.astype(jnp.bfloat16)
            stats = jnp.where(lane % 2 == 0, new_top[rows], total[rows])
            stats = stats.T[0:16, :]
            high = stats.astype(jnp.bfloat16)
            left = stats - high.astype(jnp.float32)
            middle = left.astype(jnp.bfloat16)
            low = left - middle.astype(jnp.float32)
            stats = jnp.where(
                row < 2,
                high.astype(jnp.float32),
                jnp.where(row < 4, middle.astype(jnp.float32), low),
            ).astype(jnp.bfloat16)
            for t in range(2):
                ysend[r, t, 0:64, :] = y[t * 64 : (t + 1) * 64]
                ysend[r, t, 64:80, :] = stats
            each_y(r, lambda copy: copy.start())

    attend(False, (15,), q, kv, acc, top, tot, finish)
    yrecv[chip] = ysend[HEADS - 1, dp]
    for offset in OFFSETS[::-1]:
        other, to = peer(offset)
        remote(
            yrecv.at[other], yrecv.at[other], y_send.at[0, 0], y_recv.at[other], to
        ).wait_recv()

    stats = [yrecv[s, 64:80, :].astype(jnp.float32) for s in range(PLANE)]
    tops = jnp.concatenate([x[0:1] + x[2:3] + x[4:5] for x in stats], axis=0)
    sums = jnp.concatenate([x[1:2] + x[3:4] + x[5:6] for x in stats], axis=0)
    weight = sums * jnp.exp2(tops - jnp.max(tops, axis=0, keepdims=True))
    weight = weight / jnp.sum(weight, axis=0, keepdims=True)
    wts[...] = jnp.concatenate([weight, jnp.zeros((128 - PLANE, 128), jnp.float32)], axis=0).T
    w = wts[pl.ds(pl.multiple_of(dp * 64, 64), 64), :]
    merged = None
    for s in range(PLANE):
        term = yrecv[s, 0:64, :].astype(jnp.float32) * w[:, s : s + 1]
        merged = term if merged is None else merged + term
    ho[quarter] = merged.astype(jnp.bfloat16)

    def h_copy(k):
        core = 1 - c if k % 2 else c
        x_low = 1 - xl if k >= 2 else xl
        return remote(
            ho.at[quarter], ho.at[quarter], h_send.at[k - 1], h_recv.at[k - 1], at(2 * dp + x_low, yy, core)
        )

    for k in (2, 3, 1):
        h_copy(k).start()
    for n in range(2):
        load_wo[n].wait()
        wo_copies[n].wait_recv()
        for way in range(2):
            for core in range(2):
                wo_x_arrived(way, core, n)
    for k in (1, 2, 3):
        h_copy(k).wait_recv()

    heads = jnp.concatenate([ho[k] for k in range(4)], axis=1)

    def d_copy(n, k):
        other = lax.rem(yy + k, 4)
        return remote(
            dsend.at[n, other], drecv.at[n, yy], d_send.at[n, k - 1], d_recv.at[n, yy], at(x, other, c)
        )

    def d_arrived(n, k):
        other = lax.rem(yy + k, 4)
        remote(
            dsend.at[n, other], drecv.at[n, other], d_send.at[n, k - 1], d_recv.at[n, other],
            at(x, other, c),
        ).wait_recv()

    for n in range(2):
        terms = jnp.dot(
            heads, wo[:, n * COLS : (n + 1) * COLS], preferred_element_type=jnp.float32
        )
        for i in range(4):
            dsend[n, i] = jnp.concatenate(
                [terms[i * 8 : i * 8 + 8], terms[32 + i * 8 : 40 + i * 8]], axis=0
            ).astype(jnp.bfloat16)
        for k in (2, 1, 3):
            d_copy(n, k).start()

    def e_copy(n, x_low, core):
        to_z = quarter + 4 * n
        return (to_z == z) & (x_low == xl) & (core == c), remote(
            esend.at[n, x_low, core], erecv.at[z], e_send.at[n, x_low, core], e_recv.at[z],
            ((4 * x_low + yy) * 2 + core, to_z, dp),
        )

    for n in range(2):
        drecv[n, yy] = dsend[n, yy]
        for k in (1, 3, 2):
            d_arrived(n, k)
        summed = drecv[n, 0].astype(jnp.float32)
        for i in range(1, 4):
            summed = summed + drecv[n, i].astype(jnp.float32)
        for x_low in range(2):
            for core in range(2):
                start = x_low * 8 + core * 4
                pieces = [summed[start : start + 4, k * 128 : (k + 1) * 128] for k in range(7)]
                pieces.append(jnp.zeros((4, 128), jnp.float32))
                esend[n, x_low, core] = jnp.concatenate(pieces, axis=0).astype(jnp.bfloat16)
                here, copy = e_copy(n, x_low, core)

                @pl.when(jnp.logical_not(here))
                def _():
                    copy.start()

                @pl.when(here)
                def _():
                    erecv[z] = esend[n, x_low, core]

    q_sib.wait_send()
    for step in range(1, 5):
        for h in range(2):
            if step < 4 or h == 0:
                up(step, h).wait_send()
                down(step, 1 - h).wait_send()
    for slot in SIB_ORDER:
        for h in range(2):
            across(slot, h).wait_send()
    for copy in wo_copies:
        copy.wait_send()
    for k in (1, 2, 3):
        h_copy(k).wait_send()

    for k in range(PLANE - 1):
        q_copy(k).wait_send()
    for r in range(HEADS):
        each_y(r, lambda copy: copy.wait_send())
    for way in range(2):
        v_y(way).wait_send()
        v_relay(way).wait_send()
        for i in range(4):
            v_x(i, way).wait_send()
        for core in range(2):
            for n in range(2):
                wo_x(way, core, n).wait_send()

    from_x, from_core = lax.rem(lax.div(z, 2), 2), lax.rem(z, 2)

    def e_arrived(s):
        frm = ((4 * from_x + yy) * 2 + from_core, s, dp)

        @pl.when(jnp.logical_not((s == z) & (from_x == xl) & (from_core == c)))
        def _():
            remote(
                esend.at[0, 0, 0], erecv.at[s], e_send.at[0, 0, 0], e_recv.at[s], frm
            ).wait_recv()

    loop(Z, e_arrived)
    result = erecv[0].astype(jnp.float32)
    for s in range(1, Z):
        result = result + erecv[s].astype(jnp.float32)
    for k in range(7):
        out_ref[:, k * 128 : (k + 1) * 128] = result[4 * k : 4 * k + 4]

    for n in range(2):
        for k in (1, 2, 3):
            d_copy(n, k).wait_send()
        for x_low in range(2):
            for core in range(2):
                here, copy = e_copy(n, x_low, core)

                @pl.when(jnp.logical_not(here))
                def _():
                    copy.wait_send()


def body(query_nope, query_rope, latent_cache, key_absorb, value_absorb, output_proj):
    vmem = pl.BlockSpec(memory_space=pltpu.VMEM)
    hbm = pl.BlockSpec(memory_space=pl.ANY)
    bf16, f32 = jnp.bfloat16, jnp.float32
    dma = pltpu.SemaphoreType.DMA
    return pl.pallas_call(
        kernel,
        out_shape=jax.ShapeDtypeStruct((4, COLS), f32),
        in_specs=[hbm] * 6,
        out_specs=vmem,
        scratch_shapes=[
            pltpu.VMEM((16, 2, HALFB + PACK, LATENT), bf16),
            pltpu.VMEM((ROWS, WIDTH), bf16),
            pltpu.VMEM((ROWS, LATENT), f32),
            pltpu.VMEM((ROWS, 128), f32),
            pltpu.VMEM((ROWS, 128), f32),
            pltpu.VMEM((HEADS, NOPE, LATENT), bf16),
            pltpu.VMEM((HEADS, LATENT, VDIM), bf16),
            pltpu.VMEM((4 * VDIM, QUARTER), bf16),
            pltpu.VMEM((4, 16, NOPE), bf16),
            pltpu.VMEM((4, 16, ROPE), bf16),
            pltpu.VMEM((64, NOPE), f32),
            pltpu.VMEM((64, 128), f32),
            pltpu.VMEM((2, MSG, 128), bf16),
            pltpu.VMEM((PLANE, 2, MSG, 128), bf16),
            pltpu.VMEM((ROWS, NOPE), f32),
            pltpu.VMEM((ROWS, 128), f32),
            pltpu.VMEM((BLOCK, WIDTH), bf16),
            pltpu.VMEM((HEADS, 2, 80, VDIM), bf16),
            pltpu.VMEM((PLANE, 80, VDIM), bf16),
            pltpu.VMEM((128, 128), f32),
            pltpu.VMEM((4, 64, VDIM), bf16),
            pltpu.VMEM((2, 4, 16, COLS), bf16),
            pltpu.VMEM((2, 4, 16, COLS), bf16),
            pltpu.VMEM((2, 2, 2, 32, 128), bf16),
            pltpu.VMEM((Z, 32, 128), bf16),
            dma((15,)),
            dma, dma, dma((PLANE - 1,)), dma((PLANE,)),
            dma((4, 2)), dma((4, 2)), dma((4, 2)), dma((4, 2)), dma((8, 2)), dma((8, 2)),
            dma((2,)), dma((2,)), dma((2,)), dma((2,)), dma((4, 2)), dma((4, 2)),
            dma((2,)), dma((2,)), dma((2, 2, 2)), dma((2, 2, 2)),
            dma((HEADS, 2)), dma((PLANE,)),
            dma((3,)), dma((3,)), dma((2, 3)), dma((2, 4)), dma((2, 2, 2)), dma((Z,)),
        ],
        compiler_params=pltpu.CompilerParams(
            collective_id=0, has_side_effects=True, vmem_limit_bytes=127 * 512 * 1024
        ),
        cost_estimate=pl.CostEstimate(
            flops=7_000_000_000, bytes_accessed=10_000_000, transcendentals=3_145_728
        ),
        name="latent_attention",
    )(query_nope, query_rope, latent_cache, key_absorb, value_absorb, output_proj)


def solution(mesh):
    in_specs = (
        P(("dp", "prefix"), "head", None),
        P(("dp", "prefix"), "head", None),
        P(("prefix", "head", "dp"), None),
        P("head", None, None),
        P(("head", "prefix"), None, None),
        P(("head", "prefix"), None),
    )
    out_specs = P(("dp", "prefix"), "head")
    return jax.shard_map(body, mesh=mesh, in_specs=in_specs, out_specs=out_specs, check_vma=False)
```

```python
import math

import jax
import jax.numpy as jnp
from jax import lax
from jax.experimental import pallas as pl
from jax.experimental.pallas import tpu as pltpu
from jax.sharding import PartitionSpec as P

MESH = pl.DeviceIdType.MESH

D = 7168
NOPE, ROPE, VDIM, LATENT = 128, 64, 128, 512
WIDTH = LATENT + ROPE
TOKENS = 128
Z = 8
PLANE = 16
OWNERS = 8
HEADS = 8
ROWS = HEADS * TOKENS
BLOCK = 192
MSG = 48
QUARTER = D // 4
COLS = D // Z
SCALE = (NOPE + ROPE) ** -0.5 * math.log2(math.e)

HALFB = BLOCK // 2
PACK = 16
UP = (0, 2, 6, 10, 14)
DOWN = (0, 3, 7, 11, 14)
SIB_OF = {0: 1, 2: 4, 3: 5, 6: 8, 7: 9, 10: 12, 11: 13, 14: 15}
SIB_ORDER = (0, 2, 3, 6, 7, 10, 11, 14)
TILE = 512
OFFSETS = sorted(
    [(dx, dy) for dx in range(4) for dy in range(4) if dx or dy],
    key=lambda o: -(min(o[0], 4 - o[0]) + min(o[1], 4 - o[1])),
)


def chunk_keys(kv, blocks):
    latent, rope = [], []
    for b in blocks:
        for h in range(2):
            latent.append(kv[b, h, 0:HALFB, :])
            packed = kv[b, h, HALFB : HALFB + PACK, 0 : 6 * ROPE]
            for g in range(6):
                rope.append(packed[:, g * ROPE : (g + 1) * ROPE])
    latent = jnp.concatenate(latent, axis=0)
    return jnp.concatenate([latent, jnp.concatenate(rope, axis=0)], axis=1), latent


def attend(first, blocks, q, kv, acc, top, tot, finish=None):
    keys, values = chunk_keys(kv, blocks)
    n = ROWS // TILE

    def at(i):
        return pl.ds(i * TILE, TILE)

    def score(i):
        return lax.dot_general(
            q[at(i), :], keys, (((1,), (1,)), ((), ())), preferred_element_type=jnp.float32
        )

    s = score(0)
    for i in range(n):
        later = score(i + 1) if i + 1 < n else None
        rows = at(i)
        high = jnp.max(s, axis=1, keepdims=True)
        if first:
            new_top = jnp.broadcast_to(high, (TILE, 128))
        else:
            old_top = top[rows, :]
            new_top = jnp.maximum(old_top, high)
            alpha = jnp.exp2(old_top - new_top)
        part = None
        pieces = []
        for k in range(0, s.shape[1], 128):
            width = min(128, s.shape[1] - k)
            e = jnp.exp2(s[:, k : k + width] - new_top[:, :width])
            pieces.append(e.astype(jnp.bfloat16))
            if width < 128:
                e = jnp.concatenate([e, jnp.zeros((TILE, 128 - width), jnp.float32)], axis=1)
            part = e if part is None else part + e
        p = jnp.concatenate(pieces, axis=1)
        out = jnp.dot(p, values, preferred_element_type=jnp.float32)
        if not first:
            part = tot[rows, :] * alpha + part
        if finish is not None:
            total = jnp.sum(part, axis=1, keepdims=True)
            scale = 1.0 / total
            latent = []
            for k in range(LATENT // 128):
                cols = slice(k * 128, (k + 1) * 128)
                latent.append(((acc[rows, cols] * alpha + out[:, cols]) * scale).astype(jnp.bfloat16))
            finish(i, jnp.concatenate(latent, axis=1), new_top, total)
        else:
            top[rows, :] = new_top
            tot[rows, :] = part
            for k in range(LATENT // 128):
                cols = slice(k * 128, (k + 1) * 128)
                if first:
                    acc[rows, cols] = out[:, cols]
                else:
                    acc[rows, cols] = acc[rows, cols] * alpha + out[:, cols]
        s = later


def kernel(
    qn_ref, qr_ref, kv_ref, ka_ref, va_ref, wo_ref, out_ref,
    kv, q, acc, top, tot, ka, va, wo,
    qn, qr, tmpn, tmpr, qsend, qall, q32n, q32r,
    kvraw, ysend, yrecv, wts, ho, dsend, drecv, esend, erecv,
    local, qs_send, qs_recv, q_send, q_recv,
    up_send, up_recv, dn_send, dn_recv, sb_send, sb_recv,
    vy_send, vy_recv, vf_send, vf_recv, vx_send, vx_recv, o_send, o_recv, ox_send, ox_recv,
    y_send, y_recv, h_send, h_recv, d_send, d_recv, e_send, e_recv,
):
    prefix, z, dp = lax.axis_index("prefix"), lax.axis_index("head"), lax.axis_index("dp")
    c = lax.rem(prefix, 2)
    j_me = lax.div(prefix, 2)
    chip = dp * OWNERS + j_me
    sib = (prefix + 1 - 2 * c, z, dp)
    above = (prefix, lax.rem(z + 1, Z), dp)
    below = (prefix, lax.rem(z + Z - 1, Z), dp)

    xl, yy = lax.div(j_me, 4), lax.rem(j_me, 4)
    x = 2 * dp + xl
    quarter = 2 * xl + c

    def at(x_to, y_to, core):
        x_to, y_to = lax.rem(x_to, 4), lax.rem(y_to, 4)
        return ((lax.rem(x_to, 2) * 4 + y_to) * 2 + core, z, lax.div(x_to, 2))

    def peer(offset):
        x_to, y_to = lax.rem(x + offset[0], 4), lax.rem(yy + offset[1], 4)
        x_low, x_high = lax.rem(x_to, 2), lax.div(x_to, 2)
        index = x_low * 4 + y_to
        return x_high * OWNERS + index, (2 * index + c, z, x_high)

    def head(r):
        x_low = 1 - xl if r < 4 else xl
        return x_low * 4 + lax.rem(yy + (2, 1, 3, 0)[r % 4], 4)

    def head_of(x_low, y_of):
        return x_low * 4 + lax.rem(y_of, 4)

    def columns(quarter_of, n):
        return pl.ds(pl.multiple_of((quarter_of + 4 * n) * COLS, 128), COLS)

    def owned(n):
        return pl.ds(n * COLS, COLS)

    def remote(src, dst, ssem, rsem, to):
        return pltpu.make_async_remote_copy(
            src_ref=src, dst_ref=dst, send_sem=ssem, recv_sem=rsem, device_id=to, device_id_type=MESH
        )

    def loop(n, body):
        def step(k, carry):
            body(k)
            return carry

        lax.fori_loop(0, n, step, 0)

    def load_ka(r):
        return pltpu.make_async_copy(ka_ref.at[2 * head(r) + c], ka.at[r], local.at[r])

    load_kv = pltpu.make_async_copy(kv_ref, kvraw, local.at[8])
    load_kv.start()
    load_qn = pltpu.make_async_copy(qn_ref, qn, local.at[11])
    load_qn.start()
    load_qr = pltpu.make_async_copy(qr_ref, qr, local.at[12])
    load_qr.start()

    barrier = pltpu.get_barrier_semaphore()

    def greet(to):
        pl.semaphore_signal(barrier, inc=1, device_id=to, device_id_type=MESH)

    for offset in OFFSETS:
        greet(peer(offset)[1])
    for to in (above, below, sib):
        greet(to)

    load_kv.wait()
    for h in range(2):
        rows = slice(h * HALFB, (h + 1) * HALFB)
        kv[0, h, 0:HALFB, :] = kvraw[rows, 0:LATENT]
        rope = kvraw[rows, LATENT:WIDTH].astype(jnp.float32)
        packed = [rope[g * PACK : (g + 1) * PACK] for g in range(6)]
        packed.append(jnp.zeros((PACK, LATENT - 6 * ROPE), jnp.float32))
        kv[0, h, HALFB : HALFB + PACK, :] = jnp.concatenate(packed, axis=1).astype(jnp.bfloat16)

    pl.semaphore_wait(barrier, 3 + (PLANE - 1))

    def up(step, h):
        return remote(
            kv.at[UP[step - 1], h], kv.at[UP[step], h],
            up_send.at[step - 1, h], up_recv.at[step - 1, h], above,
        )

    def down(step, h):
        return remote(
            kv.at[DOWN[step - 1], h], kv.at[DOWN[step], h],
            dn_send.at[step - 1, h], dn_recv.at[step - 1, h], below,
        )

    def across(slot, h):
        i = SIB_ORDER.index(slot)
        return remote(kv.at[slot, h], kv.at[SIB_OF[slot], h], sb_send.at[i, h], sb_recv.at[i, h], sib)

    def tick(step, h):
        up(step, h).wait_recv()
        if step < 3 or (step == 3 and h == 0):
            up(step + 1, h).start()
        down(step, 1 - h).wait_recv()
        if step < 3 or (step == 3 and h == 0):
            down(step + 1, 1 - h).start()
        across(UP[step], h).start()
        across(DOWN[step], 1 - h).start()

    def crossed(*slots):
        for slot in slots:
            for h in range(2):
                across(slot, h).wait_recv()

    for h in range(2):
        up(1, h).start()
        down(1, 1 - h).start()
    across(0, 0).start()
    across(0, 1).start()

    load_qn.wait()
    load_qr.wait()
    tmpn[...] = qn[...].astype(jnp.float32).reshape(64, NOPE)
    tmpr[:, :ROPE] = qr[...].astype(jnp.float32).reshape(64, ROPE)
    for parity in range(2):
        qsend[parity, 0:32, :] = tmpn[pl.ds(parity, 32, stride=2), :].astype(jnp.bfloat16)
        rope = tmpr[pl.ds(parity, 32, stride=2), :][:, :ROPE]
        qsend[parity, 32:48, :] = jnp.concatenate([rope[:16], rope[16:]], axis=1).astype(
            jnp.bfloat16
        )
    q_sib = remote(qsend.at[1 - c], qall.at[chip, c], qs_send, qs_recv, sib)
    q_sib.start()
    for r in range(HEADS):
        load_ka(r).start()
    load_va = pltpu.make_async_copy(va_ref.at[0], va.at[j_me], local.at[9])
    load_va.start()
    own_rows = pl.ds(pl.multiple_of(quarter * VDIM, VDIM), VDIM)
    load_wo = [
        pltpu.make_async_copy(
            wo_ref.at[:, columns(quarter, n)], wo.at[own_rows, owned(n)], local.at[13 + n]
        )
        for n in range(2)
    ]
    for copy in load_wo:
        copy.start()

    def v_y(way):
        return remote(
            va_ref.at[0], va.at[j_me], vy_send.at[way], vy_recv.at[way], at(x, yy + 1 + 2 * way, c)
        )

    def v_relay(way):
        half = va.at[head_of(xl, yy + 3 - 2 * way), pl.ds(way * 256, 256), :]
        return remote(half, half, vf_send.at[way], vf_recv.at[way], at(x, yy + 1 + 2 * way, c))

    def v_x(i, way):
        half = va.at[head_of(xl, yy + i), pl.ds(way * 256, 256), :]
        src = va_ref.at[0, pl.ds(way * 256, 256), :] if i == 0 else half
        return remote(src, half, vx_send.at[i, way], vx_recv.at[i, way], at(x + 1 + 2 * way, yy, c))

    for way in range(2):
        v_y(way).start()
        v_x(0, way).start()

    qall[chip, c] = qsend[c]
    q_sib.wait_recv()

    def q_copy(k):
        _, to = peer(OFFSETS[k])
        return remote(qall.at[chip], qall.at[chip], q_send.at[k], q_recv.at[chip], to)

    for k in range(PLANE - 1):
        q_copy(k).start()

    wo_copies = [
        remote(
            wo_ref.at[:, columns(2 * xl + 1 - c, n)], wo.at[own_rows, owned(n)],
            o_send.at[n], o_recv.at[n], sib,
        )
        for n in range(2)
    ]
    for copy in wo_copies:
        copy.start()

    def wo_x(way, core, n):
        return remote(
            wo_ref.at[pl.ds(way * 64, 64), columns(2 * (1 - xl) + core, n)],
            wo.at[pl.ds(pl.multiple_of(quarter * VDIM + way * 64, 64), 64), owned(n)],
            ox_send.at[way, core, n], ox_recv.at[way, c, n], at(x + 1 + 2 * way, yy, core),
        )

    def wo_x_arrived(way, core, n):
        rows = pl.ds(pl.multiple_of((2 * (1 - xl) + core) * VDIM + way * 64, 64), 64)
        remote(
            wo.at[rows, owned(n)], wo.at[rows, owned(n)],
            ox_send.at[way, core, n], ox_recv.at[way, core, n], at(x + 3 - 2 * way, yy, core),
        ).wait_recv()

    tick(1, 0)
    tick(1, 1)

    for k in range(PLANE - 1):
        other, to = peer(OFFSETS[k])
        remote(qall.at[other], qall.at[other], q_send.at[k], q_recv.at[other], to).wait_recv()
    for way in range(2):
        for core in range(2):
            for n in range(2):
                wo_x(way, core, n).start()

    for g in range(2 * PLANE):
        m = qall[g // 2, g % 2]
        q32n[g * 32 : (g + 1) * 32, :] = m[0:32].astype(jnp.float32)
        r = m[32:48].astype(jnp.float32)
        q32r[g * 32 : g * 32 + 16, 0:ROPE] = r[:, :ROPE]
        q32r[g * 32 + 16 : g * 32 + 32, 0:ROPE] = r[:, ROPE:]


    for way in range(2):
        v_y(way).wait_recv()
        v_relay(way).start()
    for way in range(2):
        v_x(3, way).start()
        v_x(1, way).start()
    for r in range(HEADS):
        load_ka(r).wait()

    for r in range(HEADS):
        j = head(r)
        rows = slice(r * TOKENS, (r + 1) * TOKENS)
        nope = q32n[pl.ds(j, TOKENS, stride=HEADS), :].astype(jnp.bfloat16)
        part = jnp.dot(nope, ka[r], preferred_element_type=jnp.float32)
        q[rows, 0:LATENT] = (part * SCALE).astype(jnp.bfloat16)
        rope = q32r[pl.ds(j, TOKENS, stride=HEADS), :][:, :ROPE]
        q[rows, LATENT:WIDTH] = (rope * SCALE).astype(jnp.bfloat16)
    tick(2, 0)
    tick(2, 1)

    crossed(0)
    attend(True, (0, 1), q, kv, acc, top, tot)
    crossed(2, 3)
    attend(False, (2, 3, 4, 5), q, kv, acc, top, tot)
    for way in range(2):
        v_relay(way).wait_recv()
        v_x(2, way).start()
    attend(False, (6, 7), q, kv, acc, top, tot)
    tick(3, 0)
    tick(3, 1)
    crossed(6, 7)
    attend(False, (8, 9), q, kv, acc, top, tot)
    attend(False, (10, 11), q, kv, acc, top, tot)
    up(4, 0).wait_recv()
    across(14, 0).start()
    down(4, 1).wait_recv()
    across(14, 1).start()
    crossed(10, 11)
    attend(False, (12, 13), q, kv, acc, top, tot)
    attend(False, (14,), q, kv, acc, top, tot)
    load_va.wait()

    for i in range(4):
        for way in range(2):
            v_x(i, way).wait_recv()
    crossed(14)

    per = TILE // TOKENS
    lane = lax.broadcasted_iota(jnp.int32, (TOKENS, 128), 1)
    row = lax.broadcasted_iota(jnp.int32, (16, 128), 0)

    def y_copy(r, t):
        j = head(r)
        return remote(
            ysend.at[r, t], yrecv.at[chip], y_send.at[r, t], y_recv.at[chip], (2 * j + c, z, t)
        )

    def each_y(r, action):
        for t in range(2):
            if r < HEADS - 1:
                action(y_copy(r, t))
            else:

                @pl.when(t != dp)
                def _():
                    action(y_copy(r, t))

    def finish(i, latent, new_top, total):
        for h in range(per):
            r = i * per + h
            j = head(r)
            rows = slice(h * TOKENS, (h + 1) * TOKENS)
            y = jnp.dot(latent[rows], va[j], preferred_element_type=jnp.float32)
            y = y.astype(jnp.bfloat16)
            stats = jnp.where(lane % 2 == 0, new_top[rows], total[rows])
            stats = stats.T[0:16, :]
            high = stats.astype(jnp.bfloat16)
            left = stats - high.astype(jnp.float32)
            middle = left.astype(jnp.bfloat16)
            low = left - middle.astype(jnp.float32)
            stats = jnp.where(
                row < 2,
                high.astype(jnp.float32),
                jnp.where(row < 4, middle.astype(jnp.float32), low),
            ).astype(jnp.bfloat16)
            for t in range(2):
                ysend[r, t, 0:64, :] = y[t * 64 : (t + 1) * 64]
                ysend[r, t, 64:80, :] = stats
            each_y(r, lambda copy: copy.start())

    attend(False, (15,), q, kv, acc, top, tot, finish)
    yrecv[chip] = ysend[HEADS - 1, dp]
    for offset in OFFSETS[::-1]:
        other, to = peer(offset)
        remote(
            yrecv.at[other], yrecv.at[other], y_send.at[0, 0], y_recv.at[other], to
        ).wait_recv()

    stats = [yrecv[s, 64:80, :].astype(jnp.float32) for s in range(PLANE)]
    tops = jnp.concatenate([x[0:1] + x[2:3] + x[4:5] for x in stats], axis=0)
    sums = jnp.concatenate([x[1:2] + x[3:4] + x[5:6] for x in stats], axis=0)
    weight = sums * jnp.exp2(tops - jnp.max(tops, axis=0, keepdims=True))
    weight = weight / jnp.sum(weight, axis=0, keepdims=True)
    wts[...] = jnp.concatenate([weight, jnp.zeros((128 - PLANE, 128), jnp.float32)], axis=0).T
    w = wts[pl.ds(pl.multiple_of(dp * 64, 64), 64), :]
    merged = None
    for s in range(PLANE):
        term = yrecv[s, 0:64, :].astype(jnp.float32) * w[:, s : s + 1]
        merged = term if merged is None else merged + term
    ho[quarter] = merged.astype(jnp.bfloat16)

    def h_copy(k):
        core = 1 - c if k % 2 else c
        x_low = 1 - xl if k >= 2 else xl
        return remote(
            ho.at[quarter], ho.at[quarter], h_send.at[k - 1], h_recv.at[k - 1], at(2 * dp + x_low, yy, core)
        )

    for k in (2, 3, 1):
        h_copy(k).start()
    for n in range(2):
        load_wo[n].wait()
        wo_copies[n].wait_recv()
        for way in range(2):
            for core in range(2):
                wo_x_arrived(way, core, n)
    for k in (1, 2, 3):
        h_copy(k).wait_recv()

    heads = jnp.concatenate([ho[k] for k in range(4)], axis=1)

    def d_copy(n, k):
        other = lax.rem(yy + k, 4)
        return remote(
            dsend.at[n, other], drecv.at[n, yy], d_send.at[n, k - 1], d_recv.at[n, yy], at(x, other, c)
        )

    def d_arrived(n, k):
        other = lax.rem(yy + k, 4)
        remote(
            dsend.at[n, other], drecv.at[n, other], d_send.at[n, k - 1], d_recv.at[n, other],
            at(x, other, c),
        ).wait_recv()

    for n in range(2):
        terms = jnp.dot(
            heads, wo[:, n * COLS : (n + 1) * COLS], preferred_element_type=jnp.float32
        )
        for i in range(4):
            dsend[n, i] = jnp.concatenate(
                [terms[i * 8 : i * 8 + 8], terms[32 + i * 8 : 40 + i * 8]], axis=0
            ).astype(jnp.bfloat16)
        for k in (2, 1, 3):
            d_copy(n, k).start()

    def e_copy(n, x_low, core):
        to_z = quarter + 4 * n
        return (to_z == z) & (x_low == xl) & (core == c), remote(
            esend.at[n, x_low, core], erecv.at[z], e_send.at[n, x_low, core], e_recv.at[z],
            ((4 * x_low + yy) * 2 + core, to_z, dp),
        )

    for n in range(2):
        drecv[n, yy] = dsend[n, yy]
        for k in (1, 3, 2):
            d_arrived(n, k)
        summed = drecv[n, 0].astype(jnp.float32)
        for i in range(1, 4):
            summed = summed + drecv[n, i].astype(jnp.float32)
        for x_low in range(2):
            for core in range(2):
                start = x_low * 8 + core * 4
                pieces = [summed[start : start + 4, k * 128 : (k + 1) * 128] for k in range(7)]
                pieces.append(jnp.zeros((4, 128), jnp.float32))
                esend[n, x_low, core] = jnp.concatenate(pieces, axis=0).astype(jnp.bfloat16)
                here, copy = e_copy(n, x_low, core)

                @pl.when(jnp.logical_not(here))
                def _():
                    copy.start()

                @pl.when(here)
                def _():
                    erecv[z] = esend[n, x_low, core]

    q_sib.wait_send()
    for step in range(1, 5):
        for h in range(2):
            if step < 4 or h == 0:
                up(step, h).wait_send()
                down(step, 1 - h).wait_send()
    for slot in SIB_ORDER:
        for h in range(2):
            across(slot, h).wait_send()
    for copy in wo_copies:
        copy.wait_send()
    for k in (1, 2, 3):
        h_copy(k).wait_send()

    for k in range(PLANE - 1):
        q_copy(k).wait_send()
    for r in range(HEADS):
        each_y(r, lambda copy: copy.wait_send())
    for way in range(2):
        v_y(way).wait_send()
        v_relay(way).wait_send()
        for i in range(4):
            v_x(i, way).wait_send()
        for core in range(2):
            for n in range(2):
                wo_x(way, core, n).wait_send()

    from_x, from_core = lax.rem(lax.div(z, 2), 2), lax.rem(z, 2)

    def e_arrived(s):
        frm = ((4 * from_x + yy) * 2 + from_core, s, dp)

        @pl.when(jnp.logical_not((s == z) & (from_x == xl) & (from_core == c)))
        def _():
            remote(
                esend.at[0, 0, 0], erecv.at[s], e_send.at[0, 0, 0], e_recv.at[s], frm
            ).wait_recv()

    loop(Z, e_arrived)
    result = erecv[0].astype(jnp.float32)
    for s in range(1, Z):
        result = result + erecv[s].astype(jnp.float32)
    for k in range(7):
        out_ref[:, k * 128 : (k + 1) * 128] = result[4 * k : 4 * k + 4]

    for n in range(2):
        for k in (1, 2, 3):
            d_copy(n, k).wait_send()
        for x_low in range(2):
            for core in range(2):
                here, copy = e_copy(n, x_low, core)

                @pl.when(jnp.logical_not(here))
                def _():
                    copy.wait_send()


def body(query_nope, query_rope, latent_cache, key_absorb, value_absorb, output_proj):
    vmem = pl.BlockSpec(memory_space=pltpu.VMEM)
    hbm = pl.BlockSpec(memory_space=pl.ANY)
    bf16, f32 = jnp.bfloat16, jnp.float32
    dma = pltpu.SemaphoreType.DMA
    return pl.pallas_call(
        kernel,
        out_shape=jax.ShapeDtypeStruct((4, COLS), f32),
        in_specs=[hbm] * 6,
        out_specs=vmem,
        scratch_shapes=[
            pltpu.VMEM((16, 2, HALFB + PACK, LATENT), bf16),
            pltpu.VMEM((ROWS, WIDTH), bf16),
            pltpu.VMEM((ROWS, LATENT), f32),
            pltpu.VMEM((ROWS, 128), f32),
            pltpu.VMEM((ROWS, 128), f32),
            pltpu.VMEM((HEADS, NOPE, LATENT), bf16),
            pltpu.VMEM((HEADS, LATENT, VDIM), bf16),
            pltpu.VMEM((4 * VDIM, QUARTER), bf16),
            pltpu.VMEM((4, 16, NOPE), bf16),
            pltpu.VMEM((4, 16, ROPE), bf16),
            pltpu.VMEM((64, NOPE), f32),
            pltpu.VMEM((64, 128), f32),
            pltpu.VMEM((2, MSG, 128), bf16),
            pltpu.VMEM((PLANE, 2, MSG, 128), bf16),
            pltpu.VMEM((ROWS, NOPE), f32),
            pltpu.VMEM((ROWS, 128), f32),
            pltpu.VMEM((BLOCK, WIDTH), bf16),
            pltpu.VMEM((HEADS, 2, 80, VDIM), bf16),
            pltpu.VMEM((PLANE, 80, VDIM), bf16),
            pltpu.VMEM((128, 128), f32),
            pltpu.VMEM((4, 64, VDIM), bf16),
            pltpu.VMEM((2, 4, 16, COLS), bf16),
            pltpu.VMEM((2, 4, 16, COLS), bf16),
            pltpu.VMEM((2, 2, 2, 32, 128), bf16),
            pltpu.VMEM((Z, 32, 128), bf16),
            dma((15,)),
            dma, dma, dma((PLANE - 1,)), dma((PLANE,)),
            dma((4, 2)), dma((4, 2)), dma((4, 2)), dma((4, 2)), dma((8, 2)), dma((8, 2)),
            dma((2,)), dma((2,)), dma((2,)), dma((2,)), dma((4, 2)), dma((4, 2)),
            dma((2,)), dma((2,)), dma((2, 2, 2)), dma((2, 2, 2)),
            dma((HEADS, 2)), dma((PLANE,)),
            dma((3,)), dma((3,)), dma((2, 3)), dma((2, 4)), dma((2, 2, 2)), dma((Z,)),
        ],
        compiler_params=pltpu.CompilerParams(
            collective_id=0, has_side_effects=True, vmem_limit_bytes=127 * 512 * 1024
        ),
        cost_estimate=pl.CostEstimate(
            flops=7_000_000_000, bytes_accessed=10_000_000, transcendentals=3_145_728
        ),
        name="latent_attention",
    )(query_nope, query_rope, latent_cache, key_absorb, value_absorb, output_proj)


def solution(mesh):
    in_specs = (
        P(("dp", "prefix"), "head", None),
        P(("dp", "prefix"), "head", None),
        P(("prefix", "head", "dp"), None),
        P("head", None, None),
        P(("head", "prefix"), None, None),
        P(("head", "prefix"), None),
    )
    out_specs = P(("dp", "prefix"), "head")
    return jax.shard_map(body, mesh=mesh, in_specs=in_specs, out_specs=out_specs, check_vma=False)
```

```python
import math

import jax
import jax.numpy as jnp
from jax import lax
from jax.experimental import pallas as pl
from jax.experimental.pallas import tpu as pltpu
from jax.sharding import PartitionSpec as P

MESH = pl.DeviceIdType.MESH

D = 7168
NOPE, ROPE, VDIM, LATENT = 128, 64, 128, 512
WIDTH = LATENT + ROPE
TOKENS = 128
Z = 8
PLANE = 16
OWNERS = 8
HEADS = 8
ROWS = HEADS * TOKENS
BLOCK = 192
MSG = 48
QUARTER = D // 4
COLS = D // Z
SCALE = (NOPE + ROPE) ** -0.5 * math.log2(math.e)

HALFB = BLOCK // 2
PACK = 16
UP = (0, 2, 6, 10, 14)
DOWN = (0, 3, 7, 11, 14)
SIB_OF = {0: 1, 2: 4, 3: 5, 6: 8, 7: 9, 10: 12, 11: 13, 14: 15}
SIB_ORDER = (0, 2, 3, 6, 7, 10, 11, 14)
TILE = 512
OFFSETS = sorted(
    [(dx, dy) for dx in range(4) for dy in range(4) if dx or dy],
    key=lambda o: -(min(o[0], 4 - o[0]) + min(o[1], 4 - o[1])),
)


def chunk_keys(kv, blocks):
    latent, rope = [], []
    for b in blocks:
        for h in range(2):
            latent.append(kv[b, h, 0:HALFB, :])
            packed = kv[b, h, HALFB : HALFB + PACK, 0 : 6 * ROPE]
            for g in range(6):
                rope.append(packed[:, g * ROPE : (g + 1) * ROPE])
    latent = jnp.concatenate(latent, axis=0)
    return jnp.concatenate([latent, jnp.concatenate(rope, axis=0)], axis=1), latent


def attend(first, blocks, q, kv, acc, top, tot, finish=None):
    keys, values = chunk_keys(kv, blocks)
    n = ROWS // TILE

    def at(i):
        return pl.ds(i * TILE, TILE)

    def score(i):
        return lax.dot_general(
            q[at(i), :], keys, (((1,), (1,)), ((), ())), preferred_element_type=jnp.float32
        )

    s = score(0)
    for i in range(n):
        later = score(i + 1) if i + 1 < n else None
        rows = at(i)
        high = jnp.max(s, axis=1, keepdims=True)
        if first:
            new_top = jnp.broadcast_to(high, (TILE, 128))
        else:
            old_top = top[rows, :]
            new_top = jnp.maximum(old_top, high)
            alpha = jnp.exp2(old_top - new_top)
        part = None
        pieces = []
        for k in range(0, s.shape[1], 128):
            width = min(128, s.shape[1] - k)
            e = jnp.exp2(s[:, k : k + width] - new_top[:, :width])
            pieces.append(e.astype(jnp.bfloat16))
            if width < 128:
                e = jnp.concatenate([e, jnp.zeros((TILE, 128 - width), jnp.float32)], axis=1)
            part = e if part is None else part + e
        p = jnp.concatenate(pieces, axis=1)
        out = jnp.dot(p, values, preferred_element_type=jnp.float32)
        if not first:
            part = tot[rows, :] * alpha + part
        if finish is not None:
            total = jnp.sum(part, axis=1, keepdims=True)
            scale = 1.0 / total
            latent = []
            for k in range(LATENT // 128):
                cols = slice(k * 128, (k + 1) * 128)
                latent.append(((acc[rows, cols] * alpha + out[:, cols]) * scale).astype(jnp.bfloat16))
            finish(i, jnp.concatenate(latent, axis=1), new_top, total)
        else:
            top[rows, :] = new_top
            tot[rows, :] = part
            for k in range(LATENT // 128):
                cols = slice(k * 128, (k + 1) * 128)
                if first:
                    acc[rows, cols] = out[:, cols]
                else:
                    acc[rows, cols] = acc[rows, cols] * alpha + out[:, cols]
        s = later


def kernel(
    qn_ref, qr_ref, kv_ref, ka_ref, va_ref, wo_ref, out_ref,
    kv, q, acc, top, tot, ka, va, wo,
    qn, qr, tmpn, tmpr, qsend, qall, q32n, q32r,
    kvraw, ysend, yrecv, wts, ho, dsend, drecv, esend, erecv,
    local, qs_send, qs_recv, q_send, q_recv,
    up_send, up_recv, dn_send, dn_recv, sb_send, sb_recv,
    vy_send, vy_recv, vf_send, vf_recv, vx_send, vx_recv, o_send, o_recv, ox_send, ox_recv,
    y_send, y_recv, h_send, h_recv, d_send, d_recv, e_send, e_recv,
):
    prefix, z, dp = lax.axis_index("prefix"), lax.axis_index("head"), lax.axis_index("dp")
    c = lax.rem(prefix, 2)
    j_me = lax.div(prefix, 2)
    chip = dp * OWNERS + j_me
    sib = (prefix + 1 - 2 * c, z, dp)
    above = (prefix, lax.rem(z + 1, Z), dp)
    below = (prefix, lax.rem(z + Z - 1, Z), dp)

    xl, yy = lax.div(j_me, 4), lax.rem(j_me, 4)
    x = 2 * dp + xl
    quarter = 2 * xl + c

    def at(x_to, y_to, core):
        x_to, y_to = lax.rem(x_to, 4), lax.rem(y_to, 4)
        return ((lax.rem(x_to, 2) * 4 + y_to) * 2 + core, z, lax.div(x_to, 2))

    def peer(offset):
        x_to, y_to = lax.rem(x + offset[0], 4), lax.rem(yy + offset[1], 4)
        x_low, x_high = lax.rem(x_to, 2), lax.div(x_to, 2)
        index = x_low * 4 + y_to
        return x_high * OWNERS + index, (2 * index + c, z, x_high)

    def head(r):
        x_low = 1 - xl if r < 4 else xl
        return x_low * 4 + lax.rem(yy + (2, 1, 3, 0)[r % 4], 4)

    def head_of(x_low, y_of):
        return x_low * 4 + lax.rem(y_of, 4)

    def columns(quarter_of, n):
        return pl.ds(pl.multiple_of((quarter_of + 4 * n) * COLS, 128), COLS)

    def owned(n):
        return pl.ds(n * COLS, COLS)

    def remote(src, dst, ssem, rsem, to):
        return pltpu.make_async_remote_copy(
            src_ref=src, dst_ref=dst, send_sem=ssem, recv_sem=rsem, device_id=to, device_id_type=MESH
        )

    def loop(n, body):
        def step(k, carry):
            body(k)
            return carry

        lax.fori_loop(0, n, step, 0)

    def load_ka(r):
        return pltpu.make_async_copy(ka_ref.at[2 * head(r) + c], ka.at[r], local.at[r])

    load_kv = pltpu.make_async_copy(kv_ref, kvraw, local.at[8])
    load_kv.start()
    load_qn = pltpu.make_async_copy(qn_ref, qn, local.at[11])
    load_qn.start()
    load_qr = pltpu.make_async_copy(qr_ref, qr, local.at[12])
    load_qr.start()

    barrier = pltpu.get_barrier_semaphore()

    def greet(to):
        pl.semaphore_signal(barrier, inc=1, device_id=to, device_id_type=MESH)

    for offset in OFFSETS:
        greet(peer(offset)[1])
    for to in (above, below, sib):
        greet(to)

    load_kv.wait()
    for h in range(2):
        rows = slice(h * HALFB, (h + 1) * HALFB)
        kv[0, h, 0:HALFB, :] = kvraw[rows, 0:LATENT]
        rope = kvraw[rows, LATENT:WIDTH].astype(jnp.float32)
        packed = [rope[g * PACK : (g + 1) * PACK] for g in range(6)]
        packed.append(jnp.zeros((PACK, LATENT - 6 * ROPE), jnp.float32))
        kv[0, h, HALFB : HALFB + PACK, :] = jnp.concatenate(packed, axis=1).astype(jnp.bfloat16)

    pl.semaphore_wait(barrier, 3 + (PLANE - 1))

    def up(step, h):
        return remote(
            kv.at[UP[step - 1], h], kv.at[UP[step], h],
            up_send.at[step - 1, h], up_recv.at[step - 1, h], above,
        )

    def down(step, h):
        return remote(
            kv.at[DOWN[step - 1], h], kv.at[DOWN[step], h],
            dn_send.at[step - 1, h], dn_recv.at[step - 1, h], below,
        )

    def across(slot, h):
        i = SIB_ORDER.index(slot)
        return remote(kv.at[slot, h], kv.at[SIB_OF[slot], h], sb_send.at[i, h], sb_recv.at[i, h], sib)

    def tick(step, h):
        up(step, h).wait_recv()
        if step < 3 or (step == 3 and h == 0):
            up(step + 1, h).start()
        down(step, 1 - h).wait_recv()
        if step < 3 or (step == 3 and h == 0):
            down(step + 1, 1 - h).start()
        across(UP[step], h).start()
        across(DOWN[step], 1 - h).start()

    def crossed(*slots):
        for slot in slots:
            for h in range(2):
                across(slot, h).wait_recv()

    for h in range(2):
        up(1, h).start()
        down(1, 1 - h).start()
    across(0, 0).start()
    across(0, 1).start()

    load_qn.wait()
    load_qr.wait()
    tmpn[...] = qn[...].astype(jnp.float32).reshape(64, NOPE)
    tmpr[:, :ROPE] = qr[...].astype(jnp.float32).reshape(64, ROPE)
    for parity in range(2):
        qsend[parity, 0:32, :] = tmpn[pl.ds(parity, 32, stride=2), :].astype(jnp.bfloat16)
        rope = tmpr[pl.ds(parity, 32, stride=2), :][:, :ROPE]
        qsend[parity, 32:48, :] = jnp.concatenate([rope[:16], rope[16:]], axis=1).astype(
            jnp.bfloat16
        )
    q_sib = remote(qsend.at[1 - c], qall.at[chip, c], qs_send, qs_recv, sib)
    q_sib.start()
    for r in range(HEADS):
        load_ka(r).start()
    load_va = pltpu.make_async_copy(va_ref.at[0], va.at[j_me], local.at[9])
    load_va.start()
    own_rows = pl.ds(pl.multiple_of(quarter * VDIM, VDIM), VDIM)
    load_wo = [
        pltpu.make_async_copy(
            wo_ref.at[:, columns(quarter, n)], wo.at[own_rows, owned(n)], local.at[13 + n]
        )
        for n in range(2)
    ]
    for copy in load_wo:
        copy.start()

    def v_y(way):
        return remote(
            va_ref.at[0], va.at[j_me], vy_send.at[way], vy_recv.at[way], at(x, yy + 1 + 2 * way, c)
        )

    def v_relay(way):
        half = va.at[head_of(xl, yy + 3 - 2 * way), pl.ds(way * 256, 256), :]
        return remote(half, half, vf_send.at[way], vf_recv.at[way], at(x, yy + 1 + 2 * way, c))

    def v_x(i, way):
        half = va.at[head_of(xl, yy + i), pl.ds(way * 256, 256), :]
        src = va_ref.at[0, pl.ds(way * 256, 256), :] if i == 0 else half
        return remote(src, half, vx_send.at[i, way], vx_recv.at[i, way], at(x + 1 + 2 * way, yy, c))

    qall[chip, c] = qsend[c]
    q_sib.wait_recv()

    def q_copy(k):
        _, to = peer(OFFSETS[k])
        return remote(qall.at[chip], qall.at[chip], q_send.at[k], q_recv.at[chip], to)

    for k in range(PLANE - 1):
        q_copy(k).start()

    for way in range(2):
        v_y(way).start()
        v_x(0, way).start()

    wo_copies = [
        remote(
            wo_ref.at[:, columns(2 * xl + 1 - c, n)], wo.at[own_rows, owned(n)],
            o_send.at[n], o_recv.at[n], sib,
        )
        for n in range(2)
    ]
    for copy in wo_copies:
        copy.start()

    def wo_x(way, core, n):
        return remote(
            wo_ref.at[pl.ds(way * 64, 64), columns(2 * (1 - xl) + core, n)],
            wo.at[pl.ds(pl.multiple_of(quarter * VDIM + way * 64, 64), 64), owned(n)],
            ox_send.at[way, core, n], ox_recv.at[way, c, n], at(x + 1 + 2 * way, yy, core),
        )

    def wo_x_arrived(way, core, n):
        rows = pl.ds(pl.multiple_of((2 * (1 - xl) + core) * VDIM + way * 64, 64), 64)
        remote(
            wo.at[rows, owned(n)], wo.at[rows, owned(n)],
            ox_send.at[way, core, n], ox_recv.at[way, core, n], at(x + 3 - 2 * way, yy, core),
        ).wait_recv()

    tick(1, 0)
    tick(1, 1)

    for k in range(PLANE - 1):
        other, to = peer(OFFSETS[k])
        remote(qall.at[other], qall.at[other], q_send.at[k], q_recv.at[other], to).wait_recv()
    for way in range(2):
        for core in range(2):
            for n in range(2):
                wo_x(way, core, n).start()

    for g in range(2 * PLANE):
        m = qall[g // 2, g % 2]
        q32n[g * 32 : (g + 1) * 32, :] = m[0:32].astype(jnp.float32)
        r = m[32:48].astype(jnp.float32)
        q32r[g * 32 : g * 32 + 16, 0:ROPE] = r[:, :ROPE]
        q32r[g * 32 + 16 : g * 32 + 32, 0:ROPE] = r[:, ROPE:]


    for r in range(HEADS):
        load_ka(r).wait()

    for r in range(HEADS):
        j = head(r)
        rows = slice(r * TOKENS, (r + 1) * TOKENS)
        nope = q32n[pl.ds(j, TOKENS, stride=HEADS), :].astype(jnp.bfloat16)
        part = jnp.dot(nope, ka[r], preferred_element_type=jnp.float32)
        q[rows, 0:LATENT] = (part * SCALE).astype(jnp.bfloat16)
        rope = q32r[pl.ds(j, TOKENS, stride=HEADS), :][:, :ROPE]
        q[rows, LATENT:WIDTH] = (rope * SCALE).astype(jnp.bfloat16)
    for way in range(2):
        v_y(way).wait_recv()
        v_relay(way).start()
    for way in range(2):
        v_x(3, way).start()
        v_x(1, way).start()
    tick(2, 0)
    tick(2, 1)

    crossed(0)
    attend(True, (0, 1), q, kv, acc, top, tot)
    for way in range(2):
        v_relay(way).wait_recv()
        v_x(2, way).start()
    crossed(2, 3)
    attend(False, (2, 3, 4, 5), q, kv, acc, top, tot)
    tick(3, 0)
    tick(3, 1)
    crossed(6, 7)
    attend(False, (6, 7, 8, 9), q, kv, acc, top, tot)
    crossed(10, 11)
    attend(False, (10, 11, 12, 13), q, kv, acc, top, tot)
    up(4, 0).wait_recv()
    across(14, 0).start()
    down(4, 1).wait_recv()
    across(14, 1).start()

    attend(False, (14,), q, kv, acc, top, tot)
    load_va.wait()

    for i in range(4):
        for way in range(2):
            v_x(i, way).wait_recv()
    crossed(14)

    per = TILE // TOKENS
    lane = lax.broadcasted_iota(jnp.int32, (TOKENS, 128), 1)
    row = lax.broadcasted_iota(jnp.int32, (16, 128), 0)

    def y_copy(r, t):
        j = head(r)
        return remote(
            ysend.at[r, t], yrecv.at[chip], y_send.at[r, t], y_recv.at[chip], (2 * j + c, z, t)
        )

    def each_y(r, action):
        for t in range(2):
            if r < HEADS - 1:
                action(y_copy(r, t))
            else:

                @pl.when(t != dp)
                def _():
                    action(y_copy(r, t))

    def finish(i, latent, new_top, total):
        for h in range(per):
            r = i * per + h
            j = head(r)
            rows = slice(h * TOKENS, (h + 1) * TOKENS)
            y = jnp.dot(latent[rows], va[j], preferred_element_type=jnp.float32)
            y = y.astype(jnp.bfloat16)
            stats = jnp.where(lane % 2 == 0, new_top[rows], total[rows])
            stats = stats.T[0:16, :]
            high = stats.astype(jnp.bfloat16)
            left = stats - high.astype(jnp.float32)
            middle = left.astype(jnp.bfloat16)
            low = left - middle.astype(jnp.float32)
            stats = jnp.where(
                row < 2,
                high.astype(jnp.float32),
                jnp.where(row < 4, middle.astype(jnp.float32), low),
            ).astype(jnp.bfloat16)
            for t in range(2):
                ysend[r, t, 0:64, :] = y[t * 64 : (t + 1) * 64]
                ysend[r, t, 64:80, :] = stats
            each_y(r, lambda copy: copy.start())

    attend(False, (15,), q, kv, acc, top, tot, finish)
    yrecv[chip] = ysend[HEADS - 1, dp]
    for offset in OFFSETS[::-1]:
        other, to = peer(offset)
        remote(
            yrecv.at[other], yrecv.at[other], y_send.at[0, 0], y_recv.at[other], to
        ).wait_recv()

    stats = [yrecv[s, 64:80, :].astype(jnp.float32) for s in range(PLANE)]
    tops = jnp.concatenate([x[0:1] + x[2:3] + x[4:5] for x in stats], axis=0)
    sums = jnp.concatenate([x[1:2] + x[3:4] + x[5:6] for x in stats], axis=0)
    weight = sums * jnp.exp2(tops - jnp.max(tops, axis=0, keepdims=True))
    weight = weight / jnp.sum(weight, axis=0, keepdims=True)
    wts[...] = jnp.concatenate([weight, jnp.zeros((128 - PLANE, 128), jnp.float32)], axis=0).T
    w = wts[pl.ds(pl.multiple_of(dp * 64, 64), 64), :]
    merged = None
    for s in range(PLANE):
        term = yrecv[s, 0:64, :].astype(jnp.float32) * w[:, s : s + 1]
        merged = term if merged is None else merged + term
    ho[quarter] = merged.astype(jnp.bfloat16)

    def h_copy(k):
        core = 1 - c if k % 2 else c
        x_low = 1 - xl if k >= 2 else xl
        return remote(
            ho.at[quarter], ho.at[quarter], h_send.at[k - 1], h_recv.at[k - 1], at(2 * dp + x_low, yy, core)
        )

    for k in (2, 3, 1):
        h_copy(k).start()
    for n in range(2):
        load_wo[n].wait()
        wo_copies[n].wait_recv()
    h_copy(1).wait_recv()

    def project(x_low, n):
        heads = jnp.concatenate([ho[2 * x_low], ho[2 * x_low + 1]], axis=1)
        rows = pl.ds(pl.multiple_of(x_low * 2 * VDIM, 2 * VDIM), 2 * VDIM)
        return jnp.dot(heads, wo[rows, owned(n)], preferred_element_type=jnp.float32)

    own_terms = [project(xl, n) for n in range(2)]
    for n in range(2):
        for way in range(2):
            for core in range(2):
                wo_x_arrived(way, core, n)
    for k in (2, 3):
        h_copy(k).wait_recv()

    def d_copy(n, k):
        other = lax.rem(yy + k, 4)
        return remote(
            dsend.at[n, other], drecv.at[n, yy], d_send.at[n, k - 1], d_recv.at[n, yy], at(x, other, c)
        )

    def d_arrived(n, k):
        other = lax.rem(yy + k, 4)
        remote(
            dsend.at[n, other], drecv.at[n, other], d_send.at[n, k - 1], d_recv.at[n, other],
            at(x, other, c),
        ).wait_recv()

    for n in range(2):
        terms = own_terms[n] + project(1 - xl, n)
        for i in range(4):
            dsend[n, i] = jnp.concatenate(
                [terms[i * 8 : i * 8 + 8], terms[32 + i * 8 : 40 + i * 8]], axis=0
            ).astype(jnp.bfloat16)
        for k in (2, 1, 3):
            d_copy(n, k).start()

    def e_copy(n, x_low, core):
        to_z = quarter + 4 * n
        return (to_z == z) & (x_low == xl) & (core == c), remote(
            esend.at[n, x_low, core], erecv.at[z], e_send.at[n, x_low, core], e_recv.at[z],
            ((4 * x_low + yy) * 2 + core, to_z, dp),
        )

    for n in range(2):
        drecv[n, yy] = dsend[n, yy]
        for k in (1, 3, 2):
            d_arrived(n, k)
        summed = drecv[n, 0].astype(jnp.float32)
        for i in range(1, 4):
            summed = summed + drecv[n, i].astype(jnp.float32)
        for x_low in range(2):
            for core in range(2):
                start = x_low * 8 + core * 4
                pieces = [summed[start : start + 4, k * 128 : (k + 1) * 128] for k in range(7)]
                pieces.append(jnp.zeros((4, 128), jnp.float32))
                esend[n, x_low, core] = jnp.concatenate(pieces, axis=0).astype(jnp.bfloat16)
                here, copy = e_copy(n, x_low, core)

                @pl.when(jnp.logical_not(here))
                def _():
                    copy.start()

                @pl.when(here)
                def _():
                    erecv[z] = esend[n, x_low, core]

    q_sib.wait_send()
    for step in range(1, 5):
        for h in range(2):
            if step < 4 or h == 0:
                up(step, h).wait_send()
                down(step, 1 - h).wait_send()
    for slot in SIB_ORDER:
        for h in range(2):
            across(slot, h).wait_send()
    for copy in wo_copies:
        copy.wait_send()
    for k in (1, 2, 3):
        h_copy(k).wait_send()

    for k in range(PLANE - 1):
        q_copy(k).wait_send()
    for r in range(HEADS):
        each_y(r, lambda copy: copy.wait_send())
    for way in range(2):
        v_y(way).wait_send()
        v_relay(way).wait_send()
        for i in range(4):
            v_x(i, way).wait_send()
        for core in range(2):
            for n in range(2):
                wo_x(way, core, n).wait_send()

    from_x, from_core = lax.rem(lax.div(z, 2), 2), lax.rem(z, 2)

    def e_arrived(s):
        frm = ((4 * from_x + yy) * 2 + from_core, s, dp)

        @pl.when(jnp.logical_not((s == z) & (from_x == xl) & (from_core == c)))
        def _():
            remote(
                esend.at[0, 0, 0], erecv.at[s], e_send.at[0, 0, 0], e_recv.at[s], frm
            ).wait_recv()

    loop(Z, e_arrived)
    result = erecv[0].astype(jnp.float32)
    for s in range(1, Z):
        result = result + erecv[s].astype(jnp.float32)
    for k in range(7):
        out_ref[:, k * 128 : (k + 1) * 128] = result[4 * k : 4 * k + 4]

    for n in range(2):
        for k in (1, 2, 3):
            d_copy(n, k).wait_send()
        for x_low in range(2):
            for core in range(2):
                here, copy = e_copy(n, x_low, core)

                @pl.when(jnp.logical_not(here))
                def _():
                    copy.wait_send()


def body(query_nope, query_rope, latent_cache, key_absorb, value_absorb, output_proj):
    vmem = pl.BlockSpec(memory_space=pltpu.VMEM)
    hbm = pl.BlockSpec(memory_space=pl.ANY)
    bf16, f32 = jnp.bfloat16, jnp.float32
    dma = pltpu.SemaphoreType.DMA
    return pl.pallas_call(
        kernel,
        out_shape=jax.ShapeDtypeStruct((4, COLS), f32),
        in_specs=[hbm] * 6,
        out_specs=vmem,
        scratch_shapes=[
            pltpu.VMEM((16, 2, HALFB + PACK, LATENT), bf16),
            pltpu.VMEM((ROWS, WIDTH), bf16),
            pltpu.VMEM((ROWS, LATENT), f32),
            pltpu.VMEM((ROWS, 128), f32),
            pltpu.VMEM((ROWS, 128), f32),
            pltpu.VMEM((HEADS, NOPE, LATENT), bf16),
            pltpu.VMEM((HEADS, LATENT, VDIM), bf16),
            pltpu.VMEM((4 * VDIM, QUARTER), bf16),
            pltpu.VMEM((4, 16, NOPE), bf16),
            pltpu.VMEM((4, 16, ROPE), bf16),
            pltpu.VMEM((64, NOPE), f32),
            pltpu.VMEM((64, 128), f32),
            pltpu.VMEM((2, MSG, 128), bf16),
            pltpu.VMEM((PLANE, 2, MSG, 128), bf16),
            pltpu.VMEM((ROWS, NOPE), f32),
            pltpu.VMEM((ROWS, 128), f32),
            pltpu.VMEM((BLOCK, WIDTH), bf16),
            pltpu.VMEM((HEADS, 2, 80, VDIM), bf16),
            pltpu.VMEM((PLANE, 80, VDIM), bf16),
            pltpu.VMEM((128, 128), f32),
            pltpu.VMEM((4, 64, VDIM), bf16),
            pltpu.VMEM((2, 4, 16, COLS), bf16),
            pltpu.VMEM((2, 4, 16, COLS), bf16),
            pltpu.VMEM((2, 2, 2, 32, 128), bf16),
            pltpu.VMEM((Z, 32, 128), bf16),
            dma((15,)),
            dma, dma, dma((PLANE - 1,)), dma((PLANE,)),
            dma((4, 2)), dma((4, 2)), dma((4, 2)), dma((4, 2)), dma((8, 2)), dma((8, 2)),
            dma((2,)), dma((2,)), dma((2,)), dma((2,)), dma((4, 2)), dma((4, 2)),
            dma((2,)), dma((2,)), dma((2, 2, 2)), dma((2, 2, 2)),
            dma((HEADS, 2)), dma((PLANE,)),
            dma((3,)), dma((3,)), dma((2, 3)), dma((2, 4)), dma((2, 2, 2)), dma((Z,)),
        ],
        compiler_params=pltpu.CompilerParams(
            collective_id=0, has_side_effects=True, vmem_limit_bytes=127 * 512 * 1024
        ),
        cost_estimate=pl.CostEstimate(
            flops=7_000_000_000, bytes_accessed=10_000_000, transcendentals=3_145_728
        ),
        name="latent_attention",
    )(query_nope, query_rope, latent_cache, key_absorb, value_absorb, output_proj)


def solution(mesh):
    in_specs = (
        P(("dp", "prefix"), "head", None),
        P(("dp", "prefix"), "head", None),
        P(("prefix", "head", "dp"), None),
        P("head", None, None),
        P(("head", "prefix"), None, None),
        P(("head", "prefix"), None),
    )
    out_specs = P(("dp", "prefix"), "head")
    return jax.shard_map(body, mesh=mesh, in_specs=in_specs, out_specs=out_specs, check_vma=False)
```

```python
import math

import jax
import jax.numpy as jnp
from jax import lax
from jax.experimental import pallas as pl
from jax.experimental.pallas import tpu as pltpu
from jax.sharding import PartitionSpec as P

MESH = pl.DeviceIdType.MESH

D = 7168
NOPE, ROPE, VDIM, LATENT = 128, 64, 128, 512
WIDTH = LATENT + ROPE
TOKENS = 128
Z = 8
PLANE = 16
OWNERS = 8
HEADS = 8
ROWS = HEADS * TOKENS
BLOCK = 192
MSG = 48
QUARTER = D // 4
COLS = D // Z
SCALE = (NOPE + ROPE) ** -0.5 * math.log2(math.e)

HALFB = BLOCK // 2
PACK = 16
UP = (0, 2, 6, 10, 14)
DOWN = (0, 3, 7, 11, 14)
SIB_OF = {0: 1, 2: 4, 3: 5, 6: 8, 7: 9, 10: 12, 11: 13, 14: 15}
SIB_ORDER = (0, 2, 3, 6, 7, 10, 11, 14)
TILE = 512
OFFSETS = sorted(
    [(dx, dy) for dx in range(4) for dy in range(4) if dx or dy],
    key=lambda o: -(min(o[0], 4 - o[0]) + min(o[1], 4 - o[1])),
)


def chunk_keys(kv, blocks):
    latent, rope = [], []
    for b in blocks:
        for h in range(2):
            latent.append(kv[b, h, 0:HALFB, :])
            packed = kv[b, h, HALFB : HALFB + PACK, 0 : 6 * ROPE]
            for g in range(6):
                rope.append(packed[:, g * ROPE : (g + 1) * ROPE])
    latent = jnp.concatenate(latent, axis=0)
    return jnp.concatenate([latent, jnp.concatenate(rope, axis=0)], axis=1), latent


def attend(first, blocks, q, kv, acc, top, tot, finish=None):
    keys, values = chunk_keys(kv, blocks)
    n = ROWS // TILE

    def at(i):
        return pl.ds(i * TILE, TILE)

    def score(i):
        return lax.dot_general(
            q[at(i), :], keys, (((1,), (1,)), ((), ())), preferred_element_type=jnp.float32
        )

    s = score(0)
    for i in range(n):
        later = score(i + 1) if i + 1 < n else None
        rows = at(i)
        high = jnp.max(s, axis=1, keepdims=True)
        if first:
            new_top = jnp.broadcast_to(high, (TILE, 128))
        else:
            old_top = top[rows, :]
            new_top = jnp.maximum(old_top, high)
            alpha = jnp.exp2(old_top - new_top)
        part = None
        pieces = []
        for k in range(0, s.shape[1], 128):
            width = min(128, s.shape[1] - k)
            e = jnp.exp2(s[:, k : k + width] - new_top[:, :width])
            pieces.append(e.astype(jnp.bfloat16))
            if width < 128:
                e = jnp.concatenate([e, jnp.zeros((TILE, 128 - width), jnp.float32)], axis=1)
            part = e if part is None else part + e
        p = jnp.concatenate(pieces, axis=1)
        out = jnp.dot(p, values, preferred_element_type=jnp.float32)
        if not first:
            part = tot[rows, :] * alpha + part
        if finish is not None:
            total = jnp.sum(part, axis=1, keepdims=True)
            scale = 1.0 / total
            latent = []
            for k in range(LATENT // 128):
                cols = slice(k * 128, (k + 1) * 128)
                latent.append(((acc[rows, cols] * alpha + out[:, cols]) * scale).astype(jnp.bfloat16))
            finish(i, jnp.concatenate(latent, axis=1), new_top, total)
        else:
            top[rows, :] = new_top
            tot[rows, :] = part
            for k in range(LATENT // 128):
                cols = slice(k * 128, (k + 1) * 128)
                if first:
                    acc[rows, cols] = out[:, cols]
                else:
                    acc[rows, cols] = acc[rows, cols] * alpha + out[:, cols]
        s = later


def kernel(
    qn_ref, qr_ref, kv_ref, ka_ref, va_ref, wo_ref, out_ref,
    kv, q, acc, top, tot, ka, va, wo,
    qn, qr, tmpn, tmpr, qsend, qall, q32n, q32r,
    kvraw, ysend, yrecv, wts, ho, dsend, drecv, esend, erecv,
    local, qs_send, qs_recv, q_send, q_recv,
    up_send, up_recv, dn_send, dn_recv, sb_send, sb_recv,
    vy_send, vy_recv, vf_send, vf_recv, vx_send, vx_recv, o_send, o_recv, ox_send, ox_recv,
    y_send, y_recv, h_send, h_recv, d_send, d_recv, e_send, e_recv,
):
    prefix, z, dp = lax.axis_index("prefix"), lax.axis_index("head"), lax.axis_index("dp")
    c = lax.rem(prefix, 2)
    j_me = lax.div(prefix, 2)
    chip = dp * OWNERS + j_me
    sib = (prefix + 1 - 2 * c, z, dp)
    above = (prefix, lax.rem(z + 1, Z), dp)
    below = (prefix, lax.rem(z + Z - 1, Z), dp)

    xl, yy = lax.div(j_me, 4), lax.rem(j_me, 4)
    x = 2 * dp + xl
    quarter = 2 * xl + c

    def at(x_to, y_to, core):
        x_to, y_to = lax.rem(x_to, 4), lax.rem(y_to, 4)
        return ((lax.rem(x_to, 2) * 4 + y_to) * 2 + core, z, lax.div(x_to, 2))

    def peer(offset):
        x_to, y_to = lax.rem(x + offset[0], 4), lax.rem(yy + offset[1], 4)
        x_low, x_high = lax.rem(x_to, 2), lax.div(x_to, 2)
        index = x_low * 4 + y_to
        return x_high * OWNERS + index, (2 * index + c, z, x_high)

    def head(r):
        x_low = 1 - xl if r < 4 else xl
        return x_low * 4 + lax.rem(yy + (2, 1, 3, 0)[r % 4], 4)

    def head_of(x_low, y_of):
        return x_low * 4 + lax.rem(y_of, 4)

    def columns(quarter_of, n):
        return pl.ds(pl.multiple_of((quarter_of + 4 * n) * COLS, 128), COLS)

    def owned(n):
        return pl.ds(n * COLS, COLS)

    def remote(src, dst, ssem, rsem, to):
        return pltpu.make_async_remote_copy(
            src_ref=src, dst_ref=dst, send_sem=ssem, recv_sem=rsem, device_id=to, device_id_type=MESH
        )

    def loop(n, body):
        def step(k, carry):
            body(k)
            return carry

        lax.fori_loop(0, n, step, 0)

    def load_ka(r):
        return pltpu.make_async_copy(ka_ref.at[2 * head(r) + c], ka.at[r], local.at[r])

    load_kv = pltpu.make_async_copy(kv_ref, kvraw, local.at[8])
    load_kv.start()
    load_qn = pltpu.make_async_copy(qn_ref, qn, local.at[11])
    load_qn.start()
    load_qr = pltpu.make_async_copy(qr_ref, qr, local.at[12])
    load_qr.start()

    barrier = pltpu.get_barrier_semaphore()

    def greet(to):
        pl.semaphore_signal(barrier, inc=1, device_id=to, device_id_type=MESH)

    for offset in OFFSETS:
        greet(peer(offset)[1])
    for to in (above, below, sib):
        greet(to)

    load_kv.wait()
    for h in range(2):
        rows = slice(h * HALFB, (h + 1) * HALFB)
        kv[0, h, 0:HALFB, :] = kvraw[rows, 0:LATENT]
        rope = kvraw[rows, LATENT:WIDTH].astype(jnp.float32)
        packed = [rope[g * PACK : (g + 1) * PACK] for g in range(6)]
        packed.append(jnp.zeros((PACK, LATENT - 6 * ROPE), jnp.float32))
        kv[0, h, HALFB : HALFB + PACK, :] = jnp.concatenate(packed, axis=1).astype(jnp.bfloat16)

    pl.semaphore_wait(barrier, 3 + (PLANE - 1))

    def up(step, h):
        return remote(
            kv.at[UP[step - 1], h], kv.at[UP[step], h],
            up_send.at[step - 1, h], up_recv.at[step - 1, h], above,
        )

    def down(step, h):
        return remote(
            kv.at[DOWN[step - 1], h], kv.at[DOWN[step], h],
            dn_send.at[step - 1, h], dn_recv.at[step - 1, h], below,
        )

    def across(slot, h):
        i = SIB_ORDER.index(slot)
        return remote(kv.at[slot, h], kv.at[SIB_OF[slot], h], sb_send.at[i, h], sb_recv.at[i, h], sib)

    def tick(step, h):
        up(step, h).wait_recv()
        if step < 3 or (step == 3 and h == 0):
            up(step + 1, h).start()
        down(step, 1 - h).wait_recv()
        if step < 3 or (step == 3 and h == 0):
            down(step + 1, 1 - h).start()
        across(UP[step], h).start()
        across(DOWN[step], 1 - h).start()

    def crossed(*slots):
        for slot in slots:
            for h in range(2):
                across(slot, h).wait_recv()

    for h in range(2):
        up(1, h).start()
        down(1, 1 - h).start()
    across(0, 0).start()
    across(0, 1).start()

    load_qn.wait()
    load_qr.wait()
    tmpn[...] = qn[...].astype(jnp.float32).reshape(64, NOPE)
    tmpr[:, :ROPE] = qr[...].astype(jnp.float32).reshape(64, ROPE)
    for parity in range(2):
        qsend[parity, 0:32, :] = tmpn[pl.ds(parity, 32, stride=2), :].astype(jnp.bfloat16)
        rope = tmpr[pl.ds(parity, 32, stride=2), :][:, :ROPE]
        qsend[parity, 32:48, :] = jnp.concatenate([rope[:16], rope[16:]], axis=1).astype(
            jnp.bfloat16
        )
    q_sib = remote(qsend.at[1 - c], qall.at[chip, c], qs_send, qs_recv, sib)
    q_sib.start()
    for r in range(HEADS):
        load_ka(r).start()
    load_va = pltpu.make_async_copy(va_ref.at[0], va.at[j_me], local.at[9])
    load_va.start()
    own_rows = pl.ds(pl.multiple_of(quarter * VDIM, VDIM), VDIM)
    load_wo = [
        pltpu.make_async_copy(
            wo_ref.at[:, columns(quarter, n)], wo.at[own_rows, owned(n)], local.at[13 + n]
        )
        for n in range(2)
    ]
    for copy in load_wo:
        copy.start()

    def v_y(way):
        return remote(
            va_ref.at[0], va.at[j_me], vy_send.at[way], vy_recv.at[way], at(x, yy + 1 + 2 * way, c)
        )

    def v_relay(way):
        half = va.at[head_of(xl, yy + 3 - 2 * way), pl.ds(way * 256, 256), :]
        return remote(half, half, vf_send.at[way], vf_recv.at[way], at(x, yy + 1 + 2 * way, c))

    def v_x(i, way):
        half = va.at[head_of(xl, yy + i), pl.ds(way * 256, 256), :]
        src = va_ref.at[0, pl.ds(way * 256, 256), :] if i == 0 else half
        return remote(src, half, vx_send.at[i, way], vx_recv.at[i, way], at(x + 1 + 2 * way, yy, c))

    for way in range(2):
        v_y(way).start()
        v_x(0, way).start()

    qall[chip, c] = qsend[c]
    q_sib.wait_recv()

    def q_copy(k):
        _, to = peer(OFFSETS[k])
        return remote(qall.at[chip], qall.at[chip], q_send.at[k], q_recv.at[chip], to)

    for k in range(PLANE - 1):
        q_copy(k).start()

    wo_copies = [
        remote(
            wo_ref.at[:, columns(2 * xl + 1 - c, n)], wo.at[own_rows, owned(n)],
            o_send.at[n], o_recv.at[n], sib,
        )
        for n in range(2)
    ]
    for copy in wo_copies:
        copy.start()

    def wo_x(way, core, n):
        return remote(
            wo_ref.at[pl.ds(way * 64, 64), columns(2 * (1 - xl) + core, n)],
            wo.at[pl.ds(pl.multiple_of(quarter * VDIM + way * 64, 64), 64), owned(n)],
            ox_send.at[way, core, n], ox_recv.at[way, c, n], at(x + 1 + 2 * way, yy, core),
        )

    def wo_x_arrived(way, core, n):
        rows = pl.ds(pl.multiple_of((2 * (1 - xl) + core) * VDIM + way * 64, 64), 64)
        remote(
            wo.at[rows, owned(n)], wo.at[rows, owned(n)],
            ox_send.at[way, core, n], ox_recv.at[way, core, n], at(x + 3 - 2 * way, yy, core),
        ).wait_recv()

    tick(1, 0)
    tick(1, 1)

    for k in range(PLANE - 1):
        other, to = peer(OFFSETS[k])
        remote(qall.at[other], qall.at[other], q_send.at[k], q_recv.at[other], to).wait_recv()
    for way in range(2):
        for core in range(2):
            for n in range(2):
                wo_x(way, core, n).start()

    for g in range(2 * PLANE):
        m = qall[g // 2, g % 2]
        q32n[g * 32 : (g + 1) * 32, :] = m[0:32].astype(jnp.float32)
        r = m[32:48].astype(jnp.float32)
        q32r[g * 32 : g * 32 + 16, 0:ROPE] = r[:, :ROPE]
        q32r[g * 32 + 16 : g * 32 + 32, 0:ROPE] = r[:, ROPE:]


    for r in range(HEADS):
        load_ka(r).wait()

    for r in range(HEADS):
        j = head(r)
        rows = slice(r * TOKENS, (r + 1) * TOKENS)
        nope = q32n[pl.ds(j, TOKENS, stride=HEADS), :].astype(jnp.bfloat16)
        part = jnp.dot(nope, ka[r], preferred_element_type=jnp.float32)
        q[rows, 0:LATENT] = (part * SCALE).astype(jnp.bfloat16)
        rope = q32r[pl.ds(j, TOKENS, stride=HEADS), :][:, :ROPE]
        q[rows, LATENT:WIDTH] = (rope * SCALE).astype(jnp.bfloat16)
    for way in range(2):
        v_y(way).wait_recv()
        v_relay(way).start()
    for way in range(2):
        v_x(3, way).start()
        v_x(1, way).start()
    tick(2, 0)
    tick(2, 1)

    crossed(0)
    attend(True, (0, 1), q, kv, acc, top, tot)
    crossed(2, 3)
    attend(False, (2, 3, 4, 5), q, kv, acc, top, tot)
    for way in range(2):
        v_relay(way).wait_recv()
        v_x(2, way).start()
    tick(3, 0)
    tick(3, 1)
    crossed(6, 7)
    attend(False, (6, 7, 8, 9), q, kv, acc, top, tot)
    crossed(10, 11)
    attend(False, (10, 11, 12, 13), q, kv, acc, top, tot)
    up(4, 0).wait_recv()
    across(14, 0).start()
    down(4, 1).wait_recv()
    across(14, 1).start()

    attend(False, (14,), q, kv, acc, top, tot)
    load_va.wait()

    for i in range(4):
        for way in range(2):
            v_x(i, way).wait_recv()
    crossed(14)

    per = TILE // TOKENS
    lane = lax.broadcasted_iota(jnp.int32, (TOKENS, 128), 1)
    row = lax.broadcasted_iota(jnp.int32, (16, 128), 0)

    def y_copy(r, t):
        j = head(r)
        return remote(
            ysend.at[r, t], yrecv.at[chip], y_send.at[r, t], y_recv.at[chip], (2 * j + c, z, t)
        )

    def each_y(r, action):
        for t in range(2):
            if r < HEADS - 1:
                action(y_copy(r, t))
            else:

                @pl.when(t != dp)
                def _():
                    action(y_copy(r, t))

    def finish(i, latent, new_top, total):
        for h in range(per):
            r = i * per + h
            j = head(r)
            rows = slice(h * TOKENS, (h + 1) * TOKENS)
            y = jnp.dot(latent[rows], va[j], preferred_element_type=jnp.float32)
            y = y.astype(jnp.bfloat16)
            stats = jnp.where(lane % 2 == 0, new_top[rows], total[rows])
            stats = stats.T[0:16, :]
            high = stats.astype(jnp.bfloat16)
            left = stats - high.astype(jnp.float32)
            middle = left.astype(jnp.bfloat16)
            low = left - middle.astype(jnp.float32)
            stats = jnp.where(
                row < 2,
                high.astype(jnp.float32),
                jnp.where(row < 4, middle.astype(jnp.float32), low),
            ).astype(jnp.bfloat16)
            for t in range(2):
                ysend[r, t, 0:64, :] = y[t * 64 : (t + 1) * 64]
                ysend[r, t, 64:80, :] = stats
            each_y(r, lambda copy: copy.start())

    attend(False, (15,), q, kv, acc, top, tot, finish)
    yrecv[chip] = ysend[HEADS - 1, dp]
    for offset in OFFSETS[::-1]:
        other, to = peer(offset)
        remote(
            yrecv.at[other], yrecv.at[other], y_send.at[0, 0], y_recv.at[other], to
        ).wait_recv()

    stats = [yrecv[s, 64:80, :].astype(jnp.float32) for s in range(PLANE)]
    tops = jnp.concatenate([x[0:1] + x[2:3] + x[4:5] for x in stats], axis=0)
    sums = jnp.concatenate([x[1:2] + x[3:4] + x[5:6] for x in stats], axis=0)
    weight = sums * jnp.exp2(tops - jnp.max(tops, axis=0, keepdims=True))
    weight = weight / jnp.sum(weight, axis=0, keepdims=True)
    wts[...] = jnp.concatenate([weight, jnp.zeros((128 - PLANE, 128), jnp.float32)], axis=0).T
    w = wts[pl.ds(pl.multiple_of(dp * 64, 64), 64), :]
    merged = None
    for s in range(PLANE):
        term = yrecv[s, 0:64, :].astype(jnp.float32) * w[:, s : s + 1]
        merged = term if merged is None else merged + term
    ho[quarter] = merged.astype(jnp.bfloat16)

    def h_copy(k):
        core = 1 - c if k % 2 else c
        x_low = 1 - xl if k >= 2 else xl
        return remote(
            ho.at[quarter], ho.at[quarter], h_send.at[k - 1], h_recv.at[k - 1], at(2 * dp + x_low, yy, core)
        )

    for k in (2, 3, 1):
        h_copy(k).start()
    for n in range(2):
        load_wo[n].wait()
        wo_copies[n].wait_recv()
    h_copy(1).wait_recv()

    def project(x_low, n):
        heads = jnp.concatenate([ho[2 * x_low], ho[2 * x_low + 1]], axis=1)
        rows = pl.ds(pl.multiple_of(x_low * 2 * VDIM, 2 * VDIM), 2 * VDIM)
        return jnp.dot(heads, wo[rows, owned(n)], preferred_element_type=jnp.float32)

    own_terms = [project(xl, n) for n in range(2)]
    for n in range(2):
        for way in range(2):
            for core in range(2):
                wo_x_arrived(way, core, n)
    for k in (2, 3):
        h_copy(k).wait_recv()

    def d_copy(n, k):
        other = lax.rem(yy + k, 4)
        return remote(
            dsend.at[n, other], drecv.at[n, yy], d_send.at[n, k - 1], d_recv.at[n, yy], at(x, other, c)
        )

    def d_arrived(n, k):
        other = lax.rem(yy + k, 4)
        remote(
            dsend.at[n, other], drecv.at[n, other], d_send.at[n, k - 1], d_recv.at[n, other],
            at(x, other, c),
        ).wait_recv()

    for n in range(2):
        terms = own_terms[n] + project(1 - xl, n)
        for i in range(4):
            dsend[n, i] = jnp.concatenate(
                [terms[i * 8 : i * 8 + 8], terms[32 + i * 8 : 40 + i * 8]], axis=0
            ).astype(jnp.bfloat16)
        for k in (2, 1, 3):
            d_copy(n, k).start()

    def e_copy(n, x_low, core):
        to_z = quarter + 4 * n
        return (to_z == z) & (x_low == xl) & (core == c), remote(
            esend.at[n, x_low, core], erecv.at[z], e_send.at[n, x_low, core], e_recv.at[z],
            ((4 * x_low + yy) * 2 + core, to_z, dp),
        )

    for n in range(2):
        drecv[n, yy] = dsend[n, yy]
        for k in (1, 3, 2):
            d_arrived(n, k)
        summed = drecv[n, 0].astype(jnp.float32)
        for i in range(1, 4):
            summed = summed + drecv[n, i].astype(jnp.float32)
        for x_low in range(2):
            for core in range(2):
                start = x_low * 8 + core * 4
                pieces = [summed[start : start + 4, k * 128 : (k + 1) * 128] for k in range(7)]
                pieces.append(jnp.zeros((4, 128), jnp.float32))
                esend[n, x_low, core] = jnp.concatenate(pieces, axis=0).astype(jnp.bfloat16)
                here, copy = e_copy(n, x_low, core)

                @pl.when(jnp.logical_not(here))
                def _():
                    copy.start()

                @pl.when(here)
                def _():
                    erecv[z] = esend[n, x_low, core]

    q_sib.wait_send()
    for step in range(1, 5):
        for h in range(2):
            if step < 4 or h == 0:
                up(step, h).wait_send()
                down(step, 1 - h).wait_send()
    for slot in SIB_ORDER:
        for h in range(2):
            across(slot, h).wait_send()
    for copy in wo_copies:
        copy.wait_send()
    for k in (1, 2, 3):
        h_copy(k).wait_send()

    for k in range(PLANE - 1):
        q_copy(k).wait_send()
    for r in range(HEADS):
        each_y(r, lambda copy: copy.wait_send())
    for way in range(2):
        v_y(way).wait_send()
        v_relay(way).wait_send()
        for i in range(4):
            v_x(i, way).wait_send()
        for core in range(2):
            for n in range(2):
                wo_x(way, core, n).wait_send()

    from_x, from_core = lax.rem(lax.div(z, 2), 2), lax.rem(z, 2)

    def e_arrived(s):
        frm = ((4 * from_x + yy) * 2 + from_core, s, dp)

        @pl.when(jnp.logical_not((s == z) & (from_x == xl) & (from_core == c)))
        def _():
            remote(
                esend.at[0, 0, 0], erecv.at[s], e_send.at[0, 0, 0], e_recv.at[s], frm
            ).wait_recv()

    loop(Z, e_arrived)
    result = erecv[0].astype(jnp.float32)
    for s in range(1, Z):
        result = result + erecv[s].astype(jnp.float32)
    for k in range(7):
        out_ref[:, k * 128 : (k + 1) * 128] = result[4 * k : 4 * k + 4]

    for n in range(2):
        for k in (1, 2, 3):
            d_copy(n, k).wait_send()
        for x_low in range(2):
            for core in range(2):
                here, copy = e_copy(n, x_low, core)

                @pl.when(jnp.logical_not(here))
                def _():
                    copy.wait_send()


def body(query_nope, query_rope, latent_cache, key_absorb, value_absorb, output_proj):
    vmem = pl.BlockSpec(memory_space=pltpu.VMEM)
    hbm = pl.BlockSpec(memory_space=pl.ANY)
    bf16, f32 = jnp.bfloat16, jnp.float32
    dma = pltpu.SemaphoreType.DMA
    return pl.pallas_call(
        kernel,
        out_shape=jax.ShapeDtypeStruct((4, COLS), f32),
        in_specs=[hbm] * 6,
        out_specs=vmem,
        scratch_shapes=[
            pltpu.VMEM((16, 2, HALFB + PACK, LATENT), bf16),
            pltpu.VMEM((ROWS, WIDTH), bf16),
            pltpu.VMEM((ROWS, LATENT), f32),
            pltpu.VMEM((ROWS, 128), f32),
            pltpu.VMEM((ROWS, 128), f32),
            pltpu.VMEM((HEADS, NOPE, LATENT), bf16),
            pltpu.VMEM((HEADS, LATENT, VDIM), bf16),
            pltpu.VMEM((4 * VDIM, QUARTER), bf16),
            pltpu.VMEM((4, 16, NOPE), bf16),
            pltpu.VMEM((4, 16, ROPE), bf16),
            pltpu.VMEM((64, NOPE), f32),
            pltpu.VMEM((64, 128), f32),
            pltpu.VMEM((2, MSG, 128), bf16),
            pltpu.VMEM((PLANE, 2, MSG, 128), bf16),
            pltpu.VMEM((ROWS, NOPE), f32),
            pltpu.VMEM((ROWS, 128), f32),
            pltpu.VMEM((BLOCK, WIDTH), bf16),
            pltpu.VMEM((HEADS, 2, 80, VDIM), bf16),
            pltpu.VMEM((PLANE, 80, VDIM), bf16),
            pltpu.VMEM((128, 128), f32),
            pltpu.VMEM((4, 64, VDIM), bf16),
            pltpu.VMEM((2, 4, 16, COLS), bf16),
            pltpu.VMEM((2, 4, 16, COLS), bf16),
            pltpu.VMEM((2, 2, 2, 32, 128), bf16),
            pltpu.VMEM((Z, 32, 128), bf16),
            dma((15,)),
            dma, dma, dma((PLANE - 1,)), dma((PLANE,)),
            dma((4, 2)), dma((4, 2)), dma((4, 2)), dma((4, 2)), dma((8, 2)), dma((8, 2)),
            dma((2,)), dma((2,)), dma((2,)), dma((2,)), dma((4, 2)), dma((4, 2)),
            dma((2,)), dma((2,)), dma((2, 2, 2)), dma((2, 2, 2)),
            dma((HEADS, 2)), dma((PLANE,)),
            dma((3,)), dma((3,)), dma((2, 3)), dma((2, 4)), dma((2, 2, 2)), dma((Z,)),
        ],
        compiler_params=pltpu.CompilerParams(
            collective_id=0, has_side_effects=True, vmem_limit_bytes=127 * 512 * 1024
        ),
        cost_estimate=pl.CostEstimate(
            flops=7_000_000_000, bytes_accessed=10_000_000, transcendentals=3_145_728
        ),
        name="latent_attention",
    )(query_nope, query_rope, latent_cache, key_absorb, value_absorb, output_proj)


def solution(mesh):
    in_specs = (
        P(("dp", "prefix"), "head", None),
        P(("dp", "prefix"), "head", None),
        P(("prefix", "head", "dp"), None),
        P("head", None, None),
        P(("head", "prefix"), None, None),
        P(("head", "prefix"), None),
    )
    out_specs = P(("dp", "prefix"), "head")
    return jax.shard_map(body, mesh=mesh, in_specs=in_specs, out_specs=out_specs, check_vma=False)
```

```python
import math

import jax
import jax.numpy as jnp
from jax import lax
from jax.experimental import pallas as pl
from jax.experimental.pallas import tpu as pltpu
from jax.sharding import PartitionSpec as P

MESH = pl.DeviceIdType.MESH

D = 7168
NOPE, ROPE, VDIM, LATENT = 128, 64, 128, 512
WIDTH = LATENT + ROPE
TOKENS = 128
Z = 8
PLANE = 16
OWNERS = 8
HEADS = 8
ROWS = HEADS * TOKENS
BLOCK = 192
MSG = 48
QUARTER = D // 4
COLS = D // Z
SCALE = (NOPE + ROPE) ** -0.5 * math.log2(math.e)

HALFB = BLOCK // 2
PACK = 16
UP = (0, 2, 6, 10, 14)
DOWN = (0, 3, 7, 11, 14)
SIB_OF = {0: 1, 2: 4, 3: 5, 6: 8, 7: 9, 10: 12, 11: 13, 14: 15}
SIB_ORDER = (0, 2, 3, 6, 7, 10, 11, 14)
TILE = 512
OFFSETS = sorted(
    [(dx, dy) for dx in range(4) for dy in range(4) if dx or dy],
    key=lambda o: -(min(o[0], 4 - o[0]) + min(o[1], 4 - o[1])),
)


def chunk_keys(kv, blocks):
    latent, rope = [], []
    for b in blocks:
        for h in range(2):
            latent.append(kv[b, h, 0:HALFB, :])
            packed = kv[b, h, HALFB : HALFB + PACK, 0 : 6 * ROPE]
            for g in range(6):
                rope.append(packed[:, g * ROPE : (g + 1) * ROPE])
    latent = jnp.concatenate(latent, axis=0)
    return jnp.concatenate([latent, jnp.concatenate(rope, axis=0)], axis=1), latent


def attend(first, blocks, q, kv, acc, top, tot, finish=None):
    keys, values = chunk_keys(kv, blocks)
    n = ROWS // TILE

    def at(i):
        return pl.ds(i * TILE, TILE)

    def score(i):
        return lax.dot_general(
            q[at(i), :], keys, (((1,), (1,)), ((), ())), preferred_element_type=jnp.float32
        )

    s = score(0)
    for i in range(n):
        later = score(i + 1) if i + 1 < n else None
        rows = at(i)
        high = jnp.max(s, axis=1, keepdims=True)
        if first:
            new_top = jnp.broadcast_to(high, (TILE, 128))
        else:
            old_top = top[rows, :]
            new_top = jnp.maximum(old_top, high)
            alpha = jnp.exp2(old_top - new_top)
        part = None
        pieces = []
        for k in range(0, s.shape[1], 128):
            width = min(128, s.shape[1] - k)
            e = jnp.exp2(s[:, k : k + width] - new_top[:, :width])
            pieces.append(e.astype(jnp.bfloat16))
            if width < 128:
                e = jnp.concatenate([e, jnp.zeros((TILE, 128 - width), jnp.float32)], axis=1)
            part = e if part is None else part + e
        p = jnp.concatenate(pieces, axis=1)
        out = jnp.dot(p, values, preferred_element_type=jnp.float32)
        if not first:
            part = tot[rows, :] * alpha + part
        if finish is not None:
            total = jnp.sum(part, axis=1, keepdims=True)
            scale = 1.0 / total
            latent = []
            for k in range(LATENT // 128):
                cols = slice(k * 128, (k + 1) * 128)
                latent.append(((acc[rows, cols] * alpha + out[:, cols]) * scale).astype(jnp.bfloat16))
            finish(i, jnp.concatenate(latent, axis=1), new_top, total)
        else:
            top[rows, :] = new_top
            tot[rows, :] = part
            for k in range(LATENT // 128):
                cols = slice(k * 128, (k + 1) * 128)
                if first:
                    acc[rows, cols] = out[:, cols]
                else:
                    acc[rows, cols] = acc[rows, cols] * alpha + out[:, cols]
        s = later


def kernel(
    qn_ref, qr_ref, kv_ref, ka_ref, va_ref, wo_ref, out_ref,
    kv, q, acc, top, tot, ka, va, wo,
    qn, qr, tmpn, tmpr, qsend, qall, q32n, q32r,
    kvraw, ysend, yrecv, wts, ho, dsend, drecv, esend, erecv,
    local, qs_send, qs_recv, q_send, q_recv,
    up_send, up_recv, dn_send, dn_recv, sb_send, sb_recv,
    vy_send, vy_recv, vf_send, vf_recv, vx_send, vx_recv, o_send, o_recv, ox_send, ox_recv,
    y_send, y_recv, h_send, h_recv, d_send, d_recv, e_send, e_recv,
):
    prefix, z, dp = lax.axis_index("prefix"), lax.axis_index("head"), lax.axis_index("dp")
    c = lax.rem(prefix, 2)
    j_me = lax.div(prefix, 2)
    chip = dp * OWNERS + j_me
    sib = (prefix + 1 - 2 * c, z, dp)
    above = (prefix, lax.rem(z + 1, Z), dp)
    below = (prefix, lax.rem(z + Z - 1, Z), dp)

    xl, yy = lax.div(j_me, 4), lax.rem(j_me, 4)
    x = 2 * dp + xl
    quarter = 2 * xl + c

    def at(x_to, y_to, core):
        x_to, y_to = lax.rem(x_to, 4), lax.rem(y_to, 4)
        return ((lax.rem(x_to, 2) * 4 + y_to) * 2 + core, z, lax.div(x_to, 2))

    def peer(offset):
        x_to, y_to = lax.rem(x + offset[0], 4), lax.rem(yy + offset[1], 4)
        x_low, x_high = lax.rem(x_to, 2), lax.div(x_to, 2)
        index = x_low * 4 + y_to
        return x_high * OWNERS + index, (2 * index + c, z, x_high)

    def head(r):
        x_low = 1 - xl if r < 4 else xl
        return x_low * 4 + lax.rem(yy + (2, 1, 3, 0)[r % 4], 4)

    def head_of(x_low, y_of):
        return x_low * 4 + lax.rem(y_of, 4)

    def columns(quarter_of, n):
        return pl.ds(pl.multiple_of((quarter_of + 4 * n) * COLS, 128), COLS)

    def owned(n):
        return pl.ds(n * COLS, COLS)

    def remote(src, dst, ssem, rsem, to):
        return pltpu.make_async_remote_copy(
            src_ref=src, dst_ref=dst, send_sem=ssem, recv_sem=rsem, device_id=to, device_id_type=MESH
        )

    def loop(n, body):
        def step(k, carry):
            body(k)
            return carry

        lax.fori_loop(0, n, step, 0)

    def load_ka(r):
        return pltpu.make_async_copy(ka_ref.at[2 * head(r) + c], ka.at[r], local.at[r])

    load_kv = pltpu.make_async_copy(kv_ref, kvraw, local.at[8])
    load_kv.start()
    load_qn = pltpu.make_async_copy(qn_ref, qn, local.at[11])
    load_qn.start()
    load_qr = pltpu.make_async_copy(qr_ref, qr, local.at[12])
    load_qr.start()

    barrier = pltpu.get_barrier_semaphore()

    def greet(to):
        pl.semaphore_signal(barrier, inc=1, device_id=to, device_id_type=MESH)

    for offset in OFFSETS:
        greet(peer(offset)[1])
    for to in (above, below, sib):
        greet(to)

    load_kv.wait()
    for h in range(2):
        rows = slice(h * HALFB, (h + 1) * HALFB)
        kv[0, h, 0:HALFB, :] = kvraw[rows, 0:LATENT]
        rope = kvraw[rows, LATENT:WIDTH].astype(jnp.float32)
        packed = [rope[g * PACK : (g + 1) * PACK] for g in range(6)]
        packed.append(jnp.zeros((PACK, LATENT - 6 * ROPE), jnp.float32))
        kv[0, h, HALFB : HALFB + PACK, :] = jnp.concatenate(packed, axis=1).astype(jnp.bfloat16)

    pl.semaphore_wait(barrier, 3 + (PLANE - 1))

    def up(step, h):
        return remote(
            kv.at[UP[step - 1], h], kv.at[UP[step], h],
            up_send.at[step - 1, h], up_recv.at[step - 1, h], above,
        )

    def down(step, h):
        return remote(
            kv.at[DOWN[step - 1], h], kv.at[DOWN[step], h],
            dn_send.at[step - 1, h], dn_recv.at[step - 1, h], below,
        )

    def across(slot, h):
        i = SIB_ORDER.index(slot)
        return remote(kv.at[slot, h], kv.at[SIB_OF[slot], h], sb_send.at[i, h], sb_recv.at[i, h], sib)

    def tick(step, h):
        up(step, h).wait_recv()
        if step < 3 or (step == 3 and h == 0):
            up(step + 1, h).start()
        down(step, 1 - h).wait_recv()
        if step < 3 or (step == 3 and h == 0):
            down(step + 1, 1 - h).start()
        across(UP[step], h).start()
        across(DOWN[step], 1 - h).start()

    def crossed(*slots):
        for slot in slots:
            for h in range(2):
                across(slot, h).wait_recv()

    for h in range(2):
        up(1, h).start()
        down(1, 1 - h).start()
    across(0, 0).start()
    across(0, 1).start()

    load_qn.wait()
    load_qr.wait()
    tmpn[...] = qn[...].astype(jnp.float32).reshape(64, NOPE)
    tmpr[:, :ROPE] = qr[...].astype(jnp.float32).reshape(64, ROPE)
    for parity in range(2):
        qsend[parity, 0:32, :] = tmpn[pl.ds(parity, 32, stride=2), :].astype(jnp.bfloat16)
        rope = tmpr[pl.ds(parity, 32, stride=2), :][:, :ROPE]
        qsend[parity, 32:48, :] = jnp.concatenate([rope[:16], rope[16:]], axis=1).astype(
            jnp.bfloat16
        )
    q_sib = remote(qsend.at[1 - c], qall.at[chip, c], qs_send, qs_recv, sib)
    q_sib.start()

    def v_y(way):
        return remote(
            va_ref.at[0], va.at[j_me], vy_send.at[way], vy_recv.at[way], at(x, yy + 1 + 2 * way, c)
        )

    def v_relay(way):
        half = va.at[head_of(xl, yy + 3 - 2 * way), pl.ds(way * 256, 256), :]
        return remote(half, half, vf_send.at[way], vf_recv.at[way], at(x, yy + 1 + 2 * way, c))

    def v_x(i, way):
        half = va.at[head_of(xl, yy + i), pl.ds(way * 256, 256), :]
        src = va_ref.at[0, pl.ds(way * 256, 256), :] if i == 0 else half
        return remote(src, half, vx_send.at[i, way], vx_recv.at[i, way], at(x + 1 + 2 * way, yy, c))

    for way in range(2):
        v_y(way).start()
        v_x(0, way).start()

    qall[chip, c] = qsend[c]
    q_sib.wait_recv()

    def q_copy(k):
        _, to = peer(OFFSETS[k])
        return remote(qall.at[chip], qall.at[chip], q_send.at[k], q_recv.at[chip], to)

    for k in range(PLANE - 1):
        q_copy(k).start()

    for r in range(HEADS):
        load_ka(r).start()
    load_va = pltpu.make_async_copy(va_ref.at[0], va.at[j_me], local.at[9])
    load_va.start()
    own_rows = pl.ds(pl.multiple_of(quarter * VDIM, VDIM), VDIM)
    load_wo = [
        pltpu.make_async_copy(
            wo_ref.at[:, columns(quarter, n)], wo.at[own_rows, owned(n)], local.at[13 + n]
        )
        for n in range(2)
    ]
    for copy in load_wo:
        copy.start()

    wo_copies = [
        remote(
            wo_ref.at[:, columns(2 * xl + 1 - c, n)], wo.at[own_rows, owned(n)],
            o_send.at[n], o_recv.at[n], sib,
        )
        for n in range(2)
    ]
    for copy in wo_copies:
        copy.start()

    def wo_x(way, core, n):
        return remote(
            wo_ref.at[pl.ds(way * 64, 64), columns(2 * (1 - xl) + core, n)],
            wo.at[pl.ds(pl.multiple_of(quarter * VDIM + way * 64, 64), 64), owned(n)],
            ox_send.at[way, core, n], ox_recv.at[way, c, n], at(x + 1 + 2 * way, yy, core),
        )

    def wo_x_arrived(way, core, n):
        rows = pl.ds(pl.multiple_of((2 * (1 - xl) + core) * VDIM + way * 64, 64), 64)
        remote(
            wo.at[rows, owned(n)], wo.at[rows, owned(n)],
            ox_send.at[way, core, n], ox_recv.at[way, core, n], at(x + 3 - 2 * way, yy, core),
        ).wait_recv()

    tick(1, 0)
    tick(1, 1)

    for k in range(PLANE - 1):
        other, to = peer(OFFSETS[k])
        remote(qall.at[other], qall.at[other], q_send.at[k], q_recv.at[other], to).wait_recv()
    for way in range(2):
        for core in range(2):
            for n in range(2):
                wo_x(way, core, n).start()

    for g in range(2 * PLANE):
        m = qall[g // 2, g % 2]
        q32n[g * 32 : (g + 1) * 32, :] = m[0:32].astype(jnp.float32)
        r = m[32:48].astype(jnp.float32)
        q32r[g * 32 : g * 32 + 16, 0:ROPE] = r[:, :ROPE]
        q32r[g * 32 + 16 : g * 32 + 32, 0:ROPE] = r[:, ROPE:]


    for r in range(HEADS):
        load_ka(r).wait()

    for r in range(HEADS):
        j = head(r)
        rows = slice(r * TOKENS, (r + 1) * TOKENS)
        nope = q32n[pl.ds(j, TOKENS, stride=HEADS), :].astype(jnp.bfloat16)
        part = jnp.dot(nope, ka[r], preferred_element_type=jnp.float32)
        q[rows, 0:LATENT] = (part * SCALE).astype(jnp.bfloat16)
        rope = q32r[pl.ds(j, TOKENS, stride=HEADS), :][:, :ROPE]
        q[rows, LATENT:WIDTH] = (rope * SCALE).astype(jnp.bfloat16)
    for way in range(2):
        v_y(way).wait_recv()
        v_relay(way).start()
    for way in range(2):
        v_x(3, way).start()
        v_x(1, way).start()
    tick(2, 0)
    tick(2, 1)

    crossed(0)
    attend(True, (0, 1), q, kv, acc, top, tot)
    crossed(2, 3)
    attend(False, (2, 3, 4, 5), q, kv, acc, top, tot)
    for way in range(2):
        v_relay(way).wait_recv()
        v_x(2, way).start()
    tick(3, 0)
    tick(3, 1)
    crossed(6, 7)
    attend(False, (6, 7, 8, 9), q, kv, acc, top, tot)
    crossed(10, 11)
    attend(False, (10, 11, 12, 13), q, kv, acc, top, tot)
    up(4, 0).wait_recv()
    across(14, 0).start()
    down(4, 1).wait_recv()
    across(14, 1).start()

    attend(False, (14,), q, kv, acc, top, tot)
    load_va.wait()

    for i in range(4):
        for way in range(2):
            v_x(i, way).wait_recv()
    crossed(14)

    per = TILE // TOKENS
    lane = lax.broadcasted_iota(jnp.int32, (TOKENS, 128), 1)
    row = lax.broadcasted_iota(jnp.int32, (16, 128), 0)

    def y_copy(r, t):
        j = head(r)
        return remote(
            ysend.at[r, t], yrecv.at[chip], y_send.at[r, t], y_recv.at[chip], (2 * j + c, z, t)
        )

    def each_y(r, action):
        for t in range(2):
            if r < HEADS - 1:
                action(y_copy(r, t))
            else:

                @pl.when(t != dp)
                def _():
                    action(y_copy(r, t))

    def finish(i, latent, new_top, total):
        for h in range(per):
            r = i * per + h
            j = head(r)
            rows = slice(h * TOKENS, (h + 1) * TOKENS)
            y = jnp.dot(latent[rows], va[j], preferred_element_type=jnp.float32)
            y = y.astype(jnp.bfloat16)
            stats = jnp.where(lane % 2 == 0, new_top[rows], total[rows])
            stats = stats.T[0:16, :]
            high = stats.astype(jnp.bfloat16)
            left = stats - high.astype(jnp.float32)
            middle = left.astype(jnp.bfloat16)
            low = left - middle.astype(jnp.float32)
            stats = jnp.where(
                row < 2,
                high.astype(jnp.float32),
                jnp.where(row < 4, middle.astype(jnp.float32), low),
            ).astype(jnp.bfloat16)
            for t in range(2):
                ysend[r, t, 0:64, :] = y[t * 64 : (t + 1) * 64]
                ysend[r, t, 64:80, :] = stats
            each_y(r, lambda copy: copy.start())

    attend(False, (15,), q, kv, acc, top, tot, finish)
    yrecv[chip] = ysend[HEADS - 1, dp]
    for offset in OFFSETS[::-1]:
        other, to = peer(offset)
        remote(
            yrecv.at[other], yrecv.at[other], y_send.at[0, 0], y_recv.at[other], to
        ).wait_recv()

    stats = [yrecv[s, 64:80, :].astype(jnp.float32) for s in range(PLANE)]
    tops = jnp.concatenate([x[0:1] + x[2:3] + x[4:5] for x in stats], axis=0)
    sums = jnp.concatenate([x[1:2] + x[3:4] + x[5:6] for x in stats], axis=0)
    weight = sums * jnp.exp2(tops - jnp.max(tops, axis=0, keepdims=True))
    weight = weight / jnp.sum(weight, axis=0, keepdims=True)
    wts[...] = jnp.concatenate([weight, jnp.zeros((128 - PLANE, 128), jnp.float32)], axis=0).T
    w = wts[pl.ds(pl.multiple_of(dp * 64, 64), 64), :]
    merged = None
    for s in range(PLANE):
        term = yrecv[s, 0:64, :].astype(jnp.float32) * w[:, s : s + 1]
        merged = term if merged is None else merged + term
    ho[quarter] = merged.astype(jnp.bfloat16)

    def h_copy(k):
        core = 1 - c if k % 2 else c
        x_low = 1 - xl if k >= 2 else xl
        return remote(
            ho.at[quarter], ho.at[quarter], h_send.at[k - 1], h_recv.at[k - 1], at(2 * dp + x_low, yy, core)
        )

    for k in (2, 3, 1):
        h_copy(k).start()
    for n in range(2):
        load_wo[n].wait()
        wo_copies[n].wait_recv()
    h_copy(1).wait_recv()

    def project(x_low, n):
        heads = jnp.concatenate([ho[2 * x_low], ho[2 * x_low + 1]], axis=1)
        rows = pl.ds(pl.multiple_of(x_low * 2 * VDIM, 2 * VDIM), 2 * VDIM)
        return jnp.dot(heads, wo[rows, owned(n)], preferred_element_type=jnp.float32)

    own_terms = [project(xl, n) for n in range(2)]
    for n in range(2):
        for way in range(2):
            for core in range(2):
                wo_x_arrived(way, core, n)
    for k in (2, 3):
        h_copy(k).wait_recv()

    def d_copy(n, k):
        other = lax.rem(yy + k, 4)
        return remote(
            dsend.at[n, other], drecv.at[n, yy], d_send.at[n, k - 1], d_recv.at[n, yy], at(x, other, c)
        )

    def d_arrived(n, k):
        other = lax.rem(yy + k, 4)
        remote(
            dsend.at[n, other], drecv.at[n, other], d_send.at[n, k - 1], d_recv.at[n, other],
            at(x, other, c),
        ).wait_recv()

    for n in range(2):
        terms = own_terms[n] + project(1 - xl, n)
        for i in range(4):
            dsend[n, i] = jnp.concatenate(
                [terms[i * 8 : i * 8 + 8], terms[32 + i * 8 : 40 + i * 8]], axis=0
            ).astype(jnp.bfloat16)
        for k in (2, 1, 3):
            d_copy(n, k).start()

    def e_copy(n, x_low, core):
        to_z = quarter + 4 * n
        return (to_z == z) & (x_low == xl) & (core == c), remote(
            esend.at[n, x_low, core], erecv.at[z], e_send.at[n, x_low, core], e_recv.at[z],
            ((4 * x_low + yy) * 2 + core, to_z, dp),
        )

    for n in range(2):
        drecv[n, yy] = dsend[n, yy]
        for k in (1, 3, 2):
            d_arrived(n, k)
        summed = drecv[n, 0].astype(jnp.float32)
        for i in range(1, 4):
            summed = summed + drecv[n, i].astype(jnp.float32)
        for x_low in range(2):
            for core in range(2):
                start = x_low * 8 + core * 4
                pieces = [summed[start : start + 4, k * 128 : (k + 1) * 128] for k in range(7)]
                pieces.append(jnp.zeros((4, 128), jnp.float32))
                esend[n, x_low, core] = jnp.concatenate(pieces, axis=0).astype(jnp.bfloat16)
                here, copy = e_copy(n, x_low, core)

                @pl.when(jnp.logical_not(here))
                def _():
                    copy.start()

                @pl.when(here)
                def _():
                    erecv[z] = esend[n, x_low, core]

    q_sib.wait_send()
    for step in range(1, 5):
        for h in range(2):
            if step < 4 or h == 0:
                up(step, h).wait_send()
                down(step, 1 - h).wait_send()
    for slot in SIB_ORDER:
        for h in range(2):
            across(slot, h).wait_send()
    for copy in wo_copies:
        copy.wait_send()
    for k in (1, 2, 3):
        h_copy(k).wait_send()

    for k in range(PLANE - 1):
        q_copy(k).wait_send()
    for r in range(HEADS):
        each_y(r, lambda copy: copy.wait_send())
    for way in range(2):
        v_y(way).wait_send()
        v_relay(way).wait_send()
        for i in range(4):
            v_x(i, way).wait_send()
        for core in range(2):
            for n in range(2):
                wo_x(way, core, n).wait_send()

    from_x, from_core = lax.rem(lax.div(z, 2), 2), lax.rem(z, 2)

    def e_arrived(s):
        frm = ((4 * from_x + yy) * 2 + from_core, s, dp)

        @pl.when(jnp.logical_not((s == z) & (from_x == xl) & (from_core == c)))
        def _():
            remote(
                esend.at[0, 0, 0], erecv.at[s], e_send.at[0, 0, 0], e_recv.at[s], frm
            ).wait_recv()

    loop(Z, e_arrived)
    result = erecv[0].astype(jnp.float32)
    for s in range(1, Z):
        result = result + erecv[s].astype(jnp.float32)
    for k in range(7):
        out_ref[:, k * 128 : (k + 1) * 128] = result[4 * k : 4 * k + 4]

    for n in range(2):
        for k in (1, 2, 3):
            d_copy(n, k).wait_send()
        for x_low in range(2):
            for core in range(2):
                here, copy = e_copy(n, x_low, core)

                @pl.when(jnp.logical_not(here))
                def _():
                    copy.wait_send()


def body(query_nope, query_rope, latent_cache, key_absorb, value_absorb, output_proj):
    vmem = pl.BlockSpec(memory_space=pltpu.VMEM)
    hbm = pl.BlockSpec(memory_space=pl.ANY)
    bf16, f32 = jnp.bfloat16, jnp.float32
    dma = pltpu.SemaphoreType.DMA
    return pl.pallas_call(
        kernel,
        out_shape=jax.ShapeDtypeStruct((4, COLS), f32),
        in_specs=[hbm] * 6,
        out_specs=vmem,
        scratch_shapes=[
            pltpu.VMEM((16, 2, HALFB + PACK, LATENT), bf16),
            pltpu.VMEM((ROWS, WIDTH), bf16),
            pltpu.VMEM((ROWS, LATENT), f32),
            pltpu.VMEM((ROWS, 128), f32),
            pltpu.VMEM((ROWS, 128), f32),
            pltpu.VMEM((HEADS, NOPE, LATENT), bf16),
            pltpu.VMEM((HEADS, LATENT, VDIM), bf16),
            pltpu.VMEM((4 * VDIM, QUARTER), bf16),
            pltpu.VMEM((4, 16, NOPE), bf16),
            pltpu.VMEM((4, 16, ROPE), bf16),
            pltpu.VMEM((64, NOPE), f32),
            pltpu.VMEM((64, 128), f32),
            pltpu.VMEM((2, MSG, 128), bf16),
            pltpu.VMEM((PLANE, 2, MSG, 128), bf16),
            pltpu.VMEM((ROWS, NOPE), f32),
            pltpu.VMEM((ROWS, 128), f32),
            pltpu.VMEM((BLOCK, WIDTH), bf16),
            pltpu.VMEM((HEADS, 2, 80, VDIM), bf16),
            pltpu.VMEM((PLANE, 80, VDIM), bf16),
            pltpu.VMEM((128, 128), f32),
            pltpu.VMEM((4, 64, VDIM), bf16),
            pltpu.VMEM((2, 4, 16, COLS), bf16),
            pltpu.VMEM((2, 4, 16, COLS), bf16),
            pltpu.VMEM((2, 2, 2, 32, 128), bf16),
            pltpu.VMEM((Z, 32, 128), bf16),
            dma((15,)),
            dma, dma, dma((PLANE - 1,)), dma((PLANE,)),
            dma((4, 2)), dma((4, 2)), dma((4, 2)), dma((4, 2)), dma((8, 2)), dma((8, 2)),
            dma((2,)), dma((2,)), dma((2,)), dma((2,)), dma((4, 2)), dma((4, 2)),
            dma((2,)), dma((2,)), dma((2, 2, 2)), dma((2, 2, 2)),
            dma((HEADS, 2)), dma((PLANE,)),
            dma((3,)), dma((3,)), dma((2, 3)), dma((2, 4)), dma((2, 2, 2)), dma((Z,)),
        ],
        compiler_params=pltpu.CompilerParams(
            collective_id=0, has_side_effects=True, vmem_limit_bytes=127 * 512 * 1024
        ),
        cost_estimate=pl.CostEstimate(
            flops=7_000_000_000, bytes_accessed=10_000_000, transcendentals=3_145_728
        ),
        name="latent_attention",
    )(query_nope, query_rope, latent_cache, key_absorb, value_absorb, output_proj)


def solution(mesh):
    in_specs = (
        P(("dp", "prefix"), "head", None),
        P(("dp", "prefix"), "head", None),
        P(("prefix", "head", "dp"), None),
        P("head", None, None),
        P(("head", "prefix"), None, None),
        P(("head", "prefix"), None),
    )
    out_specs = P(("dp", "prefix"), "head")
    return jax.shard_map(body, mesh=mesh, in_specs=in_specs, out_specs=out_specs, check_vma=False)
```
